32 devices in a mesh: dp: 8 (over z, y), tensor: 4 (over x, core).
Axes of the slice: x: 2, y: 2, z: 4, core: 2. Of those that a mesh axis runs over, the one named last changes fastest.
Arguments:
- tokens: bfloat16 [2, 8192, 1024], P(None, ('dp', 'tensor')), may hold values from -6 to 6
- cotangent: float32 [2, 8192, 1024], P(None, ('dp', 'tensor')), may hold values from -6 to 6
- slot_order: int32 [2, 8, 1024], P(None, 'dp'), may hold values from 0 to 1023, each once within a row
- lengths: int32 [2, 8, 3], P(None, 'dp'), may hold values from 1 to 512, 1024 in all within a row
- live_mask: int32 [2, 8, 1024], P(None, 'dp'), may hold values 0 or 1
- w_in: float32 [4, 1024, 1024], P(None, 'dp', 'tensor'), may hold values from -0.1875 to 0.1875
- w_out: float32 [1024, 1024], P('tensor', 'dp'), may hold values from -0.75 to 0.75
- w_ff: float32 [2, 1024, 2816], P(None, 'dp', 'tensor'), may hold values from -0.1875 to 0.1875
- w_down: float32 [2816, 1024], P('tensor', 'dp'), may hold values from -0.21875 to 0.21875
- norm_gains: float32 [2, 1024], replicated, may hold values from 0.5 to 1.5
- conv_taps: float32 [3, 4, 1024], P(None, None, 'tensor'), may hold values from -3 to 3
- decay_w: float32 [1024, 8], P(None, 'tensor'), may hold values from -0.09375 to 0.09375
- mesa_bias: float32 [2, 8], P(None, 'tensor'), may hold values from -7 to -3
- mom_in: float32 [4, 1024, 1024], P(None, 'dp', 'tensor'), may hold values from -12 to 12
- mom_out: float32 [1024, 1024], P('tensor', 'dp'), may hold values from -12 to 12
- mom_ff: float32 [2, 1024, 2816], P(None, 'dp', 'tensor'), may hold values from -12 to 12
- mom_down: float32 [2816, 1024], P('tensor', 'dp'), may hold values from -12 to 12
- mom_gains: float32 [2, 1024], replicated, may hold values from -96 to 96
- mom_conv: float32 [3, 4, 1024], P(None, None, 'tensor'), may hold values from -8 to 8
- mom_decay: float32 [1024, 8], P(None, 'tensor'), may hold values from -8 to 8
- mom_bias: float32 [2, 8], P(None, 'tensor'), may hold values from -8 to 8
- err_in: float32 [8, 4, 1024, 1024], P('dp', None, None, 'tensor'), may hold values from -14 to 14
- err_out: float32 [8, 1024, 1024], P('dp', 'tensor'), may hold values from -14 to 14
- err_ff: float32 [8, 2, 1024, 2816], P('dp', None, None, 'tensor'), may hold values from -14 to 14
- err_down: float32 [8, 2816, 1024], P('dp', 'tensor'), may hold values from -14 to 14
- basis_in: float32 [4, 1024, 8], P(None, 'tensor'), may hold values from -6 to 6
- basis_out: float32 [4, 1024, 8], P('tensor'), may hold values from -6 to 6
- basis_ff: float32 [2, 2816, 8], P(None, 'tensor'), may hold values from -6 to 6
- basis_down: float32 [4, 1024, 8], P('tensor'), may hold values from -6 to 6
Outputs:
- out_tokens: bfloat16 [2, 8192, 1024], P(None, ('dp', 'tensor'))
- d_tokens: float32 [2, 8192, 1024], P(None, ('dp', 'tensor'))
- w_in_new: float32 [4, 1024, 1024], P(None, 'dp', 'tensor')
- mom_in_new: float32 [4, 1024, 1024], P(None, 'dp', 'tensor')
- err_in_new: float32 [8, 4, 1024, 1024], P('dp', None, None, 'tensor')
- basis_in_new: float32 [4, 1024, 8], P(None, 'tensor')
- w_out_new: float32 [1024, 1024], P('tensor', 'dp')
- mom_out_new: float32 [1024, 1024], P('tensor', 'dp')
- err_out_new: float32 [8, 1024, 1024], P('dp', 'tensor')
- basis_out_new: float32 [4, 1024, 8], P('tensor')
- w_ff_new: float32 [2, 1024, 2816], P(None, 'dp', 'tensor')
- mom_ff_new: float32 [2, 1024, 2816], P(None, 'dp', 'tensor')
- err_ff_new: float32 [8, 2, 1024, 2816], P('dp', None, None, 'tensor')
- basis_ff_new: float32 [2, 2816, 8], P(None, 'tensor')
- w_down_new: float32 [2816, 1024], P('tensor', 'dp')
- mom_down_new: float32 [2816, 1024], P('tensor', 'dp')
- err_down_new: float32 [8, 2816, 1024], P('dp', 'tensor')
- basis_down_new: float32 [4, 1024, 8], P('tensor')
- gains_new: float32 [2, 1024], replicated
- mom_gains_new: float32 [2, 1024], replicated
- conv_new: float32 [3, 4, 1024], P(None, None, 'tensor')
- mom_conv_new: float32 [3, 4, 1024], P(None, None, 'tensor')
- decay_new: float32 [1024, 8], P(None, 'tensor')
- mom_decay_new: float32 [1024, 8], P(None, 'tensor')
- bias_new: float32 [2, 8], P(None, 'tensor')
- mom_bias_new: float32 [2, 8], P(None, 'tensor')
The draws below stay inside these ranges and needn't reach their ends.
Inputs may be any that keep to these rules, and one draw needn't show every extreme that they name: `slot_order`: each row is a permutation of the pack's 1024 slots: entry j names the group slot placed at packed position j. Each row holds 3 lengths that sum to 1024; the largest is exactly 512.
All inputs are finite; a program needn't handle non-finite values. No bound on the sum of `live_mask` on one device may be relied on, other than what follows from the above.
Results may differ from the reference program's by a relative error of at most 0.033.
Values may be sent and summed in bfloat16 or wider, within the bound.
No kernel may reach another device: no remote copies, remote signals or barrier semaphores. Data moves between devices by JAX's collectives and lax.ppermute only.
A program may use at most 448 MiB of HBM per device.

```python
import math
import jax
import jax.numpy as jnp
import numpy as np
from jax import lax

D = 1024
H = 8
FF = 2816
TAPS = 4
CG_STEPS = 8
STRETCH = 64
RANK = 8
MB = 2
NSEQ = 3
GRP = 1024
MOST = 512
TOKENS = 8192
N_DP = 8
N_TENSOR = 4


def touch_ends(entries, rng, smallest, largest):
    longest = entries.shape.index(max(entries.shape))
    spots = []
    for shift in (0, 1):
        where = [jax.random.randint(jax.random.fold_in(rng, axis), (), 0, length) for axis, length in enumerate(entries.shape)]
        where[longest] = (where[longest] + shift) % entries.shape[longest]
        spots.append(tuple(where))
    return entries.at[spots[0]].set(smallest).at[spots[1]].set(largest)


def steps_of(stream_key, dims, shards, least, largest):
    factor_of = 1.0
    for dim, shards_of in shards:
        steps = jax.random.uniform(jax.random.fold_in(jax.random.fold_in(stream_key, 6), dim), (shards_of,), jnp.float32, least / len(shards), largest / len(shards))
        factor_of = factor_of * jnp.repeat(jnp.exp(steps), dims[dim] // shards_of).reshape((-1,) + (1,) * (len(dims) - 1 - dim))
    return factor_of


def length_profile(count, total, reach, slope):
    weights = [(1 << 20) // math.isqrt(rank ** slope) + 1 for rank in range(2, count + 1)]
    surplus, holding = total - reach - (count - 1), [1] * (count - 1)
    while surplus > 0:
        movable = [i for i in range(count - 1) if holding[i] < reach]
        whole, remaining = sum([weights[i] for i in movable]), surplus
        for i in movable:
            extra = min(reach - holding[i], max(1, remaining * weights[i] // whole), surplus)
            holding[i] = holding[i] + extra
            surplus = surplus - extra
    return np.array([reach] + holding)


def uneven_parts(stream_key, amount, total, limit, lean):
    if amount == 2:
        one = jax.random.randint(stream_key, (), max(1, total - limit), min(limit, total - 1) + 1)
        return jnp.stack([one, total - one])
    tallies = jnp.asarray(length_profile(amount, total, limit, lean), jnp.int32)
    couples = (amount - 1) // 2
    giver, receiver = tallies[1:1 + 2 * couples:2], tallies[2:2 + 2 * couples:2]
    slack = jnp.minimum(giver - 1, limit - receiver)
    passed = jax.random.randint(jax.random.fold_in(stream_key, 1), (couples,), 0, 1 << 20) % (slack + 1)
    tallies = tallies.at[1:1 + 2 * couples:2].set(giver - passed).at[2:2 + 2 * couples:2].set(receiver + passed)
    return tallies[jax.random.permutation(jax.random.fold_in(stream_key, 2), amount)]


def bell_draw(rng, dims, scale, bound, split=(), held_as=jnp.bfloat16):
    values = scale * jax.random.normal(rng, dims, jnp.float32)
    if split:
        values = values * steps_of(rng, dims, split, -0.22, 0.18)
    return jnp.clip(values, -bound, bound).astype(held_as)


def setup_inputs(seed: int = 0) -> dict:
    seeds = jax.random.split(jax.random.key(seed), 30)
    tokens = bell_draw(seeds[0], (MB, TOKENS, D), 1.0, 6.0, ((1, 32),))
    cotangent = bell_draw(seeds[1], (MB, TOKENS, D), 1.0, 6.0, ((1, 32),), jnp.float32)
    slot_order = jax.vmap(lambda own: jax.random.permutation(own, GRP))(jax.random.split(seeds[2], MB * N_DP)).reshape((MB, N_DP, GRP)).astype(jnp.int32)
    lengths = jax.vmap(lambda own: uneven_parts(own, NSEQ, GRP, MOST, 2))(jax.random.split(seeds[3], MB * N_DP)).reshape((MB, N_DP, NSEQ)).astype(jnp.int32)
    live_mask = touch_ends((jax.random.randint(seeds[4], (MB, N_DP, GRP), 0, 8) < 7).astype(jnp.int32), jax.random.fold_in(seeds[4], 1), 0, 1)
    w_in = bell_draw(seeds[5], (4, D, D), D ** -0.5, 0.1875, ((1, 8), (2, 4)), jnp.float32)
    w_out = bell_draw(seeds[6], (D, D), (D // 16) ** -0.5, 0.75, ((0, 4), (1, 8)), jnp.float32)
    w_ff = bell_draw(seeds[7], (2, D, FF), D ** -0.5, 0.1875, ((1, 8), (2, 4)), jnp.float32)
    w_down = bell_draw(seeds[8], (FF, D), (FF // 4) ** -0.5, 0.21875, ((0, 4), (1, 8)), jnp.float32)
    norm_gains = jnp.clip(1.0 + 0.1 * jax.random.normal(seeds[9], (2, D), jnp.float32), 0.5, 1.5)
    conv_taps = bell_draw(seeds[10], (3, TAPS, D), 0.5, 3.0, ((2, 4),), jnp.float32)
    decay_w = bell_draw(seeds[11], (D, H), (4 * D) ** -0.5, 0.09375, ((1, 4),), jnp.float32)
    mesa_bias = jnp.clip(-7.0 + 4.0 * jax.random.uniform(seeds[12], (2, H), jnp.float32) ** steps_of(seeds[12], (2, H), ((1, 4),), -0.2, 0.2), -7.0, -3.0)
    mom_in = bell_draw(seeds[13], (4, D, D), (0.12 * (MB * GRP) ** 0.5 / N_DP ** 0.5), 12.0, ((1, 8), (2, 4)), jnp.float32)
    mom_out = bell_draw(seeds[14], (D, D), (0.12 * (MB * GRP) ** 0.5 / N_DP ** 0.5), 12.0, ((0, 4), (1, 8)), jnp.float32)
    mom_ff = bell_draw(seeds[15], (2, D, FF), (0.12 * (MB * GRP) ** 0.5 / N_DP ** 0.5), 12.0, ((1, 8), (2, 4)), jnp.float32)
    mom_down = bell_draw(seeds[16], (FF, D), (0.12 * (MB * GRP) ** 0.5 / N_DP ** 0.5), 12.0, ((0, 4), (1, 8)), jnp.float32)
    mom_gains = bell_draw(seeds[17], (2, D), ((MB * GRP) ** 0.5 / N_DP ** 0.5), 96.0, (), jnp.float32)
    mom_conv = bell_draw(seeds[18], (3, TAPS, D), (0.03 * (MB * GRP) ** 0.5), 8.0, ((2, 4),), jnp.float32)
    mom_decay = bell_draw(seeds[19], (D, H), (0.03 * (MB * GRP) ** 0.5), 8.0, ((1, 4),), jnp.float32)
    mom_bias = bell_draw(seeds[20], (2, H), (0.03 * (MB * GRP) ** 0.5), 8.0, ((1, 4),), jnp.float32)
    err_in = bell_draw(seeds[21], (N_DP, 4, D, D), (0.05 * (MB * GRP) ** 0.5), 14.0, ((0, 8), (3, 4)), jnp.float32)
    err_out = bell_draw(seeds[22], (N_DP, D, D), (0.05 * (MB * GRP) ** 0.5), 14.0, ((0, 8), (1, 4)), jnp.float32)
    err_ff = bell_draw(seeds[23], (N_DP, 2, D, FF), (0.05 * (MB * GRP) ** 0.5), 14.0, ((0, 8), (3, 4)), jnp.float32)
    err_down = bell_draw(seeds[24], (N_DP, FF, D), (0.05 * (MB * GRP) ** 0.5), 14.0, ((0, 8), (1, 4)), jnp.float32)
    basis_in = bell_draw(seeds[25], (4, D, RANK), 1.0, 6.0, ((1, 4),), jnp.float32)
    basis_out = bell_draw(seeds[26], (N_TENSOR, D, RANK), 1.0, 6.0, ((0, 4),), jnp.float32)
    basis_ff = bell_draw(seeds[27], (2, FF, RANK), 1.0, 6.0, ((1, 4),), jnp.float32)
    basis_down = bell_draw(seeds[28], (N_TENSOR, D, RANK), 1.0, 6.0, ((0, 4),), jnp.float32)
    return {"tokens": tokens, "cotangent": cotangent, "slot_order": slot_order, "lengths": lengths, "live_mask": live_mask, "w_in": w_in, "w_out": w_out, "w_ff": w_ff, "w_down": w_down, "norm_gains": norm_gains, "conv_taps": conv_taps, "decay_w": decay_w, "mesa_bias": mesa_bias, "mom_in": mom_in, "mom_out": mom_out, "mom_ff": mom_ff, "mom_down": mom_down, "mom_gains": mom_gains, "mom_conv": mom_conv, "mom_decay": mom_decay, "mom_bias": mom_bias, "err_in": err_in, "err_out": err_out, "err_ff": err_ff, "err_down": err_down, "basis_in": basis_in, "basis_out": basis_out, "basis_ff": basis_ff, "basis_down": basis_down}


precise = lax.Precision.HIGHEST
tiny_eps = 1e-06
solve_floor = 0.01
momentum_decay = 0.5
step_rate = 1.0
small_rate = 0.05
ridge_shift = 9.0

@jax.custom_vjp
def low(v):
    return lax.optimization_barrier(v.astype(jnp.bfloat16)).astype(jnp.float32)

@jax.custom_vjp
def low_back(v):
    return v

def low_keep(v):
    return (low(v), None)

def low_pass(kept, grad):
    return (grad,)

def back_keep(v):
    return (v, None)

def back_low(kept, grad):
    return (low(grad),)
low.defvjp(low_keep, low_pass)
low_back.defvjp(back_keep, back_low)

def rms_norm(values, gain):
    return values * lax.rsqrt(lax.optimization_barrier(jnp.mean(values * values, axis=-1, keepdims=True)) + tiny_eps) * gain

def shift_rows(matrix, offset):
    return jnp.pad(matrix, ((offset, 0), (0, 0)))[:matrix.shape[0]]

def shift_ids(seg_ids, offset):
    return jnp.concatenate([jnp.full((offset,), -1, jnp.int32), seg_ids[:seg_ids.shape[0] - offset]])

def short_conv(projected, tap_weights, seg_ids):
    result = projected * tap_weights[0]
    for offset in range(1, tap_weights.shape[0]):
        same_seg = (shift_ids(seg_ids, offset) == seg_ids)[:, None]
        result = result + jnp.where(same_seg, shift_rows(projected, offset), 0.0) * tap_weights[offset]
    return result

def segment_ids(length_row, total_rows):
    seq_ends = jnp.cumsum(length_row).astype(jnp.int32)
    places = jnp.arange(total_rows, dtype=jnp.int32)
    return lax.optimization_barrier(jnp.sum((places[:, None] >= seq_ends[None, :]).astype(jnp.int32), axis=1)).astype(jnp.int32)

def mesa_head(queries, key_rows, values, log_decay, ridge_term, seg_ids):
    row_count, head_width = queries.shape
    block_count = row_count // STRETCH
    queries = queries.reshape(block_count, STRETCH, head_width)
    key_rows = key_rows.reshape(block_count, STRETCH, head_width)
    values = values.reshape(block_count, STRETCH, head_width)
    cumulative = jnp.cumsum(log_decay.reshape(block_count, STRETCH), axis=1)
    seg_block = seg_ids.reshape(block_count, STRETCH)
    previous = jnp.concatenate([jnp.full((1,), -1, jnp.int32), seg_block[:-1, -1]])
    from_start = jnp.where(seg_block == previous[:, None], jnp.exp(cumulative), 0.0)
    causal = jnp.arange(STRETCH)[:, None] >= jnp.arange(STRETCH)[None, :]
    allowed = causal[None] & (seg_block[:, :, None] == seg_block[:, None, :])
    spread = jnp.where(allowed, cumulative[:, :, None] - cumulative[:, None, :], 0.0)
    within = jnp.where(allowed, jnp.exp(spread), 0.0)
    last_seg = seg_block[:, -1:]
    to_end = jnp.where(seg_block == last_seg, jnp.exp(cumulative[:, -1:] - cumulative), 0.0)
    keep_end = jnp.where(last_seg[:, 0] == previous, jnp.exp(cumulative[:, -1]), 0.0)
    key_sums = jnp.einsum('ncd,nc,nce->nde', key_rows, to_end, key_rows, precision=precise)
    value_sums = jnp.einsum('ncv,nc,ncd->nvd', values, to_end, key_rows, precision=precise)

    def advance(state_pair, pieces):
        key_state, value_state = state_pair
        keep_now, key_add, value_add = pieces
        new_pair = (keep_now * key_state + key_add, keep_now * value_state + value_add)
        return (new_pair, state_pair)
    zero_state = jnp.zeros((head_width, head_width), jnp.float32)
    unused, starts = lax.scan(advance, (zero_state, zero_state), (keep_end, key_sums, value_sums))
    key_start, value_start = starts

    def apply_ridge(vectors):
        scores = jnp.einsum('ncd,ntd->nct', vectors, key_rows, precision=precise) * within
        inside = jnp.einsum('nct,ntd->ncd', scores, key_rows, precision=precise)
        state_part = jnp.einsum('ncd,nde->nce', vectors, key_start, precision=precise)
        return ridge_term * vectors + from_start[:, :, None] * state_part + inside

    def solve_raw(state_now):
        solved, residual, direction, norm_now = state_now
        image = apply_ridge(direction)
        curvature = lax.optimization_barrier(jnp.sum(direction * image, axis=2, keepdims=True))
        step_size = norm_now / (curvature + solve_floor)
        solved = solved + step_size * direction
        residual = residual - step_size * image
        norm_next = lax.optimization_barrier(jnp.sum(residual * residual, axis=2, keepdims=True))
        direction = residual + norm_next / (norm_now + solve_floor) * direction
        return (solved, residual, direction, norm_next)
    solve_step = jax.checkpoint(solve_raw)
    state_now = (jnp.zeros_like(queries), queries, queries, lax.optimization_barrier(jnp.sum(queries * queries, axis=2, keepdims=True)))
    for step_index in range(CG_STEPS):
        state_now = solve_step(state_now)
    solved = state_now[0]
    scores = jnp.einsum('ncd,ntd->nct', solved, key_rows, precision=precise) * within
    inside = jnp.einsum('nct,ntv->ncv', scores, values, precision=precise)
    state_part = jnp.einsum('ncd,nvd->ncv', solved, value_start, precision=precise)
    return (from_start[:, :, None] * state_part + inside).reshape(row_count, head_width)

def mixer_core(pre_q, pre_k, pre_v, pre_g, pre_a, tap_weights, head_rows, seg_ids, live_slots):
    row_count = pre_q.shape[0]
    head_count = pre_a.shape[1]
    head_width = pre_q.shape[1] // head_count

    def prepared(projected, taps_now):
        return jax.nn.silu(short_conv(projected, taps_now, seg_ids)).reshape(row_count, head_count, head_width)
    queries = prepared(pre_q, tap_weights[0])
    queries = queries * lax.rsqrt(lax.optimization_barrier(jnp.sum(queries * queries, axis=2, keepdims=True)) + tiny_eps)
    key_rows = prepared(pre_k, tap_weights[1])
    key_rows = key_rows * lax.rsqrt(lax.optimization_barrier(jnp.sum(key_rows * key_rows, axis=2, keepdims=True)) + tiny_eps) * live_slots[:, None, None]
    values = prepared(pre_v, tap_weights[2]) * live_slots[:, None, None]
    log_decay = -jax.nn.softplus(pre_a + head_rows[0])
    ridge_term = jax.nn.softplus(head_rows[1] + ridge_shift)
    solved = jax.vmap(mesa_head, in_axes=(1, 1, 1, 1, 0, None), out_axes=1)(queries, key_rows, values, log_decay, ridge_term, seg_ids)
    return solved.reshape(row_count, head_count * head_width) * jax.nn.sigmoid(pre_g)

def orthonormal(sketch):
    columns = []
    for position in range(sketch.shape[2]):
        column = sketch[:, :, position]
        for earlier in columns:
            column = column - lax.optimization_barrier(jnp.sum(earlier * column, axis=1, keepdims=True)) * earlier
        column = column * lax.rsqrt(lax.optimization_barrier(jnp.sum(column * column, axis=1, keepdims=True)) + tiny_eps)
        columns.append(column)
    return jnp.stack(columns, axis=2)

def matmul(left, right):
    return jnp.dot(left, right, precision=precise)

def layer_pack(token_rows, params, slot_order, inverse, seg_ids, live_slots):
    norm_gains, conv_taps, decay_w, mesa_bias, w_in, w_out, w_ff, w_down = params
    w_in = low(w_in)
    w_out = low(w_out)
    w_ff = low(w_ff)
    w_down = low(w_down)
    decay_w = low(decay_w)
    col_share = D // N_TENSOR
    hidden_share = FF // N_TENSOR
    head_share = H // N_TENSOR
    normed_one = low(rms_norm(token_rows, norm_gains[0]))
    mixed = jnp.zeros_like(token_rows)
    for shard_index in range(N_TENSOR):
        col_span = slice(shard_index * col_share, (shard_index + 1) * col_share)
        head_span = slice(shard_index * head_share, (shard_index + 1) * head_share)
        packed = low_back(normed_one)[slot_order]
        projected = [low_back(matmul(packed, w_in[slot_index][:, col_span])) for slot_index in range(4)]
        pre_a = low_back(matmul(packed, decay_w[:, head_span]))
        gated = mixer_core(projected[0], projected[1], projected[2], projected[3], pre_a, conv_taps[:, :, col_span], mesa_bias[:, head_span], seg_ids, live_slots)
        mix_term = low(matmul(low(gated), w_out[col_span, :]))
        mixed = mixed + mix_term[inverse]
    resid_one = token_rows + low_back(mixed)
    normed_two = low(rms_norm(resid_one, norm_gains[1]))
    ffn_total = jnp.zeros_like(token_rows)
    for shard_index in range(N_TENSOR):
        hidden_span = slice(shard_index * hidden_share, (shard_index + 1) * hidden_share)
        ffn_in = low_back(normed_two)
        gate_pre = low_back(matmul(ffn_in, w_ff[0][:, hidden_span]))
        up_pre = low_back(matmul(ffn_in, w_ff[1][:, hidden_span]))
        hidden = low(jax.nn.silu(gate_pre) * up_pre)
        ffn_total = ffn_total + low(matmul(hidden, w_down[hidden_span, :]))
    return resid_one + low_back(ffn_total)

def compress(matrices, basis_now):
    sketch = jnp.einsum('gsmn,snr->smr', matrices, basis_now, precision=precise) / N_DP
    frame = orthonormal(sketch)
    basis_new = jnp.einsum('gsmn,smr->snr', matrices, frame, precision=precise) / N_DP
    approx = jnp.einsum('smr,snr->smn', frame, basis_new, precision=precise)
    return (approx, basis_new, matrices - approx[None])

def by_columns(full, basis_all, share):
    pieces = [compress(full[..., shard_index * share:(shard_index + 1) * share], basis_all[:, shard_index * share:(shard_index + 1) * share]) for shard_index in range(N_TENSOR)]
    return (jnp.concatenate([piece[0] for piece in pieces], axis=2), jnp.concatenate([piece[1] for piece in pieces], axis=1), jnp.concatenate([piece[2] for piece in pieces], axis=3))

def by_rows(full, basis_all, share):
    pieces = [compress(full[:, None, shard_index * share:(shard_index + 1) * share, :], basis_all[shard_index][None]) for shard_index in range(N_TENSOR)]
    return (jnp.concatenate([piece[0][0] for piece in pieces], axis=0), jnp.concatenate([piece[1] for piece in pieces], axis=0), jnp.concatenate([piece[2][:, 0] for piece in pieces], axis=1))

def advance_weight(weight, moment, grad_now, rate):
    moment_new = momentum_decay * moment + grad_now
    return (weight - rate * moment_new, moment_new)

def reference(tokens, cotangent, slot_order, lengths, live_mask, w_in, w_out, w_ff, w_down, norm_gains, conv_taps, decay_w, mesa_bias, mom_in, mom_out, mom_ff, mom_down, mom_gains, mom_conv, mom_decay, mom_bias, err_in, err_out, err_ff, err_down, basis_in, basis_out, basis_ff, basis_down):
    params = (norm_gains, conv_taps, decay_w, mesa_bias, w_in, w_out, w_ff, w_down)

    def regroup(array):
        return jnp.swapaxes(array.reshape(MB, N_DP, GRP, D), 0, 1)
    inputs = (regroup(tokens.astype(jnp.float32)), regroup(cotangent), jnp.swapaxes(slot_order, 0, 1), jnp.swapaxes(lengths, 0, 1), jnp.swapaxes(live_mask, 0, 1))

    def per_group(state_unused, group_inputs):
        token_group, back_group, order_group, length_group, live_group = group_inputs
        grad_total = jax.tree.map(jnp.zeros_like, params)
        outs_now = []
        backs_now = []
        for micro_index in range(MB):
            order_now = order_group[micro_index]
            inverse = jnp.zeros((GRP,), jnp.int32).at[order_now].set(jnp.arange(GRP, dtype=jnp.int32))
            seg_ids = segment_ids(length_group[micro_index], GRP)
            live_slots = live_group[micro_index].astype(jnp.float32)

            def forward(token_rows, weights_now):
                return layer_pack(token_rows, weights_now, order_now, inverse, seg_ids, live_slots)
            result, pullback = jax.vjp(forward, token_group[micro_index], params)
            d_tok, d_params = pullback(back_group[micro_index])
            grad_total = jax.tree.map(jnp.add, grad_total, d_params)
            outs_now.append(result)
            backs_now.append(d_tok)
        return (state_unused, (jnp.stack(outs_now), jnp.stack(backs_now), grad_total))
    unused, scanned = lax.scan(per_group, 0, inputs)
    out_groups, back_groups, gradients = scanned
    out_tokens = jnp.swapaxes(out_groups, 0, 1).reshape(MB, TOKENS, D).astype(jnp.bfloat16)
    d_tokens = jnp.swapaxes(back_groups, 0, 1).reshape(MB, TOKENS, D)
    col_share = D // N_TENSOR
    hidden_share = FF // N_TENSOR
    approx_in, basis_in_new, err_in_new = by_columns(gradients[4] + err_in, basis_in, col_share)
    approx_out, basis_out_new, err_out_new = by_rows(gradients[5] + err_out, basis_out, col_share)
    approx_ff, basis_ff_new, err_ff_new = by_columns(gradients[6] + err_ff, basis_ff, hidden_share)
    approx_down, basis_down_new, err_down_new = by_rows(gradients[7] + err_down, basis_down, hidden_share)
    w_in_new, mom_in_new = advance_weight(w_in, mom_in, approx_in, step_rate)
    w_out_new, mom_out_new = advance_weight(w_out, mom_out, approx_out, step_rate)
    w_ff_new, mom_ff_new = advance_weight(w_ff, mom_ff, approx_ff, step_rate)
    w_down_new, mom_down_new = advance_weight(w_down, mom_down, approx_down, step_rate)
    gains_new, mom_gains_new = advance_weight(norm_gains, mom_gains, lax.optimization_barrier(jnp.sum(gradients[0], axis=0)) / N_DP, small_rate)
    conv_new, mom_conv_new = advance_weight(conv_taps, mom_conv, lax.optimization_barrier(jnp.sum(gradients[1], axis=0)) / N_DP, small_rate)
    decay_new, mom_decay_new = advance_weight(decay_w, mom_decay, lax.optimization_barrier(jnp.sum(gradients[2], axis=0)) / N_DP, small_rate)
    bias_new, mom_bias_new = advance_weight(mesa_bias, mom_bias, lax.optimization_barrier(jnp.sum(gradients[3], axis=0)) / N_DP, small_rate)
    return (out_tokens, d_tokens, w_in_new, mom_in_new, err_in_new, basis_in_new, w_out_new, mom_out_new, err_out_new, basis_out_new, w_ff_new, mom_ff_new, err_ff_new, basis_ff_new, w_down_new, mom_down_new, err_down_new, basis_down_new, gains_new, mom_gains_new, conv_new, mom_conv_new, decay_new, mom_decay_new, bias_new, mom_bias_new)
```

```python
import functools

import jax
import jax.numpy as jnp
from jax import lax
from jax.experimental import pallas as pl
from jax.experimental.pallas import tpu as pltpu
from jax.sharding import PartitionSpec as P

CG_STEPS = 8
BLK = 128
tiny_eps = 1e-06
solve_floor = 0.01
ridge_shift = 9.0
precise = lax.Precision.HIGHEST
F32 = jnp.float32
BF = jnp.bfloat16


def softplus(x):
    return jnp.maximum(x, 0.0) + jnp.log1p(jnp.exp(-jnp.abs(x)))


def mm(a, b):
    return jnp.dot(a, b, preferred_element_type=F32)


def nt(a, b):
    return lax.dot_general(a, b, (((1,), (1,)), ((), ())), preferred_element_type=F32)


def col_sum(x):
    return jnp.sum(x, axis=0, keepdims=True)


def start_of(lens_ref, places):
    begin = jnp.zeros_like(places)
    edge = jnp.int32(0)
    for item in range(lens_ref.shape[0] - 1):
        edge = edge + lens_ref[item]
        begin = jnp.where(places >= edge, edge, begin)
    return begin


def conv_masks(lens_ref, total, taps):
    places = lax.broadcasted_iota(jnp.int32, (1, total), 1)
    begin = start_of(lens_ref, places)
    return [(places - i >= begin).astype(F32) for i in range(taps)]


def conv_rows(rows, taps_now, masks):
    acc = rows * taps_now[:, 0:1]
    for i in range(1, len(masks)):
        acc = acc + (pltpu.roll(rows, i, 1) * masks[i]) * taps_now[:, i : i + 1]
    return acc


CHUNK = 16


def set_up(head, proj_ref, prea_ref, taps_ref, live_ref, lens_ref, bias_ref, sc):
    width, total = proj_ref.shape[1], proj_ref.shape[2]
    blocks = total // BLK
    taps = taps_ref.shape[2]
    masks = conv_masks(lens_ref, total, taps)
    live = live_ref[...]

    def squares(j, dst):
        def body(c, acc):
            at = pl.ds(pl.multiple_of(c * CHUNK, CHUNK), CHUNK)
            u = conv_rows(proj_ref[j, at, :], taps_ref[j, at, :], masks)
            x = u * jax.nn.sigmoid(u)
            dst[at, :] = x
            return acc + x * x

        acc = lax.fori_loop(0, width // CHUNK, body, jnp.zeros((CHUNK, total), F32))
        return lax.rsqrt(col_sum(acc) + tiny_eps)

    scale_q = squares(0, sc["q"])
    scale_k = squares(1, sc["x"])
    sc["scale"][0:1, :] = scale_q
    sc["scale"][1:2, :] = scale_k
    scale_k = scale_k * live
    for n in range(blocks):
        at = pl.ds(n * BLK, BLK)
        sc["q"][:, at] = sc["q"][:, at] * scale_q[:, n * BLK : (n + 1) * BLK]
        kt = sc["x"][:, at] * scale_k[:, n * BLK : (n + 1) * BLK]
        sc["kt"][:, at] = kt.astype(BF)
        sc["ks"][n, 0:BLK, :] = kt.T.astype(BF)
    squares(2, sc["x"])
    for n in range(blocks):
        at = pl.ds(n * BLK, BLK)
        vt = sc["x"][:, at] * live[:, n * BLK : (n + 1) * BLK]
        sc["vt"][:, at] = vt.astype(BF)
        if "vg" in sc:
            sc["vg"][n, 0:BLK, :] = vt.T.astype(BF)
    base = prea_ref[0, :, :] + jnp.full((1, total), bias_ref[0, head], F32)
    base = jnp.concatenate([base[:, n * BLK : (n + 1) * BLK] for n in range(blocks)], axis=0)
    forget = -softplus(base)
    row_i = lax.broadcasted_iota(jnp.int32, (BLK, BLK), 0)
    col_i = lax.broadcasted_iota(jnp.int32, (BLK, BLK), 1)
    cum = jnp.dot(forget, (row_i <= col_i).astype(F32), precision=precise, preferred_element_type=F32)
    first = lax.broadcasted_iota(jnp.int32, (blocks, BLK), 0) * BLK
    places = first + lax.broadcasted_iota(jnp.int32, (blocks, BLK), 1)
    begin = start_of(lens_ref, places)
    begin_last = start_of(lens_ref, first + (BLK - 1))
    end = jnp.broadcast_to(cum[:, BLK - 1 : BLK], cum.shape)
    from_start = jnp.where(begin < first, jnp.exp(cum), 0.0)
    to_end = jnp.where(places >= begin_last, jnp.exp(end - cum), 0.0)
    keep = jnp.where(begin_last < first, jnp.exp(end), 0.0)
    sc["dec"][0] = from_start
    sc["dec"][1] = to_end
    sc["dec"][2] = keep
    cum_col = jnp.transpose(cum)
    for n in range(blocks):
        spread = cum[n : n + 1, :] - cum_col[:, n : n + 1]
        allowed = (row_i <= col_i) & (row_i + n * BLK >= begin[n : n + 1, :])
        sc["dt"][n] = jnp.where(allowed, jnp.exp(jnp.where(allowed, spread, 0.0)), 0.0)
    state = jnp.zeros((2 * width, width), F32)
    for n in range(blocks):
        sc["ks"][n, BLK:, :] = state[:width].astype(BF)
        sc["g"][n] = state[width:].astype(BF)
        if "vg" in sc:
            sc["vg"][n, BLK:, :] = state[width:].T.astype(BF)
        if n + 1 < blocks:
            at = pl.ds(n * BLK, BLK)
            to_row = to_end[n : n + 1, :]
            scaled = jnp.concatenate(
                [sc["kt"][:, at].astype(F32) * to_row, sc["vt"][:, at].astype(F32) * to_row], axis=0
            ).astype(BF)
            state = keep[n : n + 1, :] * state + mm(scaled, sc["ks"][n, 0:BLK, :])
    return softplus(jnp.full((1, BLK), bias_ref[1, head], F32) + ridge_shift)


def apply_ridge(n, vec, lam, sc):
    at = pl.ds(n * BLK, BLK)
    both = mm(sc["ks"][n], vec.astype(BF))
    scores = (sc["dt"][n] * both[:BLK]).astype(BF)
    inside = mm(sc["kt"][:, at], scores)
    state_part = sc["dec"][0, n : n + 1, :] * both[BLK:]
    return lam * vec + state_part + inside, both, scores, state_part


def solve(lam, sc, keep_all):
    blocks = sc["dt"].shape[0]
    for n in range(blocks):
        at = pl.ds(n * BLK, BLK)
        q = sc["q"][:, at]
        sc["rho"][0:1, at] = col_sum(q * q)
        sc["z"][:, at] = jnp.zeros_like(q)
        if keep_all:
            sc["ph"][0, :, at] = q
        else:
            sc["p"][:, at] = q
            sc["r"][:, at] = q

    def step(i, last):
        for n in range(blocks):
            at = pl.ds(n * BLK, BLK)
            if keep_all:
                p = sc["ph"][i, :, at]
            else:
                p = sc["p"][:, at]
            rho = sc["rho"][0:1, at]
            w, both, scores, state_part = apply_ridge(n, p, lam, sc)
            inv_c = 1.0 / (col_sum(p * w) + solve_floor)
            s = rho * inv_c
            sc["z"][:, at] = sc["z"][:, at] + s * p
            if keep_all:
                sc["wh"][i, :, at] = w
                sc["bh"][i, n] = scores
                sc["sh"][i, 0:1, at] = s
                sc["sh"][i, 1:2, at] = inv_c
            if not last:
                if keep_all:
                    q = sc["q"][:, at]
                    r = jnp.where(i == 0, q, sc["rh"][jnp.maximum(i - 1, 0), :, at]) - s * w
                    sc["rh"][i, :, at] = r
                else:
                    r = sc["r"][:, at] - s * w
                    sc["r"][:, at] = r
                rho_next = col_sum(r * r)
                inv_rho = 1.0 / (rho + solve_floor)
                beta = rho_next * inv_rho
                p_next = r + beta * p
                sc["rho"][0:1, at] = rho_next
                if keep_all:
                    sc["ph"][i + 1, :, at] = p_next
                    sc["sh"][i, 2:3, at] = inv_rho
                    sc["sh"][i, 3:4, at] = beta
                else:
                    sc["p"][:, at] = p_next

    def body(i, carry):
        step(i, False)
        return carry

    lax.fori_loop(0, CG_STEPS - 1, body, 0)
    step(CG_STEPS - 1, True)


def forward_kernel(names, proj_ref, prea_ref, taps_ref, live_ref, lens_ref, bias_ref, out_ref, *scratch):
    sc = dict(zip(names, scratch))
    head = pl.program_id(0)
    lam = set_up(head, proj_ref, prea_ref, taps_ref, live_ref, lens_ref, bias_ref, sc)
    solve(lam, sc, False)
    for n in range(sc["dt"].shape[0]):
        at = pl.ds(n * BLK, BLK)
        z = sc["z"][:, at].astype(BF)
        scores = (sc["dt"][n] * mm(sc["ks"][n, 0:BLK, :], z)).astype(BF)
        o = mm(sc["vt"][:, at], scores) + sc["dec"][0, n : n + 1, :] * mm(sc["g"][n], z)
        out_ref[:, at] = (o * jax.nn.sigmoid(proj_ref[3, :, at])).astype(BF)


def backward_kernel(
    names, proj_ref, prea_ref, taps_ref, live_ref, dg_ref, lens_ref, bias_ref,
    dproj_ref, da_ref, dtaps_ref, dhead_ref, *scratch
):
    sc = dict(zip(names, scratch))
    head = pl.program_id(0)
    width, total = proj_ref.shape[1], proj_ref.shape[2]
    blocks = total // BLK
    lam = set_up(head, proj_ref, prea_ref, taps_ref, live_ref, lens_ref, bias_ref, sc)
    solve(lam, sc, True)
    row_i = lax.broadcasted_iota(jnp.int32, (BLK, BLK), 0)
    col_i = lax.broadcasted_iota(jnp.int32, (BLK, BLK), 1)
    dkt, dvt, zb, rb_s, pb_s = sc["dkt"], sc["dvt"], sc["zb"], sc["rb"], sc["pb"]
    dlam = jnp.zeros((1, BLK), F32)

    last = CG_STEPS - 1
    for n in range(blocks):
        at = pl.ds(n * BLK, BLK)
        dt = sc["dt"][n]
        from_row = sc["dec"][0, n : n + 1, :]
        z = sc["z"][:, at]
        z_low = z.astype(BF)
        scores = (dt * mm(sc["ks"][n, 0:BLK, :], z_low)).astype(BF)
        o = mm(sc["vt"][:, at], scores) + from_row * mm(sc["g"][n], z_low)
        sig = jax.nn.sigmoid(proj_ref[3, :, at])
        dg = dg_ref[:, at]
        dproj_ref[3, :, at] = (dg * o * sig * (1.0 - sig)).astype(BF)
        do = (dg * sig).astype(BF)
        both = mm(sc["vg"][n], do)
        d_scores = (dt * both[:BLK]).astype(BF)
        state_part = from_row * both[BLK:]
        zbar = state_part + mm(sc["kt"][:, at], d_scores)
        zb[:, at] = zbar
        dvt[:, at] = nt(do, scores)
        sc["dg0"][n] = nt(do, (from_row * z).astype(BF))
        p = sc["ph"][last, :, at]
        w = sc["wh"][last, :, at]
        s = sc["sh"][last, 0:1, at]
        inv_c = sc["sh"][last, 1:2, at]
        sbar = col_sum(zbar * p)
        cbar = -sbar * s * inv_c
        wb = (cbar * p).astype(BF)
        pb_s[:, at] = s * zbar + (2.0 * cbar) * w
        rb_s[:, at] = jnp.zeros_like(p)
        sc["rho"][0:1, at] = sbar * inv_c
        kept = sc["bh"][last, n]
        w_both = mm(sc["ks"][n], wb)
        w_scores = (dt * w_both[:BLK]).astype(BF)
        w_state = from_row * w_both[BLK:]
        p_low = p.astype(BF)
        dkt[:, at] = nt(z_low, d_scores) + nt(wb, kept) + nt(p_low, w_scores)
        sc["ds0"][n] = nt(wb, (from_row * p).astype(BF))
        sc["xm"][n] = scores.astype(F32) * both[:BLK] + kept.astype(F32) * w_both[:BLK]
        sc["fm"][0:1, at] = col_sum(z * state_part + p * w_state)
        sc["fm"][1:2, at] = col_sum(wb.astype(F32) * p)

    def body(it, carry):
        i = CG_STEPS - 2 - it
        for n in range(blocks):
            at = pl.ds(n * BLK, BLK)
            dt = sc["dt"][n]
            from_row = sc["dec"][0, n : n + 1, :]
            p = sc["ph"][i, :, at]
            w = sc["wh"][i, :, at]
            r_next = sc["rh"][i, :, at]
            s = sc["sh"][i, 0:1, at]
            inv_c = sc["sh"][i, 1:2, at]
            inv_rho = sc["sh"][i, 2:3, at]
            beta = sc["sh"][i, 3:4, at]
            zbar = zb[:, at]
            pb_next = pb_s[:, at]
            beta_bar = col_sum(pb_next * p)
            rho_next_bar = sc["rho"][0:1, at] + beta_bar * inv_rho
            rb = rb_s[:, at] + pb_next + (2.0 * rho_next_bar) * r_next
            sbar = col_sum(zbar * p - rb * w)
            cbar = -sbar * s * inv_c
            sc["rho"][0:1, at] = sbar * inv_c - beta_bar * beta * inv_rho
            wb32 = cbar * p - s * rb
            wb = wb32.astype(BF)
            image, w_both, w_scores, w_state = apply_ridge(n, wb32, lam, sc)
            pb_s[:, at] = beta * pb_next + s * zbar + cbar * w + image
            rb_s[:, at] = rb
            kept = sc["bh"][i, n]
            p_low = p.astype(BF)
            dkt[:, at] += nt(wb, kept) + nt(p_low, w_scores)
            sc["ds0"][n] += nt(wb, (from_row * p).astype(BF))
            sc["xm"][n] += kept.astype(F32) * w_both[:BLK]
            sc["fm"][0:1, at] += col_sum(p * w_state)
            sc["fm"][1:2, at] += col_sum(wb32 * p)
        return carry

    lax.fori_loop(0, CG_STEPS - 1, body, 0)

    d_sym = jnp.zeros((width, width), F32)
    d_g = jnp.zeros((width, width), F32)
    g_rows = [None] * blocks
    f_rows = [None] * blocks
    x_rows = [None] * blocks
    keep_rows = [None] * blocks
    lower = (row_i >= col_i).astype(BF)
    before = row_i < col_i
    for n in reversed(range(blocks)):
        at = pl.ds(n * BLK, BLK)
        kt = sc["kt"][:, at]
        to_row = sc["dec"][1, n : n + 1, :]
        keep = sc["dec"][2, n : n + 1, :]
        if n + 1 < blocks:
            vt = sc["vt"][:, at]
            g_low = d_g.astype(BF)
            part_s = to_row * mm(d_sym.astype(BF), kt)
            part_v = to_row * mm(g_low, kt)
            part_k = to_row * mm(d_g.T.astype(BF), vt)
            dkt[:, at] += part_s + part_k
            dvt[:, at] += part_v
            g_rows[n] = col_sum(0.5 * kt.astype(F32) * part_s + vt.astype(F32) * part_v)
            inner = 0.5 * d_sym * sc["ks"][n, BLK:, :].astype(F32) + d_g * sc["g"][n].astype(F32)
            keep_rows[n] = keep * jnp.sum(col_sum(inner), axis=1, keepdims=True)
        else:
            g_rows[n] = jnp.zeros((1, BLK), F32)
            keep_rows[n] = jnp.zeros((1, BLK), F32)
        ds0 = sc["ds0"][n]
        d_sym = keep * d_sym + ds0 + ds0.T
        d_g = keep * d_g + sc["dg0"][n]
        x = sc["xm"][n]
        high = x.astype(BF)
        low = (x - high.astype(F32)).astype(BF)
        summed = mm(high, lower) + mm(low, lower)
        x_rows[n] = col_sum(jnp.where(before, summed, 0.0))
        f_rows[n] = sc["fm"][0:1, at]
    f_all = jnp.concatenate(f_rows, axis=0)
    g_all = jnp.concatenate(g_rows, axis=0)
    da = (
        jnp.dot(f_all, (row_i >= col_i).astype(F32), precision=precise, preferred_element_type=F32)
        + jnp.dot(g_all, before.astype(F32), precision=precise, preferred_element_type=F32)
        + jnp.concatenate(x_rows, axis=0)
        + jnp.concatenate(keep_rows, axis=0)
    )
    da = jnp.concatenate([da[n : n + 1, :] for n in range(blocks)], axis=1)
    base = prea_ref[0, :, :] + jnp.full((1, total), bias_ref[0, head], F32)
    da = -jax.nn.sigmoid(base) * da
    da_ref[0, :, :] = da
    d_bias = jnp.sum(da, axis=1, keepdims=True)
    d_lam = jnp.sum(sc["fm"][1:2, :], axis=1, keepdims=True)
    d_lam = d_lam * jax.nn.sigmoid(jnp.full((1, BLK), bias_ref[1, head], F32) + ridge_shift)
    lane = lax.broadcasted_iota(jnp.int32, (1, BLK), 1)
    dhead_ref[0, :, :] = jnp.where(lane == 0, d_bias, d_lam)

    taps = taps_ref.shape[2]
    masks = conv_masks(lens_ref, total, taps)
    live = live_ref[...]
    scale_q = sc["scale"][0:1, :]
    scale_k = sc["scale"][1:2, :]

    def d_query(at):
        grad = rb_s[at, :] + pb_s[at, :] + (2.0 * sc["rho"][0:1, :]) * sc["q"][at, :]
        return grad

    def finish(j, grad_of, scale):
        def activated(at):
            u = conv_rows(proj_ref[j, at, :], taps_ref[j, at, :], masks)
            sig = jax.nn.sigmoid(u)
            return u, sig

        if scale is not None:

            def dots(c, acc):
                at = pl.ds(pl.multiple_of(c * CHUNK, CHUNK), CHUNK)
                u, sig = activated(at)
                return acc + (u * sig * scale) * grad_of(at)

            mean = col_sum(lax.fori_loop(0, width // CHUNK, dots, jnp.zeros((CHUNK, total), F32)))

        def body(c, carry):
            at = pl.ds(pl.multiple_of(c * CHUNK, CHUNK), CHUNK)
            u, sig = activated(at)
            grad = grad_of(at)
            if scale is not None:
                grad = scale * (grad - (u * sig * scale) * mean)
            du = grad * (sig * (1.0 + u * (1.0 - sig)))
            rows = proj_ref[j, at, :]
            taps_now = taps_ref[j, at, :]
            d_rows = du * taps_now[:, 0:1]
            sums = [jnp.sum(rows * du, axis=1, keepdims=True)]
            for i in range(1, taps):
                masked = du * masks[i]
                d_rows = d_rows + pltpu.roll(masked, total - i, 1) * taps_now[:, i : i + 1]
                sums.append(jnp.sum(pltpu.roll(rows, i, 1) * masked, axis=1, keepdims=True))
            dproj_ref[j, at, :] = d_rows.astype(BF)
            dtaps_ref[j, at, :] = jnp.concatenate(sums, axis=1)
            return carry

        lax.fori_loop(0, width // CHUNK, body, 0)

    finish(0, d_query, scale_q)
    finish(1, lambda at: dkt[at, :] * live, scale_k)
    finish(2, lambda at: dvt[at, :] * live, None)


def scratch_of(width, total, backward):
    blocks = total // BLK
    own = {
        "q": ((width, total), F32),
        "x": ((width, total), F32),
        "kt": ((width, total), BF),
        "vt": ((width, total), BF),
        "ks": ((blocks, 2 * BLK, width), BF),
        "g": ((blocks, width, width), BF),
        "dt": ((blocks, BLK, BLK), F32),
        "dec": ((3, blocks, BLK), F32),
        "scale": ((8, total), F32),
        "rho": ((8, total), F32),
        "z": ((width, total), F32),
    }
    if backward:
        own.update({
            "vg": ((blocks, 2 * BLK, width), BF),
            "ph": ((CG_STEPS, width, total), F32),
            "wh": ((CG_STEPS, width, total), F32),
            "rh": ((CG_STEPS, width, total), F32),
            "bh": ((CG_STEPS, blocks, BLK, BLK), BF),
            "sh": ((CG_STEPS, 8, total), F32),
            "dkt": ((width, total), F32),
            "dvt": ((width, total), F32),
            "zb": ((width, total), F32),
            "rb": ((width, total), F32),
            "pb": ((width, total), F32),
            "dg0": ((blocks, width, width), F32),
            "ds0": ((blocks, width, width), F32),
            "xm": ((blocks, BLK, BLK), F32),
            "fm": ((8, total), F32),
        })
    else:
        own.update({"p": ((width, total), F32), "r": ((width, total), F32)})
    return list(own), [pltpu.VMEM(shape, kind) for shape, kind in own.values()]


def mixer_forward(proj, pre_a, taps, live, lens, bias):
    slots, columns, total = proj.shape
    heads = pre_a.shape[0]
    width = columns // heads
    names, scratch = scratch_of(width, total, False)
    smem = pl.BlockSpec(memory_space=pltpu.SMEM)
    return pl.pallas_call(
        functools.partial(forward_kernel, names),
        grid=(heads,),
        in_specs=[
            pl.BlockSpec((slots, width, total), lambda h: (0, h, 0)),
            pl.BlockSpec((1, 1, total), lambda h: (h, 0, 0)),
            pl.BlockSpec((taps.shape[0], width, taps.shape[2]), lambda h: (0, h, 0)),
            pl.BlockSpec((1, total), lambda h: (0, 0)),
            smem,
            smem,
        ],
        out_specs=pl.BlockSpec((width, total), lambda h: (h, 0)),
        out_shape=jax.ShapeDtypeStruct((columns, total), BF),
        scratch_shapes=scratch,
        compiler_params=pltpu.CompilerParams(vmem_limit_bytes=56 * 2**20),
        name="mixer_forward",
    )(proj, pre_a, taps, live, lens, bias)


def mixer_backward(proj, pre_a, taps, live, d_gated, lens, bias):
    slots, columns, total = proj.shape
    heads = pre_a.shape[0]
    width = columns // heads
    names, scratch = scratch_of(width, total, True)
    smem = pl.BlockSpec(memory_space=pltpu.SMEM)
    kinds, count = taps.shape[0], taps.shape[2]
    return pl.pallas_call(
        functools.partial(backward_kernel, names),
        grid=(heads,),
        in_specs=[
            pl.BlockSpec((slots, width, total), lambda h: (0, h, 0)),
            pl.BlockSpec((1, 1, total), lambda h: (h, 0, 0)),
            pl.BlockSpec((kinds, width, count), lambda h: (0, h, 0)),
            pl.BlockSpec((1, total), lambda h: (0, 0)),
            pl.BlockSpec((width, total), lambda h: (h, 0)),
            smem,
            smem,
        ],
        out_specs=(
            pl.BlockSpec((slots, width, total), lambda h: (0, h, 0)),
            pl.BlockSpec((1, 1, total), lambda h: (h, 0, 0)),
            pl.BlockSpec((kinds, width, count), lambda h: (0, h, 0)),
            pl.BlockSpec((1, 1, BLK), lambda h: (h, 0, 0)),
        ),
        out_shape=(
            jax.ShapeDtypeStruct((slots, columns, total), BF),
            jax.ShapeDtypeStruct((heads, 1, total), F32),
            jax.ShapeDtypeStruct((kinds, columns, count), F32),
            jax.ShapeDtypeStruct((heads, 1, BLK), F32),
        ),
        scratch_shapes=scratch,
        compiler_params=pltpu.CompilerParams(vmem_limit_bytes=56 * 2**20),
        name="mixer_backward",
    )(proj, pre_a, taps, live, d_gated, lens, bias)


momentum_decay = 0.5
step_rate = 1.0
small_rate = 0.05


def rms_scale(values):
    return lax.rsqrt(jnp.mean(values * values, axis=-1, keepdims=True) + tiny_eps)


def rms_pull(values, scale, gain, grad):
    unit = values * scale
    scaled = grad * gain
    d_values = scale * (scaled - unit * jnp.mean(unit * scaled, axis=-1, keepdims=True))
    return d_values, jnp.sum(grad * unit, axis=0)


def swap(value, axis, flip):
    count = lax.axis_size(axis)
    return lax.ppermute(value, axis, [(i, i ^ flip) for i in range(count)])


def gather_rows(own):
    beside = swap(own, "tensor", 1)
    across = swap(own, "tensor", 2)
    corner = swap(across, "tensor", 1)
    return jnp.concatenate([own, beside, across, corner], axis=0)


def scatter_rows(terms):
    share = terms.shape[0] // 4
    low = terms.astype(jnp.bfloat16)
    from_beside = swap(jnp.concatenate([low[share : 2 * share], low[3 * share :]], axis=0), "tensor", 1)
    passed = terms[2 * share : 3 * share] + from_beside[share:].astype(jnp.float32)
    from_across = swap(passed.astype(jnp.bfloat16), "tensor", 2)
    mine = terms[:share] + from_beside[:share].astype(jnp.float32)
    return mine + from_across.astype(jnp.float32)


def total_over(values, axis):
    flip = 1
    while flip < lax.axis_size(axis):
        moved = [swap(v, axis, flip) for v in values]
        values = [a + b for a, b in zip(values, moved)]
        flip *= 2
    return values


def orthonormal_kernel(count, *refs):
    ranks = refs[0].shape[0]
    for source, target in zip(refs[:count], refs[count:]):
        columns = [source[r] for r in range(ranks)]
        for r in range(ranks):
            column = columns[r]
            column = column * lax.rsqrt(jnp.sum(column * column, axis=1, keepdims=True) + tiny_eps)
            target[r] = column
            for later in range(r + 1, ranks):
                dot = jnp.sum(column * columns[later], axis=1, keepdims=True)
                columns[later] = columns[later] - dot * column


def orthonormal(sketches):
    return pl.pallas_call(
        functools.partial(orthonormal_kernel, len(sketches)),
        out_shape=[jax.ShapeDtypeStruct(s.shape, s.dtype) for s in sketches],
        name="orthonormal",
    )(*sketches)


def project_left(merged, basis_now):
    return jnp.einsum("smn,snr->rsm", merged, basis_now, precision=precise)


def project_right(merged, frame):
    return jnp.einsum("smn,rsm->rsn", merged, frame, precision=precise)


def rebuild(frame, basis_new):
    return jnp.einsum("rsm,rsn->smn", frame, basis_new, precision=precise)


def advance_weight(weight, moment, grad_now, rate):
    moment_new = momentum_decay * moment + grad_now
    return (weight - rate * moment_new, moment_new)


def dot32(spec, a, b):
    return jnp.einsum(spec, a, b, preferred_element_type=jnp.float32)


def on_device(
    tokens,
    cotangent,
    slot_order,
    lengths,
    live_mask,
    w_in,
    w_out,
    w_ff,
    w_down,
    norm_gains,
    conv_taps,
    decay_w,
    mesa_bias,
    mom_in,
    mom_out,
    mom_ff,
    mom_down,
    mom_gains,
    mom_conv,
    mom_decay,
    mom_bias,
    err_in,
    err_out,
    err_ff,
    err_down,
    basis_in,
    basis_out,
    basis_ff,
    basis_down,
):
    dp_count = lax.axis_size("dp")
    dp_index = lax.axis_index("dp")
    mine = lax.axis_index("tensor")
    shard_count = lax.axis_size("tensor")
    micro_count, share, width = tokens.shape
    total = share * shard_count
    low_in = w_in.astype(jnp.bfloat16)
    low_out = w_out.astype(jnp.bfloat16)
    low_ff = w_ff.astype(jnp.bfloat16)
    low_down = w_down.astype(jnp.bfloat16)
    decay_low = decay_w.astype(jnp.bfloat16)
    weights_in = lax.all_gather(low_in, "dp", axis=1, tiled=True)
    weights_out = lax.all_gather(low_out, "dp", axis=1, tiled=True)
    weights_ff = lax.all_gather(low_ff, "dp", axis=1, tiled=True)
    weights_down = lax.all_gather(low_down, "dp", axis=1, tiled=True)
    taps_cols = jnp.transpose(conv_taps, (0, 2, 1))
    micros = range(micro_count)
    rows, scale_one, group_one, d_ffn, place, live, lens = [], [], [], [], [], [], []
    for m in micros:
        rows.append(tokens[m].astype(jnp.float32))
        scale_one.append(rms_scale(rows[m]))
        normed = rows[m] * scale_one[m] * norm_gains[0]
        group_one.append(gather_rows(normed.astype(jnp.bfloat16)))
        order_now = slot_order[m, 0]
        near = jnp.bitwise_xor(order_now // share, mine) * share + order_now % share
        slots = lax.broadcasted_iota(jnp.int32, (total, total), 1)
        place.append((near[:, None] == slots).astype(jnp.bfloat16))
        live.append(live_mask[m].astype(jnp.float32))
        lens.append(lengths[m, 0])
    for m in micros:
        d_ffn.append(gather_rows(cotangent[m].astype(jnp.bfloat16)))

    proj, pre_decay, gated_u, resid_one, scale_two, group_two = [], [], [], [], [], []
    for m in micros:
        packed = dot32("ji,id->jd", place[m], group_one[m]).astype(jnp.bfloat16)
        proj.append(dot32("jdc,td->jct", weights_in, packed))
        pre_decay.append(dot32("dh,td->ht", decay_low, packed)[:, None, :])
        gated = mixer_forward(proj[m], pre_decay[m], taps_cols, live[m], lens[m], mesa_bias)
        gated_u.append(dot32("cj,ji->ci", gated, place[m]).astype(jnp.bfloat16))
        mixed = scatter_rows(dot32("ci,cd->id", gated_u[m], weights_out))
        resid_one.append(rows[m] + mixed)
        scale_two.append(rms_scale(resid_one[m]))
        normed = resid_one[m] * scale_two[m] * norm_gains[1]
        group_two.append(gather_rows(normed.astype(jnp.bfloat16)))

    grad_down = jnp.zeros((w_down.shape[0], width), jnp.float32)
    grad_ff = jnp.zeros((2, width, w_ff.shape[2]), jnp.float32)
    out_list, d_two, d_resid, d_group = [], [], [], []
    grad_gains = []
    for m in micros:
        gate = dot32("td,dh->th", group_two[m], weights_ff[0])
        up = dot32("td,dh->th", group_two[m], weights_ff[1])
        gate_sig = jax.nn.sigmoid(gate)
        gate_act = gate * gate_sig
        hidden = (gate_act * up).astype(jnp.bfloat16)
        ffn = scatter_rows(dot32("th,hd->td", hidden, weights_down))
        out_list.append((resid_one[m] + ffn).astype(jnp.bfloat16))
        d_hidden = dot32("td,hd->th", d_ffn[m], weights_down)
        d_gate = (d_hidden * up * gate_sig * (1.0 + gate * (1.0 - gate_sig))).astype(jnp.bfloat16)
        d_up = (d_hidden * gate_act).astype(jnp.bfloat16)
        d_two = scatter_rows(
            dot32("th,dh->td", d_gate, weights_ff[0]) + dot32("th,dh->td", d_up, weights_ff[1])
        )
        grad_down = grad_down + dot32("th,td->hd", hidden, d_ffn[m])
        grad_ff = grad_ff + jnp.stack(
            [dot32("td,th->dh", group_two[m], d_gate), dot32("td,th->dh", group_two[m], d_up)]
        )
        d_part, d_gain = rms_pull(resid_one[m], scale_two[m], norm_gains[1], d_two)
        grad_gains.append(d_gain)
        d_resid.append(cotangent[m] + d_part)
        d_group.append(gather_rows(d_resid[m].astype(jnp.bfloat16)))

    grad_out = jnp.zeros((w_out.shape[0], width), jnp.float32)
    grad_in = jnp.zeros((4, width, w_in.shape[2]), jnp.float32)
    grad_decay = jnp.zeros(decay_w.shape, jnp.float32)
    grad_taps = jnp.zeros(taps_cols.shape, jnp.float32)
    grad_head = jnp.zeros((mesa_bias.shape[1], 1, BLK), jnp.float32)
    back_list = []
    gains_one = []
    for m in micros:
        grad_out = grad_out + dot32("ci,id->cd", gated_u[m], d_group[m])
        d_mix = dot32("ji,id->jd", place[m], d_group[m]).astype(jnp.bfloat16)
        d_gated = dot32("cd,td->ct", weights_out, d_mix)
        d_proj, d_decay, d_taps, d_head = mixer_backward(
            proj[m], pre_decay[m], taps_cols, live[m], d_gated, lens[m], mesa_bias
        )
        grad_taps = grad_taps + d_taps
        grad_head = grad_head + d_head
        d_proj = dot32("kcj,ji->kci", d_proj, place[m]).astype(jnp.bfloat16)
        d_decay = dot32("hj,ji->hi", d_decay[:, 0].astype(jnp.bfloat16), place[m]).astype(jnp.bfloat16)
        d_one = scatter_rows(
            dot32("kci,kdc->id", d_proj, weights_in) + dot32("hi,dh->id", d_decay, decay_low)
        )
        grad_in = grad_in + dot32("id,kci->kdc", group_one[m], d_proj)
        grad_decay = grad_decay + dot32("id,hi->dh", group_one[m], d_decay)
        d_part, d_gain = rms_pull(rows[m], scale_one[m], norm_gains[0], d_one)
        gains_one.append(d_gain)
        back_list.append(d_resid[m] + d_part)

    merged_in = grad_in + err_in[0]
    merged_out = grad_out[None] + err_out
    merged_ff = grad_ff + err_ff[0]
    merged_down = grad_down[None] + err_down
    merged = (merged_in, merged_out, merged_ff, merged_down)
    bases = (basis_in, basis_out, basis_ff, basis_down)
    early = total_over([project_left(merged[i], bases[i]) for i in (1, 2, 3)], "dp")
    frame_out, frame_ff, frame_down = orthonormal([s / dp_count for s in early])
    basis_early = total_over(
        [
            project_right(merged_out, frame_out),
            project_right(merged_ff, frame_ff),
            project_right(merged_down, frame_down),
        ],
        "dp",
    )
    late = total_over(
        [project_left(merged_in, basis_in), grad_taps, grad_decay, grad_head], "dp"
    )
    (frame_in,) = orthonormal([late[0] / dp_count])
    (basis_late,) = total_over([project_right(merged_in, frame_in)], "dp")
    grad_conv = jnp.transpose(late[1], (0, 2, 1))
    grad_decay = late[2]
    grad_bias = jnp.transpose(late[3][:, 0, :2])
    (gain_total,) = total_over([jnp.stack([sum(gains_one), sum(grad_gains)])], "tensor")
    (gain_total,) = total_over([gain_total], "dp")
    gain_total = gain_total / dp_count
    frames = (frame_in, frame_out, frame_ff, frame_down)
    sums = (basis_late, basis_early[0], basis_early[1], basis_early[2])
    basis_rows = [s / dp_count for s in sums]
    basis_in_new, basis_out_new, basis_ff_new, basis_down_new = (
        jnp.transpose(b, (1, 2, 0)) for b in basis_rows
    )
    approx_in, approx_out, approx_ff, approx_down = (
        rebuild(f, b) for f, b in zip(frames, basis_rows)
    )
    err_in_new = (merged_in - approx_in)[None]
    err_out_new = merged_out - approx_out
    err_ff_new = (merged_ff - approx_ff)[None]
    err_down_new = merged_down - approx_down

    def part(rows_of, count, axis):
        return lax.dynamic_slice_in_dim(rows_of, dp_index * count, count, axis)

    owned_in = rebuild(part(frame_in, w_in.shape[1], 2), basis_rows[0])
    owned_ff = rebuild(part(frame_ff, w_ff.shape[1], 2), basis_rows[2])
    owned_out = rebuild(frame_out, part(basis_rows[1], w_out.shape[1], 2))[0]
    owned_down = rebuild(frame_down, part(basis_rows[3], w_down.shape[1], 2))[0]
    w_in_new, mom_in_new = advance_weight(w_in, mom_in, owned_in, step_rate)
    w_out_new, mom_out_new = advance_weight(w_out, mom_out, owned_out, step_rate)
    w_ff_new, mom_ff_new = advance_weight(w_ff, mom_ff, owned_ff, step_rate)
    w_down_new, mom_down_new = advance_weight(w_down, mom_down, owned_down, step_rate)
    gains_new, mom_gains_new = advance_weight(norm_gains, mom_gains, gain_total, small_rate)
    conv_new, mom_conv_new = advance_weight(conv_taps, mom_conv, grad_conv / dp_count, small_rate)
    decay_new, mom_decay_new = advance_weight(decay_w, mom_decay, grad_decay / dp_count, small_rate)
    bias_new, mom_bias_new = advance_weight(mesa_bias, mom_bias, grad_bias / dp_count, small_rate)
    out_tokens = jnp.stack(out_list)
    d_tokens = jnp.stack(back_list)
    return (
        out_tokens,
        d_tokens,
        w_in_new,
        mom_in_new,
        err_in_new,
        basis_in_new,
        w_out_new,
        mom_out_new,
        err_out_new,
        basis_out_new,
        w_ff_new,
        mom_ff_new,
        err_ff_new,
        basis_ff_new,
        w_down_new,
        mom_down_new,
        err_down_new,
        basis_down_new,
        gains_new,
        mom_gains_new,
        conv_new,
        mom_conv_new,
        decay_new,
        mom_decay_new,
        bias_new,
        mom_bias_new,
    )


def solution(mesh):
    placed = (
        P(None, ("dp", "tensor"), None),
        P(None, ("dp", "tensor"), None),
        P(None, "dp", None),
        P(None, "dp", None),
        P(None, "dp", None),
        P(None, "dp", "tensor"),
        P("tensor", "dp"),
        P(None, "dp", "tensor"),
        P("tensor", "dp"),
        P(),
        P(None, None, "tensor"),
        P(None, "tensor"),
        P(None, "tensor"),
        P(None, "dp", "tensor"),
        P("tensor", "dp"),
        P(None, "dp", "tensor"),
        P("tensor", "dp"),
        P(),
        P(None, None, "tensor"),
        P(None, "tensor"),
        P(None, "tensor"),
        P("dp", None, None, "tensor"),
        P("dp", "tensor", None),
        P("dp", None, None, "tensor"),
        P("dp", "tensor", None),
        P(None, "tensor", None),
        P("tensor", None, None),
        P(None, "tensor", None),
        P("tensor", None, None),
    )
    return jax.shard_map(
        on_device,
        mesh=mesh,
        in_specs=placed,
        out_specs=(
            P(None, ("dp", "tensor"), None),
            P(None, ("dp", "tensor"), None),
            P(None, "dp", "tensor"),
            P(None, "dp", "tensor"),
            P("dp", None, None, "tensor"),
            P(None, "tensor", None),
            P("tensor", "dp"),
            P("tensor", "dp"),
            P("dp", "tensor", None),
            P("tensor", None, None),
            P(None, "dp", "tensor"),
            P(None, "dp", "tensor"),
            P("dp", None, None, "tensor"),
            P(None, "tensor", None),
            P("tensor", "dp"),
            P("tensor", "dp"),
            P("dp", "tensor", None),
            P("tensor", None, None),
            P(),
            P(),
            P(None, None, "tensor"),
            P(None, None, "tensor"),
            P(None, "tensor"),
            P(None, "tensor"),
            P(None, "tensor"),
            P(None, "tensor"),
        ),
        check_vma=False,
    )
```

```python
import functools
from types import SimpleNamespace

import jax
import jax.numpy as jnp
from jax import lax
from jax.experimental import pallas as pl
from jax.experimental.pallas import tpu as pltpu
from jax.sharding import PartitionSpec as P

CG_STEPS = 8
BLK = 128
tiny_eps = 1e-06
solve_floor = 0.01
ridge_shift = 9.0
precise = lax.Precision.HIGHEST
F32 = jnp.float32
BF = jnp.bfloat16


def softplus(x):
    return jnp.maximum(x, 0.0) + jnp.log1p(jnp.exp(-jnp.abs(x)))


def spot_of(i):
    return pl.ds(i * BLK, BLK)


def sigmoid(x):
    return 0.5 * jnp.tanh(0.5 * x) + 0.5


def mm(a, b):
    return jnp.dot(a, b, preferred_element_type=F32)


def nt(a, b):
    return lax.dot_general(a, b, (((1,), (1,)), ((), ())), preferred_element_type=F32)


def high_low(x, axis=0):
    high = x.astype(BF).astype(F32)
    return jnp.concatenate([high, x - high], axis=axis).astype(BF)


def halves(x):
    count = x.shape[0] // 2
    return x[:count] + x[count:]


def col_sum(x):
    return jnp.sum(x, axis=0, keepdims=True)


def start_of(lens_ref, places):
    begin = jnp.zeros_like(places)
    edge = jnp.int32(0)
    for item in range(lens_ref.shape[0] - 1):
        edge = edge + lens_ref[item]
        begin = jnp.where(places >= edge, edge, begin)
    return begin


def conv_masks(lens_ref, total, taps):
    places = lax.broadcasted_iota(jnp.int32, (1, total), 1)
    begin = start_of(lens_ref, places)
    return [(places - i >= begin).astype(F32) for i in range(taps)]


def conv_rows(rows, taps_now, sc):
    acc = rows * taps_now[:, 0:1]
    for i in range(1, taps_now.shape[1]):
        acc = acc + (pltpu.roll(rows, i, 1) * sc.mask[i]) * taps_now[:, i : i + 1]
    return acc


CHUNK = 16
TOGETHER = 8


def by_chunks(width, fn, init):
    def body(c, carry):
        for k in range(TOGETHER):
            carry = fn(pl.ds(pl.multiple_of((c * TOGETHER + k) * CHUNK, CHUNK), CHUNK), carry)
        return carry

    return lax.fori_loop(0, width // (CHUNK * TOGETHER), body, init)


def set_up(head, proj_ref, prea_ref, taps_ref, live_ref, lens_ref, bias_ref, sc, keep_all):
    width, total = proj_ref.shape[1], proj_ref.shape[2]
    blocks = total // BLK
    taps = taps_ref.shape[2]
    for i, mask in enumerate(conv_masks(lens_ref, total, taps)):
        sc.mask[i] = jnp.broadcast_to(mask, (CHUNK, total))
    live = live_ref[...]

    def squares(j, dst):
        def body(at, acc):
            u = conv_rows(proj_ref[j, at, :], taps_ref[j, at, :], sc)
            sig = sigmoid(u)
            x = u * sig
            dst[at, :] = x
            if keep_all:
                sc.slope[j, at, :] = sig + x * (1.0 - sig)
            return acc + x * x

        acc = by_chunks(width, body, jnp.zeros((CHUNK, total), F32))
        return lax.rsqrt(col_sum(acc) + tiny_eps)

    keys, values = (sc.xk, sc.xv) if keep_all else (sc.x, sc.x)

    scale_q = squares(0, sc.q)
    scale_k = squares(1, keys)
    sc.scale[0:1, :] = scale_q
    sc.scale[1:2, :] = scale_k
    scale_k = scale_k * live
    for n in range(blocks):
        at = pl.ds(n * BLK, BLK)
        sc.q[:, at] = sc.q[:, at] * scale_q[:, n * BLK : (n + 1) * BLK]
        kt = keys[:, at] * scale_k[:, n * BLK : (n + 1) * BLK]
        sc.kt[:, at] = kt.astype(BF)
        sc.ks[n, 0:BLK, :] = kt.T.astype(BF)
    squares(2, values)
    for n in range(blocks):
        at = pl.ds(n * BLK, BLK)
        vt = values[:, at] * live[:, n * BLK : (n + 1) * BLK]
        sc.vt[:, at] = vt.astype(BF)
        if keep_all:
            sc.vg[n, 0:BLK, :] = vt.T.astype(BF)
    base = prea_ref[0, :, :] + jnp.full((1, total), bias_ref[0, head], F32)
    base = jnp.concatenate([base[:, n * BLK : (n + 1) * BLK] for n in range(blocks)], axis=0)
    forget = -softplus(base)
    row_i = lax.broadcasted_iota(jnp.int32, (BLK, BLK), 0)
    col_i = lax.broadcasted_iota(jnp.int32, (BLK, BLK), 1)
    cum = jnp.dot(forget, (row_i <= col_i).astype(F32), precision=precise, preferred_element_type=F32)
    first = lax.broadcasted_iota(jnp.int32, (blocks, BLK), 0) * BLK
    places = first + lax.broadcasted_iota(jnp.int32, (blocks, BLK), 1)
    begin = start_of(lens_ref, places)
    begin_last = start_of(lens_ref, first + (BLK - 1))
    end = jnp.broadcast_to(cum[:, BLK - 1 : BLK], cum.shape)
    from_start = jnp.where(begin < first, jnp.exp(cum), 0.0)
    to_end = jnp.where(places >= begin_last, jnp.exp(end - cum), 0.0)
    keep = jnp.where(begin_last < first, jnp.exp(end), 0.0)
    sc.dec[0] = from_start
    sc.dec[1] = to_end
    sc.dec[2] = keep
    cum_col = jnp.transpose(cum)
    for n in range(blocks):
        spread = cum[n : n + 1, :] - cum_col[:, n : n + 1]
        allowed = (row_i <= col_i) & (row_i + n * BLK >= begin[n : n + 1, :])
        sc.dt[n] = jnp.where(allowed, jnp.exp(jnp.where(allowed, spread, 0.0)), 0.0)
    state = jnp.zeros((2 * width, width), F32)
    for n in range(blocks):
        sc.ks[n, BLK:, :] = state[:width].astype(BF)
        sc.g[n] = state[width:].astype(BF)
        if keep_all:
            sc.vg[n, BLK:, :] = state[width:].T.astype(BF)
        if n + 1 < blocks:
            at = pl.ds(n * BLK, BLK)
            to_row = to_end[n : n + 1, :]
            scaled = jnp.concatenate(
                [sc.kt[:, at].astype(F32) * to_row, sc.vt[:, at].astype(F32) * to_row], axis=0
            ).astype(BF)
            state = keep[n : n + 1, :] * state + mm(scaled, sc.ks[n, 0:BLK, :])
    return softplus(jnp.full((1, BLK), bias_ref[1, head], F32) + ridge_shift)


def solve(lam, sc, keep_all):
    blocks = sc.dt.shape[0]
    spans = [pl.ds(n * BLK, BLK) for n in range(blocks)]
    row = sc.row
    for n, at in enumerate(spans):
        q = sc.q[:, at]
        row[0, n : n + 1, :] = col_sum(q * q)
        sc.z[:, at] = jnp.zeros_like(q)
        sc.p[:, at] = q
        sc.r[:, at] = q
        sc.pl[:, at] = q.astype(BF)

    def step(i, last):
        spot = spot_of(i)
        for n, at in enumerate(spans):
            both = mm(sc.ks[n], sc.pl[:, at])
            scores = (sc.dt[n] * both[:BLK]).astype(BF)
            sc.sl[n] = scores
            sc.w[:, at] = sc.dec[0, n : n + 1, :] * both[BLK:]
            if keep_all:
                far = spot_of(CG_STEPS + i)
                sc.rh[n, :, spot] = scores
                sc.lh[n, :, far] = sc.pl[:, at]
        for n, at in enumerate(spans):
            p = sc.p[:, at]
            w = mm(sc.kt[:, at], sc.sl[n]) + sc.w[:, at] + lam * p
            rho = row[0, n : n + 1, :]
            inv_c = 1.0 / (col_sum(p * w) + solve_floor)
            s = rho * inv_c
            sc.z[:, at] = sc.z[:, at] + s * p
            if keep_all:
                sc.ph[i, :, at] = p
                sc.wh[i, :, at] = w
                sc.fh[n, :, spot] = (sc.dec[0, n : n + 1, :] * p).astype(BF)
                sc.sh[i, 0, n : n + 1, :] = s
                sc.sh[i, 1, n : n + 1, :] = inv_c
            if not last:
                r = sc.r[:, at] - s * w
                sc.r[:, at] = r
                rho_next = col_sum(r * r)
                inv_rho = 1.0 / (rho + solve_floor)
                beta = rho_next * inv_rho
                row[0, n : n + 1, :] = rho_next
                if keep_all:
                    sc.nh[i, :, at] = r
                    sc.sh[i, 2, n : n + 1, :] = inv_rho
                    sc.sh[i, 3, n : n + 1, :] = beta
                p = r + beta * p
                sc.p[:, at] = p
                sc.pl[:, at] = p.astype(BF)

    for i in range(CG_STEPS):
        step(i, i == CG_STEPS - 1)


def forward_kernel(names, head, proj_ref, prea_ref, taps_ref, live_ref, lens_ref, bias_ref, out_ref, *scratch):
    sc = SimpleNamespace(**dict(zip(names, scratch)))
    lam = set_up(head, proj_ref, prea_ref, taps_ref, live_ref, lens_ref, bias_ref, sc, False)
    solve(lam, sc, False)
    spans = [pl.ds(n * BLK, BLK) for n in range(sc.dt.shape[0])]
    for n, at in enumerate(spans):
        z = sc.z[:, at].astype(BF)
        sc.sl[n] = (sc.dt[n] * mm(sc.ks[n, 0:BLK, :], z)).astype(BF)
        sc.w[:, at] = sc.dec[0, n : n + 1, :] * mm(sc.g[n], z)
    for n, at in enumerate(spans):
        o = mm(sc.vt[:, at], sc.sl[n]) + sc.w[:, at]
        out_ref[:, at] = (o * sigmoid(proj_ref[3, :, at])).astype(BF)


def backward_kernel(
    names, head, proj_ref, prea_ref, taps_ref, live_ref, dg_ref, basis_ref, packed_ref, left_ref, lens_ref, bias_ref,
    dproj_ref, da_ref, dtaps_ref, dhead_ref, sketch_ref, *scratch
):
    sc = SimpleNamespace(**dict(zip(names, scratch)))
    width, total = proj_ref.shape[1], proj_ref.shape[2]
    blocks = total // BLK
    lam = set_up(head, proj_ref, prea_ref, taps_ref, live_ref, lens_ref, bias_ref, sc, True)
    solve(lam, sc, True)
    row_i = lax.broadcasted_iota(jnp.int32, (BLK, BLK), 0)
    col_i = lax.broadcasted_iota(jnp.int32, (BLK, BLK), 1)
    dkt, dvt, zb, rb_s, pb_s = sc.dkt, sc.dvt, sc.zb, sc.rb, sc.pb

    spans = [pl.ds(n * BLK, BLK) for n in range(blocks)]
    row = sc.row
    last = CG_STEPS - 1

    for n, at in enumerate(spans):
        z_low = sc.z[:, at].astype(BF)
        sc.pl[:, at] = z_low
        sc.sl[n] = (sc.dt[n] * mm(sc.ks[n, 0:BLK, :], z_low)).astype(BF)
        sc.w[:, at] = sc.dec[0, n : n + 1, :] * mm(sc.g[n], z_low)
    for n, at in enumerate(spans):
        o = mm(sc.vt[:, at], sc.sl[n]) + sc.w[:, at]
        sig = sigmoid(proj_ref[3, :, at])
        dg = dg_ref[:, at]
        dproj_ref[3, :, at] = (dg * o * sig * (1.0 - sig)).astype(BF)
        sc.do[:, at] = (dg * sig).astype(BF)
    for n, at in enumerate(spans):
        from_row = sc.dec[0, n : n + 1, :]
        z = sc.z[:, at]
        both = mm(sc.vg[n], sc.do[:, at])
        state_part = from_row * both[BLK:]
        zb[:, at] = state_part
        sc.sl2[n] = (sc.dt[n] * both[:BLK]).astype(BF)
        sc.xm[n] = sc.sl[n].astype(F32) * both[:BLK]
        sc.fm[0, n : n + 1, :] = col_sum(z * state_part)
        sc.p[:, at] = from_row * z
    for n, at in enumerate(spans):
        do = sc.do[:, at]
        zb[:, at] = zb[:, at] + mm(sc.kt[:, at], sc.sl2[n])
        dvt[:, at] = nt(do, sc.sl[n])
        sc.dg0[n] = nt(do, sc.p[:, at].astype(BF))
        dkt[:, at] = nt(sc.pl[:, at], sc.sl2[n])
    for at in spans:
        zero = jnp.zeros((width, BLK), F32)
        rb_s[:, at] = zero
        pb_s[:, at] = zero
        sc.nh[last, :, at] = zero
    sc.sh[last, 2] = jnp.zeros((blocks, BLK), F32)
    sc.sh[last, 3] = jnp.zeros((blocks, BLK), F32)
    row[0] = jnp.zeros((blocks, BLK), F32)
    sc.fm[1] = jnp.zeros((blocks, BLK), F32)

    def reverse_step(i):
        spot = spot_of(i)
        far = spot_of(CG_STEPS + i)
        s_all, inv_c, inv_rho, beta = sc.sh[i, 0], sc.sh[i, 1], sc.sh[i, 2], sc.sh[i, 3]
        for n, at in enumerate(spans):
            row[1, n : n + 1, :] = col_sum(pb_s[:, at] * sc.ph[i, :, at])
        beta_bar = row[1]
        row[2] = 2.0 * (row[0] + beta_bar * inv_rho)
        for n, at in enumerate(spans):
            rb = rb_s[:, at] + pb_s[:, at] + row[2, n : n + 1, :] * sc.nh[i, :, at]
            rb_s[:, at] = rb
            row[3, n : n + 1, :] = col_sum(zb[:, at] * sc.ph[i, :, at] - rb * sc.wh[i, :, at])
        sbar = row[3]
        row[4] = -sbar * s_all * inv_c
        row[0] = sbar * inv_c - beta_bar * beta * inv_rho
        for n, at in enumerate(spans):
            p = sc.ph[i, :, at]
            cbar = row[4, n : n + 1, :]
            s = sc.sh[i, 0, n : n + 1, :]
            wb = cbar * p - s * rb_s[:, at]
            low = wb.astype(BF)
            sc.pl[:, at] = low
            sc.lh[n, :, spot] = low
            sc.fm[1, n : n + 1, :] += col_sum(wb * p)
            pb_s[:, at] = (
                sc.sh[i, 3, n : n + 1, :] * pb_s[:, at]
                + s * zb[:, at]
                + cbar * sc.wh[i, :, at]
                + lam * wb
            )
        for n, at in enumerate(spans):
            both = mm(sc.ks[n], sc.pl[:, at])
            scores = (sc.dt[n] * both[:BLK]).astype(BF)
            sc.sl[n] = scores
            sc.rh[n, :, far] = scores
            sc.xm[n] += sc.rh[n, :, spot].astype(F32) * both[:BLK]
            state_part = sc.dec[0, n : n + 1, :] * both[BLK:]
            pb_s[:, at] = pb_s[:, at] + state_part
            sc.fm[0, n : n + 1, :] += col_sum(sc.ph[i, :, at] * state_part)
        for n, at in enumerate(spans):
            pb_s[:, at] = pb_s[:, at] + mm(sc.kt[:, at], sc.sl[n])

    for i in reversed(range(CG_STEPS)):
        reverse_step(i)
    half = CG_STEPS * BLK
    for n, at in enumerate(spans):
        dkt[:, at] += nt(sc.lh[n], sc.rh[n])
        sc.ds0[n] = nt(sc.lh[n, :, 0:half], sc.fh[n])

    d_sym = jnp.zeros((width, width), F32)
    d_g = jnp.zeros((width, width), F32)
    g_rows = [None] * blocks
    f_rows = [None] * blocks
    x_rows = [None] * blocks
    keep_rows = [None] * blocks
    lower = (row_i >= col_i).astype(BF)
    before = row_i < col_i
    for n in reversed(range(blocks)):
        at = pl.ds(n * BLK, BLK)
        kt = sc.kt[:, at]
        to_row = sc.dec[1, n : n + 1, :]
        keep = sc.dec[2, n : n + 1, :]
        if n + 1 < blocks:
            vt = sc.vt[:, at]
            g_low = d_g.astype(BF)
            part_s = to_row * mm(d_sym.astype(BF), kt)
            part_v = to_row * mm(g_low, kt)
            part_k = to_row * mm(d_g.T.astype(BF), vt)
            dkt[:, at] += part_s + part_k
            dvt[:, at] += part_v
            g_rows[n] = col_sum(0.5 * kt.astype(F32) * part_s + vt.astype(F32) * part_v)
            inner = 0.5 * d_sym * sc.ks[n, BLK:, :].astype(F32) + d_g * sc.g[n].astype(F32)
            keep_rows[n] = keep * jnp.sum(col_sum(inner), axis=1, keepdims=True)
        else:
            g_rows[n] = jnp.zeros((1, BLK), F32)
            keep_rows[n] = jnp.zeros((1, BLK), F32)
        ds0 = sc.ds0[n]
        d_sym = keep * d_sym + ds0 + ds0.T
        d_g = keep * d_g + sc.dg0[n]
        x = sc.xm[n]
        high = x.astype(BF)
        low = (x - high.astype(F32)).astype(BF)
        summed = mm(high, lower) + mm(low, lower)
        x_rows[n] = col_sum(jnp.where(before, summed, 0.0))
        f_rows[n] = sc.fm[0, n : n + 1, :]
    f_all = jnp.concatenate(f_rows, axis=0)
    g_all = jnp.concatenate(g_rows, axis=0)
    da = (
        jnp.dot(f_all, (row_i >= col_i).astype(F32), precision=precise, preferred_element_type=F32)
        + jnp.dot(g_all, before.astype(F32), precision=precise, preferred_element_type=F32)
        + jnp.concatenate(x_rows, axis=0)
        + jnp.concatenate(keep_rows, axis=0)
    )
    da = jnp.concatenate([da[n : n + 1, :] for n in range(blocks)], axis=1)
    base = prea_ref[0, :, :] + jnp.full((1, total), bias_ref[0, head], F32)
    da = -sigmoid(base) * da
    da_ref[0, :, :] = da
    d_bias = jnp.sum(da, axis=1, keepdims=True)
    d_lam = jnp.sum(col_sum(sc.fm[1]), axis=1, keepdims=True)
    d_lam = d_lam * sigmoid(jnp.full((1, BLK), bias_ref[1, head], F32) + ridge_shift)
    lane = lax.broadcasted_iota(jnp.int32, (1, BLK), 1)
    dhead_ref[0, :, :] = jnp.where(lane == 0, d_bias, d_lam)

    taps = taps_ref.shape[2]
    live = live_ref[...]
    scale_k = sc.scale[1:2, :]
    rho_bar = jnp.concatenate([row[0, n : n + 1, :] for n in range(blocks)], axis=1)
    sc.wide[0] = jnp.broadcast_to(2.0 * rho_bar, (CHUNK, total))
    sc.wide[1] = jnp.broadcast_to(sc.scale[0:1, :], (CHUNK, total))
    sc.wide[2] = jnp.broadcast_to(live, (CHUNK, total))
    sc.wide[3] = jnp.broadcast_to(scale_k, (CHUNK, total))

    def query_grad(at, acc):
        q = sc.q[at, :]
        grad = rb_s[at, :] + pb_s[at, :] + sc.wide[0] * q
        pb_s[at, :] = grad
        return acc + q * grad

    def key_grad(at, acc):
        grad = dkt[at, :] * sc.wide[2]
        dkt[at, :] = grad
        return acc + (sc.xk[at, :] * sc.wide[3]) * grad

    zero = jnp.zeros((CHUNK, total), F32)
    mean_q = col_sum(by_chunks(width, query_grad, zero))
    mean_k = col_sum(by_chunks(width, key_grad, zero))
    sc.wide[0] = jnp.broadcast_to(mean_q, (CHUNK, total))
    sc.wide[4] = jnp.broadcast_to(mean_k, (CHUNK, total))

    def through(j, at, du):
        taps_now = taps_ref[j, at, :]
        rows = proj_ref[j, at, :]
        d_rows = du * taps_now[:, 0:1]
        sums = [jnp.sum(rows * du, axis=1, keepdims=True)]
        for i in range(1, taps):
            moved = pltpu.roll(du * sc.mask[i], total - i, 1)
            d_rows = d_rows + moved * taps_now[:, i : i + 1]
            sums.append(jnp.sum(rows * moved, axis=1, keepdims=True))
        dproj_ref[j, at, :] = d_rows.astype(BF)
        dtaps_ref[j, at, :] = jnp.concatenate(sums, axis=1)

    def query_rows(at, carry):
        grad = sc.wide[1] * (pb_s[at, :] - sc.q[at, :] * sc.wide[0])
        through(0, at, grad * sc.slope[0, at, :])
        return carry

    def key_rows(at, carry):
        scale = sc.wide[3]
        grad = scale * (dkt[at, :] - (sc.xk[at, :] * scale) * sc.wide[4])
        through(1, at, grad * sc.slope[1, at, :])
        return carry

    def value_rows(at, carry):
        through(2, at, (dvt[at, :] * sc.wide[2]) * sc.slope[2, at, :])
        return carry

    for fn in (query_rows, key_rows, value_rows):
        by_chunks(width, fn, 0)

    slots, rank = basis_ref.shape[0], basis_ref.shape[1]
    inner = jnp.concatenate(
        [high_low(halves(mm(high_low(basis_ref[j]), dproj_ref[j]))) for j in range(slots)], axis=0
    )
    both = mm(inner, packed_ref[...])
    deep = packed_ref.shape[1]
    for j in range(slots):
        at = slice(j * deep, (j + 1) * deep)
        sketch_ref[:, at] = left_ref[:, at] + halves(both[2 * rank * j : 2 * rank * (j + 1)])
    if left_ref.shape[1] > slots * deep:
        sketch_ref[:, slots * deep :] = left_ref[:, slots * deep :]


def scratch_of(width, total, backward):
    blocks = total // BLK
    flat = ((width, total), F32)
    flat_low = ((width, total), BF)
    square = ((blocks, BLK, BLK), F32)
    square_low = ((blocks, BLK, BLK), BF)
    own = dict(
        q=flat,
        mask=((4, CHUNK, total), F32),
        kt=flat_low,
        vt=flat_low,
        ks=((blocks, 2 * BLK, width), BF),
        g=square_low,
        dt=square,
        dec=((3, blocks, BLK), F32),
        scale=((8, total), F32),
        row=((5, blocks, BLK), F32),
        z=flat,
        p=flat,
        r=flat,
        w=flat,
        pl=flat_low,
        sl=square_low,
    )
    if backward:
        history = ((CG_STEPS, width, total), F32)
        own.update(
            xk=flat,
            xv=flat,
            slope=((3, width, total), F32),
            wide=((5, CHUNK, total), F32),
            vg=((blocks, 2 * BLK, width), BF),
            ph=history,
            wh=history,
            nh=history,
            lh=((blocks, width, 2 * CG_STEPS * BLK), BF),
            rh=((blocks, BLK, 2 * CG_STEPS * BLK), BF),
            fh=((blocks, width, CG_STEPS * BLK), BF),
            sh=((CG_STEPS, 4, blocks, BLK), F32),
            do=flat_low,
            sl2=square_low,
            dkt=flat,
            dvt=flat,
            zb=flat,
            rb=flat,
            pb=flat,
            dg0=square,
            ds0=square,
            xm=square,
            fm=((2, blocks, BLK), F32),
        )
    else:
        own.update(x=flat)
    return list(own), [pltpu.VMEM(shape, kind) for shape, kind in own.values()]


def mixer_call(kernel, backward, head, arrays, lens, bias, deps, cost):
    proj, pre_a, taps, live = arrays[:4]
    slots, columns, total = proj.shape
    heads = pre_a.shape[0]
    width = columns // heads
    names, scratch = scratch_of(width, total, backward)
    smem = pl.BlockSpec(memory_space=pltpu.SMEM)
    kinds, count = taps.shape[0], taps.shape[2]
    in_specs = [
        pl.BlockSpec((slots, width, total), lambda g: (0, head, 0)),
        pl.BlockSpec((1, 1, total), lambda g: (head, 0, 0)),
        pl.BlockSpec((kinds, width, count), lambda g: (0, head, 0)),
        pl.BlockSpec((1, total), lambda g: (0, 0)),
    ]
    if backward:
        basis, packed, left = arrays[5:]
        in_specs += [
            pl.BlockSpec((width, total), lambda g: (head, 0)),
            pl.BlockSpec((slots, basis.shape[1], width), lambda g: (0, 0, head)),
            pl.BlockSpec(packed.shape, lambda g: (0, 0)),
            pl.BlockSpec(left.shape, lambda g: (0, 0)),
        ]
        out_specs = (
            pl.BlockSpec((slots, width, total), lambda g: (0, 0, 0)),
            pl.BlockSpec((1, 1, total), lambda g: (0, 0, 0)),
            pl.BlockSpec((kinds, width, count), lambda g: (0, 0, 0)),
            pl.BlockSpec((1, 1, BLK), lambda g: (0, 0, 0)),
            pl.BlockSpec(left.shape, lambda g: (0, 0)),
        )
        out_shape = (
            jax.ShapeDtypeStruct((slots, width, total), BF),
            jax.ShapeDtypeStruct((1, 1, total), F32),
            jax.ShapeDtypeStruct((kinds, width, count), F32),
            jax.ShapeDtypeStruct((1, 1, BLK), F32),
            jax.ShapeDtypeStruct(left.shape, F32),
        )
    else:
        out_specs = pl.BlockSpec((width, total), lambda g: (0, 0))
        out_shape = jax.ShapeDtypeStruct((width, total), BF)
    in_specs += [smem, smem] + [pl.BlockSpec(memory_space=pl.ANY)] * len(deps)
    own = len(arrays) + 2

    def body(*refs):
        kernel(names, head, *refs[:own], *refs[own + len(deps) :])

    return pl.pallas_call(
        body,
        grid=(1,),
        in_specs=in_specs,
        out_specs=out_specs,
        out_shape=out_shape,
        scratch_shapes=scratch,
        compiler_params=pltpu.CompilerParams(vmem_limit_bytes=56 * 2**20),
        cost_estimate=pl.CostEstimate(flops=cost * 10**9, bytes_accessed=cost * 3 * 10**6, transcendentals=0),
        name="mixer_backward" if backward else "mixer_forward",
    )(*arrays, lens, bias, *deps)


def mixer_forward(head, proj, pre_a, taps, live, lens, bias, deps=()):
    return mixer_call(forward_kernel, False, head, (proj, pre_a, taps, live), lens, bias, deps, 11)


def mixer_backward(head, proj, pre_a, taps, live, d_gated, basis, packed, left, lens, bias, deps=()):
    arrays = (proj, pre_a, taps, live, d_gated, basis, packed, left)
    return mixer_call(backward_kernel, True, head, arrays, lens, bias, deps, 28)


def any_specs(deps):
    return [pl.BlockSpec(memory_space=pl.ANY)] * len(deps)


def row_of(pair, k):
    return pair, pl.BlockSpec((pl.squeezed,) + pair.shape[1:], lambda g: (k, 0, 0))


def call(body, name, inputs, outs, deps=(), cost=1):
    whole = pl.BlockSpec(memory_space=pltpu.VMEM)
    count = len(inputs)

    def kernel(*refs):
        body(*refs[:count], *refs[count + len(deps) :])

    kinds = [i[1] if isinstance(i, tuple) else whole for i in inputs]
    inputs = [i[0] if isinstance(i, tuple) else i for i in inputs]
    return pl.pallas_call(
        kernel,
        grid=(1,),
        in_specs=kinds + any_specs(deps),
        out_specs=[whole] * len(outs),
        out_shape=[jax.ShapeDtypeStruct(*o) for o in outs],
        compiler_params=pltpu.CompilerParams(vmem_limit_bytes=56 * 2**20),
        cost_estimate=pl.CostEstimate(flops=cost * 10**9, bytes_accessed=cost * 3 * 10**6, transcendentals=0),
        name=name,
    )(*inputs, *deps)


def pass_on(keep, received, deps=()):
    def body(keep_ref, got_ref, out_ref):
        out_ref[...] = (keep_ref[...].astype(F32) + got_ref[...].astype(F32)).astype(BF)

    return call(body, "pass_on", [row_of(keep, 1), row_of(received, 1)], [(keep.shape[1:], BF)], deps)[0]


def second_norm(tokens, keep, beside, across, gain, deps=()):
    def body(x_ref, keep_ref, beside_ref, across_ref, gain_ref, resid_ref, normed_ref):
        x = x_ref[...].astype(F32)
        x = x + (keep_ref[...].astype(F32) + beside_ref[...].astype(F32) + across_ref[...].astype(F32))
        resid_ref[...] = x
        scale = lax.rsqrt(jnp.mean(x * x, axis=1, keepdims=True) + tiny_eps)
        normed_ref[...] = (x * scale * gain_ref[...]).astype(BF)

    return call(
        body, "second_norm", [tokens, row_of(keep, 0), row_of(beside, 0), across, gain],
        [(tokens.shape, F32), (tokens.shape, BF)], deps,
    )


def pulled_back(x, keep, beside, across, gain):
    grad = keep.astype(F32) + beside.astype(F32) + across.astype(F32)
    x = x.astype(F32)
    scale = lax.rsqrt(jnp.mean(x * x, axis=1, keepdims=True) + tiny_eps)
    unit = x * scale
    scaled = grad * gain
    return scale * (scaled - unit * jnp.mean(unit * scaled, axis=1, keepdims=True)), grad, unit


def norm_back(base, x, keep, beside, across, gain, deps=()):
    def body(base_ref, x_ref, keep_ref, beside_ref, across_ref, gain_ref, out_ref, low_ref, gain_out_ref):
        back, grad, unit = pulled_back(x_ref[...], keep_ref[...], beside_ref[...], across_ref[...], gain_ref[...])
        out = base_ref[...] + back
        out_ref[...] = out
        low_ref[...] = out.astype(BF)
        gain_out_ref[...] = col_sum(grad * unit)

    return call(
        body, "norm_back", [base, x, row_of(keep, 0), row_of(beside, 0), across, gain],
        [(x.shape, F32), (x.shape, BF), (gain.shape, F32)], deps,
    )


def norm_back_into(target, m, count, base, x, keep, beside, across, gain):
    share, width = base.shape

    def body(base_ref, x_ref, keep_ref, beside_ref, across_ref, gain_ref, *refs):
        back, grad, unit = pulled_back(x_ref[...], keep_ref[...], beside_ref[...], across_ref[...], gain_ref[...])
        refs[-1][...] = base_ref[...] + back

    inputs = [base, row_of(x, m), row_of(keep, 0), row_of(beside, 0), across, gain]
    whole = pl.BlockSpec(memory_space=pltpu.VMEM)
    old = [] if target is None else [target]
    return pl.pallas_call(
        body,
        grid=(1,),
        in_specs=[i[1] if isinstance(i, tuple) else whole for i in inputs] + any_specs(old),
        out_specs=pl.BlockSpec((pl.squeezed, share, width), lambda g: (m, 0, 0)),
        out_shape=jax.ShapeDtypeStruct((count, share, width), F32),
        input_output_aliases={len(inputs): 0} if old else {},
        name="norm_back_into",
    )(*[i[0] if isinstance(i, tuple) else i for i in inputs], *old)


def add_rows(resid, parts, across, deps=()):
    count = len(resid)
    shape = (count,) + resid[0].shape

    def body(*refs):
        out_ref = refs[-1]
        for m in range(count):
            x, keep, beside, far = (r[...] for r in refs[4 * m : 4 * m + 4])
            out_ref[m] = (x + (keep.astype(F32) + beside.astype(F32) + far.astype(F32))).astype(BF)

    inputs = []
    for x, (keep, beside), far in zip(resid, parts, across):
        inputs += [x, row_of(keep, 0), row_of(beside, 0), far]
    return call(body, "add_rows", inputs, [(shape, BF)], deps)[0]


def ffn_pass(rows, grads, w_ff, basis_ff, basis_down, deps=()):
    share, width = rows[0].shape
    total = 4 * share
    hidden_width = w_ff.shape[2]
    rank = basis_ff.shape[1]
    tile = 2 * share

    def body(*refs):
        row_refs, grad_refs = refs[:4], refs[4:8]
        ff_ref, bff_ref, bdown_ref = refs[8:11]
        hidden_ref, dgu_ref, two_keep, two_send, ffn_keep, ffn_send, left_ff, left_down, x_s, dy_s = refs[11:]
        for k in range(4):
            x_s[k * share : (k + 1) * share, :] = row_refs[k][...]
            dy_s[k * share : (k + 1) * share, :] = grad_refs[k][...]
        left_ff[...] = jnp.zeros_like(left_ff)
        left_down[...] = jnp.zeros_like(left_down)

        def step(i, carry):
            at = pl.ds(pl.multiple_of(i * tile, tile), tile)
            x, dy = x_s[at, :], dy_s[at, :]
            gate = mm(x, ff_ref[0])
            up = mm(x, ff_ref[1])
            sig = jax.nn.sigmoid(gate)
            act = gate * sig
            hidden = (act * up).astype(BF)
            d_hidden = mm(dy, ff_ref[2])
            d_gate = (d_hidden * up * sig * (1.0 + gate * (1.0 - sig))).astype(BF)
            d_up = (d_hidden * act).astype(BF)
            hidden_ref[at, :] = hidden
            dgu_ref[0, at, :] = d_gate
            dgu_ref[1, at, :] = d_up
            two = (nt(d_gate, ff_ref[0]) + nt(d_up, ff_ref[1])).astype(BF)
            two_keep[i] = two[:share]
            two_send[i] = two[share:]
            ffn = nt(hidden, ff_ref[2]).astype(BF)
            ffn_keep[i] = ffn[:share]
            ffn_send[i] = ffn[share:]
            for j, d in enumerate((d_gate, d_up)):
                inner = halves(nt(high_low(bff_ref[j]), d))
                left_ff[j] += halves(mm(high_low(inner), x))
            inner = halves(nt(high_low(bdown_ref[...]), dy))
            left_down[...] += halves(mm(high_low(inner), hidden))
            return carry

        lax.fori_loop(0, 2, step, 0)

    pair = ((2, share, width), BF)
    return call(
        body, "ffn_pass", [*rows, *grads, w_ff, basis_ff, basis_down],
        [
            ((total, hidden_width), BF), ((2, total, hidden_width), BF), pair, pair, pair, pair,
            ((2, rank, width), F32), ((rank, hidden_width), F32), ((total, width), BF), ((total, width), BF),
        ],
        deps, cost=12,
    )


def add_steps(values, axis):
    flip, count = 1, lax.axis_size(axis)
    moved, deps = [jnp.zeros_like(v) for v in values], ()
    while flip < count:
        moved = [swap(v, axis, flip) for v in values]
        deps = yield values
        flip *= 2
        if flip < count:
            values = add_after(values, moved, deps)
    return values, moved, deps


def add_after(left, right, deps=()):
    count = len(left)

    def body(*refs):
        for k in range(count):
            refs[2 * count + k][...] = refs[k][...] + refs[count + k][...]

    return call(body, "add_after", [*left, *right], [(v.shape, v.dtype) for v in left], deps)


def finish_steps(steps, deps=None):
    try:
        if deps is None:
            next(steps)
        while True:
            steps.send(deps or ())
    except StopIteration as end:
        return end.value


def gate(value, deps):
    return pl.pallas_call(
        lambda *refs: None,
        in_specs=any_specs((value, *deps)),
        out_specs=pl.BlockSpec(memory_space=pl.ANY),
        out_shape=jax.ShapeDtypeStruct(value.shape, value.dtype),
        input_output_aliases={0: 0},
        name="gate",
    )(value, *deps)


def each_block(groups):
    out = []
    for k, (array, flipped) in enumerate(groups):
        count, m, n = array.shape
        m, n = (n, m) if flipped else (m, n)
        out += [(k, j, flipped, m, n) for j in range(count)]
    return out


def frames_and_basis(left, right, groups, count, deps=()):
    rank = left.shape[0]
    blocks = each_block(groups)

    def body(left_ref, right_ref, *refs):
        frame_ref, right_out = refs[len(groups) :]
        edge, edge_n = 0, 0
        for k, j, flipped, m, n in blocks:
            sketch = (left_ref[:, edge : edge + m] + right_ref[:, edge : edge + m]) * (1.0 / count)
            done = []
            for r in range(rank):
                column = sketch[0:1]
                column = column * lax.rsqrt(jnp.sum(column * column, axis=1, keepdims=True) + tiny_eps)
                done.append(column)
                if r + 1 < rank:
                    sketch = sketch[1:]
                    sketch = sketch - jnp.sum(column * sketch, axis=1, keepdims=True) * column
            frame = jnp.concatenate(done, axis=0)
            frame_ref[:, edge : edge + m] = frame
            right_out[:, edge_n : edge_n + n] = times_block(frame, refs[k][j], flipped)
            edge, edge_n = edge + m, edge_n + n

    return call(
        body, "frames_and_basis", [left, right] + [a for a, f in groups],
        [(left.shape, F32), ((rank, sum(b[4] for b in blocks)), F32)], deps,
    )


def times_block(few, block, transposed):
    both = high_low(few)
    high = block.astype(BF)
    low = (block - high.astype(F32)).astype(BF)
    by = nt if transposed else mm
    return halves(by(both, high)) + by(both, low)[: few.shape[0]]


def basis_and_errors(frame, left, right, groups, count, deps=()):
    blocks = each_block(groups)

    def body(frame_ref, left_ref, right_ref, *refs):
        basis_ref = refs[len(groups)]
        out_refs = refs[len(groups) + 1 :]
        edge, edge_n = 0, 0
        for k, j, flipped, m, n in blocks:
            basis = (left_ref[:, edge_n : edge_n + n] + right_ref[:, edge_n : edge_n + n]) * (1.0 / count)
            basis_ref[:, edge_n : edge_n + n] = basis
            frame = frame_ref[:, edge : edge + m]
            high_f, high_b = frame.astype(BF).astype(F32), basis.astype(BF).astype(F32)
            f = jnp.concatenate([high_f, frame - high_f, high_f, jnp.zeros_like(frame)], axis=0)
            b = jnp.concatenate([high_b, high_b, basis - high_b, jnp.zeros_like(basis)], axis=0)
            if flipped:
                f, b = b, f
            out_refs[k][j] = refs[k][j] - mm(f.T.astype(BF), b.astype(BF))
            edge, edge_n = edge + m, edge_n + n

    arrays = [a for a, f in groups]
    return call(
        body, "basis_and_errors", [frame, left, right, *arrays],
        [(left.shape, F32)] + [(a.shape, F32) for a in arrays], deps,
    )


def sketches(groups, bases, deps=()):
    rank = bases[0].shape[1]
    blocks = each_block(groups)

    def body(*refs):
        edge = 0
        for k, j, flipped, m, n in blocks:
            refs[-1][:, edge : edge + m] = times_block(refs[len(groups) + k][j], refs[k][j], not flipped)
            edge += m

    return call(
        body, "sketches", [a for a, f in groups] + bases, [((rank, sum(b[3] for b in blocks)), F32)], deps
    )[0]


momentum_decay = 0.5
step_rate = 1.0
small_rate = 0.05


def swap(value, axis, flip):
    count = lax.axis_size(axis)
    return lax.ppermute(value, axis, [(i, i ^ flip) for i in range(count)])


def gather_rows(own):
    beside = swap(own, "tensor", 1)
    across = swap(own, "tensor", 2)
    return [own, beside, across, swap(across, "tensor", 1)]


def advance_weight(weight, moment, grad_now, rate):
    moment_new = momentum_decay * moment + grad_now
    return (weight - rate * moment_new, moment_new)


def dot32(spec, a, b):
    return jnp.einsum(spec, a, b, preferred_element_type=jnp.float32)


def on_device(
    tokens,
    cotangent,
    slot_order,
    lengths,
    live_mask,
    w_in,
    w_out,
    w_ff,
    w_down,
    norm_gains,
    conv_taps,
    decay_w,
    mesa_bias,
    mom_in,
    mom_out,
    mom_ff,
    mom_down,
    mom_gains,
    mom_conv,
    mom_decay,
    mom_bias,
    err_in,
    err_out,
    err_ff,
    err_down,
    basis_in,
    basis_out,
    basis_ff,
    basis_down,
):
    dp_count = lax.axis_size("dp")
    dp_index = lax.axis_index("dp")
    mine = lax.axis_index("tensor")
    shard_count = lax.axis_size("tensor")
    micro_count, share, width = tokens.shape
    total = share * shard_count
    decay_low = decay_w.astype(BF)
    first = jnp.concatenate([w_in.astype(BF), jnp.transpose(w_out.astype(BF))[None]], axis=0)
    second = jnp.concatenate([w_ff.astype(BF), jnp.transpose(w_down.astype(BF))[None]], axis=0)
    weights_first = lax.all_gather(first, "dp", axis=1, tiled=True)
    weights_in = weights_first[:4]
    weights_out = weights_first[4]
    weights_ff = lax.all_gather(second, "dp", axis=1, tiled=True)
    taps_cols = jnp.transpose(conv_taps, (0, 2, 1))
    gain_one, gain_two = norm_gains[0:1], norm_gains[1:2]
    bases = [jnp.swapaxes(b, 1, 2) for b in (basis_in, basis_out, basis_ff, basis_down)]
    micros = range(micro_count)
    heads = range(mesa_bias.shape[1])
    last = micro_count - 1
    pieces_one, group_one, pieces_dy, place, live, lens = [], [], [], [], [], []
    for m in micros:
        row = tokens[m].astype(F32)
        scale = lax.rsqrt(jnp.mean(row * row, axis=1, keepdims=True) + tiny_eps)
        pieces_one.append(gather_rows((row * scale * gain_one).astype(BF)))
        group_one.append(jnp.concatenate(pieces_one[m], axis=0))
        order_now = slot_order[m, 0]
        near = jnp.bitwise_xor(order_now // share, mine) * share + order_now % share
        slots = lax.broadcasted_iota(jnp.int32, (total, total), 1)
        place.append((near[:, None] == slots).astype(BF))
        live.append(live_mask[m].astype(F32))
        lens.append(lengths[m, 0])

    packed, proj, pre_decay, gated_u = [], [], [], []
    resid, group_two, passed_mix, send_two, keep_mix, beside_mix = [], [], [], [], [], []

    def project(m):
        packed.append(dot32("ji,id->jd", place[m], group_one[m]).astype(BF))
        proj.append(dot32("jdc,td->jct", weights_in, packed[m]))
        pre_decay.append(dot32("dh,td->ht", decay_low, packed[m])[:, None, :])

    def forward(m, h, deps):
        return mixer_forward(h, proj[m], pre_decay[m], taps_cols, live[m], lens[m], mesa_bias, deps)

    def mix_out(m, gated):
        gated_u.append(dot32("cj,ji->ci", jnp.concatenate(gated, axis=0), place[m]).astype(BF))
        terms = dot32("ci,dc->id", gated_u[m], weights_out).astype(BF).reshape(2, 2, share, width)
        keep_mix.append(terms[:, 0])
        send = terms[:, 1]
        beside_mix.append(swap(send, "tensor", 1))
        return send

    def pass_mix(m, deps):
        passed_mix.append(pass_on(keep_mix[m], beside_mix[m], deps))

    def norm_two(m, deps):
        across = swap(passed_mix[m], "tensor", 2)
        own, low = second_norm(tokens[m], keep_mix[m], beside_mix[m], across, gain_two, deps)
        resid.append(own)
        send_two.append(low)
        group_two.append(gather_rows(low))

    err_ff_t = jnp.swapaxes(err_ff[0], 1, 2)
    err_left = sketches([(err_ff_t, True), (err_down, False)], [bases[2], bases[3]])
    left_in = sketches([(err_in[0], False)], [bases[0]])
    project(0)
    gated = [forward(0, h, (err_left, left_in)) for h in heads]
    for m in micros:
        pieces_dy.append(gather_rows(gate(cotangent[m].astype(BF), (gated[min(m, 1)],))))
    sent = mix_out(0, gated)
    project(1)
    pass_mix(0, (proj[1],))
    gated = [forward(1, 0, (passed_mix[0],))]
    norm_two(0, (gated[0],))
    gated.append(forward(1, 1, (send_two[0],)))
    sent = mix_out(1, gated)

    hidden, d_gate_up, two_keep, two_beside, two_passed, ffn_parts, left_ff, left_down = [[] for i in range(8)]
    rows_of_two, rows_of_dy = [], []

    def feed_forward(m, deps):
        h, dgu, keep, send, ffn_keep, ffn_send, lf, ld, rows_two, rows_dy = ffn_pass(
            group_two[m], pieces_dy[m], weights_ff, bases[2], bases[3][0], deps
        )
        hidden.append(h)
        d_gate_up.append(dgu)
        two_keep.append(keep)
        two_beside.append(swap(send, "tensor", 1))
        ffn_parts.append((ffn_keep, swap(ffn_send, "tensor", 1)))
        left_ff.append(lf)
        left_down.append(ld)
        rows_of_two.append(rows_two)
        rows_of_dy.append(rows_dy)
        return send

    d_resid, send_back, gains_two, d_group = [], [], [], []

    def back_two(m, deps):
        across = swap(two_passed[m], "tensor", 2)
        out, low, gain = norm_back(
            cotangent[m], resid[m], two_keep[m], two_beside[m], across, gain_two, deps
        )
        d_resid.append(out)
        send_back.append(low)
        gains_two.append(gain)
        d_group.append(gather_rows(low))

    def pass_two(m, deps):
        two_passed.append(pass_on(two_keep[m], two_beside[m], deps))

    def weight_grads(m):
        return dot32("jth,td->jhd", d_gate_up[m], rows_of_two[m]), dot32("th,td->hd", hidden[m], rows_of_dy[m])

    sent = feed_forward(0, (sent,))
    pass_mix(1, (sent,))
    grads_first = weight_grads(0)
    norm_two(1, grads_first)
    pass_two(0, (group_two[1][2],))
    sent = feed_forward(1, (two_passed[0],))
    back_two(0, (sent,))
    pass_two(1, (send_back[0],))
    grads_last = weight_grads(1)
    merged_early = [
        (grads_first[0] + grads_last[0] + err_ff_t, True),
        ((grads_first[1] + grads_last[1])[None] + err_down, False),
    ]
    left_ff = sum(left_ff)
    early = jnp.concatenate([left_ff[0], left_ff[1], sum(left_down)], axis=1) + err_left

    def factor_steps():
        (left,), (right,), deps = yield from add_steps([early], "dp")
        frame, own = frames_and_basis(left, right, merged_early, dp_count, deps)
        (left,), (right,), deps = yield from add_steps([own], "dp")
        return (frame,) + tuple(basis_and_errors(frame, left, right, merged_early, dp_count, deps))

    steps = factor_steps()
    next(steps)
    (waiting,) = steps.send((merged_early[0][0], merged_early[1][0]))
    grad_out, grad_in, grad_decay, grad_taps, grad_head = 0.0, 0.0, 0.0, 0.0, 0.0
    back_parts, ffn_passed, before_last = [], [], []
    for m in micros:
        grad_out = grad_out + dot32("ci,id->cd", gated_u[m], jnp.concatenate(d_group[m], axis=0))
        d_mix = dot32("ji,id->jd", place[m], jnp.concatenate(d_group[m], axis=0)).astype(BF)
        d_gated = dot32("dc,td->ct", weights_out, d_mix)
        pieces = []
        if m == last:
            merged_out = grad_out[None] + err_out
            left_in = jnp.concatenate([left_in, sketches([(merged_out, False)], [bases[1]])], axis=1)
        for h in heads:
            deps = [waiting] + before_last * (m == last and h == heads[-1])
            if m == 0 and h == 0:
                deps.append(two_passed[1])
            if m == 0 and h == 1:
                back_two(1, (pieces[0][3],))
                deps.append(send_back[1])
            pieces.append(
                mixer_backward(
                    h, proj[m], pre_decay[m], taps_cols, live[m], d_gated, bases[0], packed[m], left_in,
                    lens[m], mesa_bias, deps,
                )
            )
            left_in = pieces[-1][4]
            done = (pieces[-1][3],)
            if m < last:
                keep, beside = ffn_parts[h]
                ffn_passed.append(pass_on(keep, beside, done))
            if (m, h) != (last, heads[-1]):
                (waiting,) = steps.send(done)
        d_heads = [p[0] for p in pieces]
        d_proj = jnp.concatenate(d_heads, axis=1)
        d_decay = jnp.concatenate([p[1][0] for p in pieces], axis=0).astype(BF)
        grad_taps = grad_taps + jnp.concatenate([p[2] for p in pieces], axis=1)
        grad_head = grad_head + jnp.concatenate([p[3] for p in pieces], axis=0)[:, 0]
        d_proj = dot32("kcj,ji->kci", d_proj, place[m]).astype(BF)
        if m == last:
            late = add_steps([left_in], "dp")
            next(late)
            (summed,) = late.send((d_proj,))
            d_proj = gate(d_proj, (summed,))
        grad_in = grad_in + dot32("id,kci->kdc", group_one[m], d_proj)
        if m == last:
            merged = [(grad_in + err_in[0], False), (merged_out, False)]
            (summed,) = late.send((merged[0][0],))
            d_proj = gate(d_proj, (summed,))
        d_decay = dot32("hj,ji->hi", d_decay, place[m]).astype(BF)
        d_one = dot32("kci,kdc->id", d_proj, weights_in) + dot32("hi,dh->id", d_decay, decay_low)
        d_one = d_one.astype(BF).reshape(2, 2, share, width)
        back_parts.append((d_one[:, 0], swap(d_one[:, 1], "tensor", 1)))
        grad_decay = grad_decay + dot32("hi,id->hd", d_decay, group_one[m])
        before_last = [grad_in, d_one]

    gain_grad = jnp.sum(weights_in.astype(F32) * grad_in, axis=(0, 2)) + jnp.sum(
        decay_low.astype(F32).T * grad_decay, axis=0
    )
    gains = jnp.concatenate([gain_grad[None] / gain_one, sum(gains_two)], axis=0)
    (left,), (right,), unused = finish_steps(add_steps([gains.reshape(-1, BLK)], "tensor"))
    gains = (left + right).reshape(gains.shape)
    small = [jnp.transpose(grad_taps, (0, 2, 1)), grad_decay, grad_head, gains]
    flat = jnp.concatenate([s.reshape(-1, BLK) for s in small], axis=0)

    (left,), (right,), unused = finish_steps(late, (d_one,))
    frame_late, own = frames_and_basis(left, right, merged, dp_count, (d_one,))
    try:
        while True:
            steps.send((own,))
    except StopIteration as end:
        frame_early, basis_early, *errors_early = end.value
    back_passed = [pass_on(*back_parts[m], (own,) if m == last else ()) for m in micros]
    (left, flat), (right, flat_moved), unused = finish_steps(add_steps([own, flat], "dp"))
    flat = (flat + flat_moved) / dp_count

    across = [swap(v, "tensor", 2) for v in ffn_passed]
    out_tokens = add_rows(resid, ffn_parts, across, (own,))
    back_across = [swap(v, "tensor", 2) for v in back_passed]
    d_tokens = None
    for m in micros:
        if m == last:
            deps = (back_passed[last], d_tokens, out_tokens)
            basis_late, *errors_late = basis_and_errors(frame_late, left, right, merged, dp_count, deps)
        keep, beside = back_parts[m]
        d_tokens = norm_back_into(
            d_tokens, m, micro_count, d_resid[m], tokens, keep, beside, back_across[m], gain_one
        )
    parts, edge = [], 0
    for s in small:
        parts.append(flat[edge : edge + s.size // BLK].reshape(s.shape))
        edge += s.size // BLK
    grad_conv, grad_decay, grad_bias, gain_total = parts
    grad_decay = jnp.transpose(grad_decay)
    grad_bias = jnp.transpose(grad_bias[:, :2])

    def part(rows_of, count, axis):
        return lax.dynamic_slice_in_dim(rows_of, dp_index * count, count, axis)

    def cut(rows_of, sizes):
        edge, out = 0, []
        for size in sizes:
            out.append(rows_of[:, edge : edge + size])
            edge += size
        return out

    def outer(frame, basis):
        return jnp.einsum("rm,rn->mn", frame, basis, precision=precise)

    hidden_width = w_ff.shape[2]
    columns = w_in.shape[2]
    frames = cut(frame_late, [width] * 4 + [columns]) + cut(frame_early, [width] * 2 + [hidden_width])
    rights = cut(basis_late, [columns] * 4 + [width]) + cut(basis_early, [hidden_width] * 2 + [width])
    basis_in_new = jnp.stack([b.T for b in rights[:4]])
    basis_out_new = rights[4].T[None]
    basis_ff_new = jnp.stack([b.T for b in rights[5:7]])
    basis_down_new = rights[7].T[None]
    err_in_new, err_out_new = errors_late[0][None], errors_late[1]
    err_ff_new, err_down_new = jnp.swapaxes(errors_early[0], 1, 2)[None], errors_early[1]
    owned_in = jnp.stack([outer(part(f, w_in.shape[1], 1), b) for f, b in zip(frames[:4], rights[:4])])
    owned_ff = jnp.stack([outer(part(f, w_ff.shape[1], 1), b) for f, b in zip(frames[5:7], rights[5:7])])
    owned_out = outer(frames[4], part(rights[4], w_out.shape[1], 1))
    owned_down = outer(frames[7], part(rights[7], w_down.shape[1], 1))
    w_in_new, mom_in_new = advance_weight(w_in, mom_in, owned_in, step_rate)
    w_out_new, mom_out_new = advance_weight(w_out, mom_out, owned_out, step_rate)
    w_ff_new, mom_ff_new = advance_weight(w_ff, mom_ff, owned_ff, step_rate)
    w_down_new, mom_down_new = advance_weight(w_down, mom_down, owned_down, step_rate)
    gains_new, mom_gains_new = advance_weight(norm_gains, mom_gains, gain_total, small_rate)
    conv_new, mom_conv_new = advance_weight(conv_taps, mom_conv, grad_conv, small_rate)
    decay_new, mom_decay_new = advance_weight(decay_w, mom_decay, grad_decay, small_rate)
    bias_new, mom_bias_new = advance_weight(mesa_bias, mom_bias, grad_bias, small_rate)
    return (
        out_tokens,
        d_tokens,
        w_in_new,
        mom_in_new,
        err_in_new,
        basis_in_new,
        w_out_new,
        mom_out_new,
        err_out_new,
        basis_out_new,
        w_ff_new,
        mom_ff_new,
        err_ff_new,
        basis_ff_new,
        w_down_new,
        mom_down_new,
        err_down_new,
        basis_down_new,
        gains_new,
        mom_gains_new,
        conv_new,
        mom_conv_new,
        decay_new,
        mom_decay_new,
        bias_new,
        mom_bias_new,
    )


def solution(mesh):
    placed = (
        P(None, ("dp", "tensor"), None),
        P(None, ("dp", "tensor"), None),
        P(None, "dp", None),
        P(None, "dp", None),
        P(None, "dp", None),
        P(None, "dp", "tensor"),
        P("tensor", "dp"),
        P(None, "dp", "tensor"),
        P("tensor", "dp"),
        P(),
        P(None, None, "tensor"),
        P(None, "tensor"),
        P(None, "tensor"),
        P(None, "dp", "tensor"),
        P("tensor", "dp"),
        P(None, "dp", "tensor"),
        P("tensor", "dp"),
        P(),
        P(None, None, "tensor"),
        P(None, "tensor"),
        P(None, "tensor"),
        P("dp", None, None, "tensor"),
        P("dp", "tensor", None),
        P("dp", None, None, "tensor"),
        P("dp", "tensor", None),
        P(None, "tensor", None),
        P("tensor", None, None),
        P(None, "tensor", None),
        P("tensor", None, None),
    )
    return jax.shard_map(
        on_device,
        mesh=mesh,
        in_specs=placed,
        out_specs=(
            P(None, ("dp", "tensor"), None),
            P(None, ("dp", "tensor"), None),
            P(None, "dp", "tensor"),
            P(None, "dp", "tensor"),
            P("dp", None, None, "tensor"),
            P(None, "tensor", None),
            P("tensor", "dp"),
            P("tensor", "dp"),
            P("dp", "tensor", None),
            P("tensor", None, None),
            P(None, "dp", "tensor"),
            P(None, "dp", "tensor"),
            P("dp", None, None, "tensor"),
            P(None, "tensor", None),
            P("tensor", "dp"),
            P("tensor", "dp"),
            P("dp", "tensor", None),
            P("tensor", None, None),
            P(),
            P(),
            P(None, None, "tensor"),
            P(None, None, "tensor"),
            P(None, "tensor"),
            P(None, "tensor"),
            P(None, "tensor"),
            P(None, "tensor"),
        ),
        check_vma=False,
    )
```

```python
import functools
from types import SimpleNamespace

import jax
import jax.numpy as jnp
from jax import lax
from jax.experimental import pallas as pl
from jax.experimental.pallas import tpu as pltpu
from jax.sharding import PartitionSpec as P

CG_STEPS = 8
BLK = 128
tiny_eps = 1e-06
solve_floor = 0.01
ridge_shift = 9.0
precise = lax.Precision.HIGHEST
F32 = jnp.float32
BF = jnp.bfloat16


def softplus(x):
    return jnp.maximum(x, 0.0) + jnp.log1p(jnp.exp(-jnp.abs(x)))


def spot_of(i):
    return pl.ds(i * BLK, BLK)


def sigmoid(x):
    return 0.5 * jnp.tanh(0.5 * x) + 0.5


def mm(a, b):
    return jnp.dot(a, b, preferred_element_type=F32)


def nt(a, b):
    return lax.dot_general(a, b, (((1,), (1,)), ((), ())), preferred_element_type=F32)


def high_low(x, axis=0):
    high = x.astype(BF).astype(F32)
    return jnp.concatenate([high, x - high], axis=axis).astype(BF)


def halves(x):
    count = x.shape[0] // 2
    return x[:count] + x[count:]


def col_sum(x):
    return jnp.sum(x, axis=0, keepdims=True)


def start_of(lens_ref, places):
    begin = jnp.zeros_like(places)
    edge = jnp.int32(0)
    for item in range(lens_ref.shape[0] - 1):
        edge = edge + lens_ref[item]
        begin = jnp.where(places >= edge, edge, begin)
    return begin


def conv_masks(lens_ref, total, taps):
    places = lax.broadcasted_iota(jnp.int32, (1, total), 1)
    begin = start_of(lens_ref, places)
    return [(places - i >= begin).astype(F32) for i in range(taps)]


def conv_rows(rows, taps_now, sc):
    acc = rows * taps_now[:, 0:1]
    for i in range(1, taps_now.shape[1]):
        acc = acc + (pltpu.roll(rows, i, 1) * sc.mask[i]) * taps_now[:, i : i + 1]
    return acc


CHUNK = 16
TOGETHER = 8


def by_chunks(width, fn, init):
    def body(c, carry):
        for k in range(TOGETHER):
            carry = fn(pl.ds(pl.multiple_of((c * TOGETHER + k) * CHUNK, CHUNK), CHUNK), carry)
        return carry

    return lax.fori_loop(0, width // (CHUNK * TOGETHER), body, init)


def set_up(head, proj_ref, prea_ref, taps_ref, live_ref, lens_ref, bias_ref, sc, keep_all):
    width, total = proj_ref.shape[1], proj_ref.shape[2]
    blocks = total // BLK
    taps = taps_ref.shape[2]
    for i, mask in enumerate(conv_masks(lens_ref, total, taps)):
        sc.mask[i] = jnp.broadcast_to(mask, (CHUNK, total))
    live = live_ref[...]

    def squares(j, dst):
        def body(at, acc):
            u = conv_rows(proj_ref[j, at, :], taps_ref[j, at, :], sc)
            sig = sigmoid(u)
            x = u * sig
            dst[at, :] = x
            if keep_all:
                sc.slope[j, at, :] = sig + x * (1.0 - sig)
            return acc + x * x

        acc = by_chunks(width, body, jnp.zeros((CHUNK, total), F32))
        return lax.rsqrt(col_sum(acc) + tiny_eps)

    keys, values = (sc.xk, sc.xv) if keep_all else (sc.x, sc.x)

    scale_q = squares(0, sc.q)
    scale_k = squares(1, keys)
    sc.scale[0:1, :] = scale_q
    sc.scale[1:2, :] = scale_k
    scale_k = scale_k * live
    for n in range(blocks):
        at = pl.ds(n * BLK, BLK)
        sc.q[:, at] = sc.q[:, at] * scale_q[:, n * BLK : (n + 1) * BLK]
        kt = keys[:, at] * scale_k[:, n * BLK : (n + 1) * BLK]
        sc.kt[:, at] = kt.astype(BF)
        sc.ks[n, 0:BLK, :] = kt.T.astype(BF)
    squares(2, values)
    for n in range(blocks):
        at = pl.ds(n * BLK, BLK)
        vt = values[:, at] * live[:, n * BLK : (n + 1) * BLK]
        sc.vt[:, at] = vt.astype(BF)
        if keep_all:
            sc.vg[n, 0:BLK, :] = vt.T.astype(BF)
    base = prea_ref[0, :, :] + jnp.full((1, total), bias_ref[0, head], F32)
    base = jnp.concatenate([base[:, n * BLK : (n + 1) * BLK] for n in range(blocks)], axis=0)
    forget = -softplus(base)
    row_i = lax.broadcasted_iota(jnp.int32, (BLK, BLK), 0)
    col_i = lax.broadcasted_iota(jnp.int32, (BLK, BLK), 1)
    cum = jnp.dot(forget, (row_i <= col_i).astype(F32), precision=precise, preferred_element_type=F32)
    first = lax.broadcasted_iota(jnp.int32, (blocks, BLK), 0) * BLK
    places = first + lax.broadcasted_iota(jnp.int32, (blocks, BLK), 1)
    begin = start_of(lens_ref, places)
    begin_last = start_of(lens_ref, first + (BLK - 1))
    end = jnp.broadcast_to(cum[:, BLK - 1 : BLK], cum.shape)
    from_start = jnp.where(begin < first, jnp.exp(cum), 0.0)
    to_end = jnp.where(places >= begin_last, jnp.exp(end - cum), 0.0)
    keep = jnp.where(begin_last < first, jnp.exp(end), 0.0)
    sc.dec[0] = from_start
    sc.dec[1] = to_end
    sc.dec[2] = keep
    cum_col = jnp.transpose(cum)
    for n in range(blocks):
        spread = cum[n : n + 1, :] - cum_col[:, n : n + 1]
        allowed = (row_i <= col_i) & (row_i + n * BLK >= begin[n : n + 1, :])
        sc.dt[n] = jnp.where(allowed, jnp.exp(jnp.where(allowed, spread, 0.0)), 0.0)
    state = jnp.zeros((2 * width, width), F32)
    for n in range(blocks):
        sc.ks[n, BLK:, :] = state[:width].astype(BF)
        sc.g[n] = state[width:].astype(BF)
        if keep_all:
            sc.vg[n, BLK:, :] = state[width:].T.astype(BF)
        if n + 1 < blocks:
            at = pl.ds(n * BLK, BLK)
            to_row = to_end[n : n + 1, :]
            scaled = jnp.concatenate(
                [sc.kt[:, at].astype(F32) * to_row, sc.vt[:, at].astype(F32) * to_row], axis=0
            ).astype(BF)
            state = keep[n : n + 1, :] * state + mm(scaled, sc.ks[n, 0:BLK, :])
    return softplus(jnp.full((1, BLK), bias_ref[1, head], F32) + ridge_shift)


def solve(lam, sc, keep_all):
    blocks = sc.dt.shape[0]
    spans = [pl.ds(n * BLK, BLK) for n in range(blocks)]
    row = sc.row
    for n, at in enumerate(spans):
        q = sc.q[:, at]
        row[0, n : n + 1, :] = col_sum(q * q)
        sc.z[:, at] = jnp.zeros_like(q)
        sc.p[:, at] = q
        sc.r[:, at] = q
        sc.pl[:, at] = q.astype(BF)

    def step(i, last):
        spot = spot_of(i)
        for n, at in enumerate(spans):
            both = mm(sc.ks[n], sc.pl[:, at])
            scores = (sc.dt[n] * both[:BLK]).astype(BF)
            sc.sl[n] = scores
            sc.w[:, at] = sc.dec[0, n : n + 1, :] * both[BLK:]
            if keep_all:
                far = spot_of(CG_STEPS + i)
                sc.rh[n, :, spot] = scores
                sc.lh[n, :, far] = sc.pl[:, at]
        for n, at in enumerate(spans):
            p = sc.p[:, at]
            w = mm(sc.kt[:, at], sc.sl[n]) + sc.w[:, at] + lam * p
            rho = row[0, n : n + 1, :]
            inv_c = 1.0 / (col_sum(p * w) + solve_floor)
            s = rho * inv_c
            sc.z[:, at] = sc.z[:, at] + s * p
            if keep_all:
                sc.ph[i, :, at] = p
                sc.wh[i, :, at] = w
                sc.fh[n, :, spot] = (sc.dec[0, n : n + 1, :] * p).astype(BF)
                sc.sh[i, 0, n : n + 1, :] = s
                sc.sh[i, 1, n : n + 1, :] = inv_c
            if not last:
                r = sc.r[:, at] - s * w
                sc.r[:, at] = r
                rho_next = col_sum(r * r)
                inv_rho = 1.0 / (rho + solve_floor)
                beta = rho_next * inv_rho
                row[0, n : n + 1, :] = rho_next
                if keep_all:
                    sc.nh[i, :, at] = r
                    sc.sh[i, 2, n : n + 1, :] = inv_rho
                    sc.sh[i, 3, n : n + 1, :] = beta
                p = r + beta * p
                sc.p[:, at] = p
                sc.pl[:, at] = p.astype(BF)

    for i in range(CG_STEPS):
        step(i, i == CG_STEPS - 1)


def forward_kernel(names, head, proj_ref, prea_ref, taps_ref, live_ref, lens_ref, bias_ref, out_ref, *scratch):
    sc = SimpleNamespace(**dict(zip(names, scratch)))
    lam = set_up(head, proj_ref, prea_ref, taps_ref, live_ref, lens_ref, bias_ref, sc, False)
    solve(lam, sc, False)
    spans = [pl.ds(n * BLK, BLK) for n in range(sc.dt.shape[0])]
    for n, at in enumerate(spans):
        z = sc.z[:, at].astype(BF)
        sc.sl[n] = (sc.dt[n] * mm(sc.ks[n, 0:BLK, :], z)).astype(BF)
        sc.w[:, at] = sc.dec[0, n : n + 1, :] * mm(sc.g[n], z)
    for n, at in enumerate(spans):
        o = mm(sc.vt[:, at], sc.sl[n]) + sc.w[:, at]
        out_ref[:, at] = (o * sigmoid(proj_ref[3, :, at])).astype(BF)


def backward_kernel(
    names, head, proj_ref, prea_ref, taps_ref, live_ref, dg_ref, basis_ref, packed_ref, left_ref, lens_ref, bias_ref,
    dproj_ref, da_ref, dtaps_ref, dhead_ref, sketch_ref, *scratch
):
    sc = SimpleNamespace(**dict(zip(names, scratch)))
    width, total = proj_ref.shape[1], proj_ref.shape[2]
    blocks = total // BLK
    lam = set_up(head, proj_ref, prea_ref, taps_ref, live_ref, lens_ref, bias_ref, sc, True)
    solve(lam, sc, True)
    row_i = lax.broadcasted_iota(jnp.int32, (BLK, BLK), 0)
    col_i = lax.broadcasted_iota(jnp.int32, (BLK, BLK), 1)
    dkt, dvt, zb, rb_s, pb_s = sc.dkt, sc.dvt, sc.zb, sc.rb, sc.pb

    spans = [pl.ds(n * BLK, BLK) for n in range(blocks)]
    row = sc.row
    last = CG_STEPS - 1

    for n, at in enumerate(spans):
        z_low = sc.z[:, at].astype(BF)
        sc.pl[:, at] = z_low
        sc.sl[n] = (sc.dt[n] * mm(sc.ks[n, 0:BLK, :], z_low)).astype(BF)
        sc.w[:, at] = sc.dec[0, n : n + 1, :] * mm(sc.g[n], z_low)
    for n, at in enumerate(spans):
        o = mm(sc.vt[:, at], sc.sl[n]) + sc.w[:, at]
        sig = sigmoid(proj_ref[3, :, at])
        dg = dg_ref[:, at]
        dproj_ref[3, :, at] = (dg * o * sig * (1.0 - sig)).astype(BF)
        sc.do[:, at] = (dg * sig).astype(BF)
    for n, at in enumerate(spans):
        from_row = sc.dec[0, n : n + 1, :]
        z = sc.z[:, at]
        both = mm(sc.vg[n], sc.do[:, at])
        state_part = from_row * both[BLK:]
        zb[:, at] = state_part
        sc.sl2[n] = (sc.dt[n] * both[:BLK]).astype(BF)
        sc.xm[n] = sc.sl[n].astype(F32) * both[:BLK]
        sc.fm[0, n : n + 1, :] = col_sum(z * state_part)
        sc.p[:, at] = from_row * z
    for n, at in enumerate(spans):
        do = sc.do[:, at]
        zb[:, at] = zb[:, at] + mm(sc.kt[:, at], sc.sl2[n])
        dvt[:, at] = nt(do, sc.sl[n])
        sc.dg0[n] = nt(do, sc.p[:, at].astype(BF))
        dkt[:, at] = nt(sc.pl[:, at], sc.sl2[n])
    for at in spans:
        zero = jnp.zeros((width, BLK), F32)
        rb_s[:, at] = zero
        pb_s[:, at] = zero
        sc.nh[last, :, at] = zero
    sc.sh[last, 2] = jnp.zeros((blocks, BLK), F32)
    sc.sh[last, 3] = jnp.zeros((blocks, BLK), F32)
    row[0] = jnp.zeros((blocks, BLK), F32)
    sc.fm[1] = jnp.zeros((blocks, BLK), F32)

    def reverse_step(i):
        spot = spot_of(i)
        far = spot_of(CG_STEPS + i)
        s_all, inv_c, inv_rho, beta = sc.sh[i, 0], sc.sh[i, 1], sc.sh[i, 2], sc.sh[i, 3]
        for n, at in enumerate(spans):
            row[1, n : n + 1, :] = col_sum(pb_s[:, at] * sc.ph[i, :, at])
        beta_bar = row[1]
        row[2] = 2.0 * (row[0] + beta_bar * inv_rho)
        for n, at in enumerate(spans):
            rb = rb_s[:, at] + pb_s[:, at] + row[2, n : n + 1, :] * sc.nh[i, :, at]
            rb_s[:, at] = rb
            row[3, n : n + 1, :] = col_sum(zb[:, at] * sc.ph[i, :, at] - rb * sc.wh[i, :, at])
        sbar = row[3]
        row[4] = -sbar * s_all * inv_c
        row[0] = sbar * inv_c - beta_bar * beta * inv_rho
        for n, at in enumerate(spans):
            p = sc.ph[i, :, at]
            cbar = row[4, n : n + 1, :]
            s = sc.sh[i, 0, n : n + 1, :]
            wb = cbar * p - s * rb_s[:, at]
            low = wb.astype(BF)
            sc.pl[:, at] = low
            sc.lh[n, :, spot] = low
            sc.fm[1, n : n + 1, :] += col_sum(wb * p)
            pb_s[:, at] = (
                sc.sh[i, 3, n : n + 1, :] * pb_s[:, at]
                + s * zb[:, at]
                + cbar * sc.wh[i, :, at]
                + lam * wb
            )
        for n, at in enumerate(spans):
            both = mm(sc.ks[n], sc.pl[:, at])
            scores = (sc.dt[n] * both[:BLK]).astype(BF)
            sc.sl[n] = scores
            sc.rh[n, :, far] = scores
            sc.xm[n] += sc.rh[n, :, spot].astype(F32) * both[:BLK]
            state_part = sc.dec[0, n : n + 1, :] * both[BLK:]
            pb_s[:, at] = pb_s[:, at] + state_part
            sc.fm[0, n : n + 1, :] += col_sum(sc.ph[i, :, at] * state_part)
        for n, at in enumerate(spans):
            pb_s[:, at] = pb_s[:, at] + mm(sc.kt[:, at], sc.sl[n])

    for i in reversed(range(CG_STEPS)):
        reverse_step(i)
    half = CG_STEPS * BLK
    for n, at in enumerate(spans):
        dkt[:, at] += nt(sc.lh[n], sc.rh[n])
        sc.ds0[n] = nt(sc.lh[n, :, 0:half], sc.fh[n])

    d_sym = jnp.zeros((width, width), F32)
    d_g = jnp.zeros((width, width), F32)
    g_rows = [None] * blocks
    f_rows = [None] * blocks
    x_rows = [None] * blocks
    keep_rows = [None] * blocks
    lower = (row_i >= col_i).astype(BF)
    before = row_i < col_i
    for n in reversed(range(blocks)):
        at = pl.ds(n * BLK, BLK)
        kt = sc.kt[:, at]
        to_row = sc.dec[1, n : n + 1, :]
        keep = sc.dec[2, n : n + 1, :]
        if n + 1 < blocks:
            vt = sc.vt[:, at]
            g_low = d_g.astype(BF)
            part_s = to_row * mm(d_sym.astype(BF), kt)
            part_v = to_row * mm(g_low, kt)
            part_k = to_row * mm(d_g.T.astype(BF), vt)
            dkt[:, at] += part_s + part_k
            dvt[:, at] += part_v
            g_rows[n] = col_sum(0.5 * kt.astype(F32) * part_s + vt.astype(F32) * part_v)
            inner = 0.5 * d_sym * sc.ks[n, BLK:, :].astype(F32) + d_g * sc.g[n].astype(F32)
            keep_rows[n] = keep * jnp.sum(col_sum(inner), axis=1, keepdims=True)
        else:
            g_rows[n] = jnp.zeros((1, BLK), F32)
            keep_rows[n] = jnp.zeros((1, BLK), F32)
        ds0 = sc.ds0[n]
        d_sym = keep * d_sym + ds0 + ds0.T
        d_g = keep * d_g + sc.dg0[n]
        x = sc.xm[n]
        high = x.astype(BF)
        low = (x - high.astype(F32)).astype(BF)
        summed = mm(high, lower) + mm(low, lower)
        x_rows[n] = col_sum(jnp.where(before, summed, 0.0))
        f_rows[n] = sc.fm[0, n : n + 1, :]
    f_all = jnp.concatenate(f_rows, axis=0)
    g_all = jnp.concatenate(g_rows, axis=0)
    da = (
        jnp.dot(f_all, (row_i >= col_i).astype(F32), precision=precise, preferred_element_type=F32)
        + jnp.dot(g_all, before.astype(F32), precision=precise, preferred_element_type=F32)
        + jnp.concatenate(x_rows, axis=0)
        + jnp.concatenate(keep_rows, axis=0)
    )
    da = jnp.concatenate([da[n : n + 1, :] for n in range(blocks)], axis=1)
    base = prea_ref[0, :, :] + jnp.full((1, total), bias_ref[0, head], F32)
    da = -sigmoid(base) * da
    da_ref[0, :, :] = da
    d_bias = jnp.sum(da, axis=1, keepdims=True)
    d_lam = jnp.sum(col_sum(sc.fm[1]), axis=1, keepdims=True)
    d_lam = d_lam * sigmoid(jnp.full((1, BLK), bias_ref[1, head], F32) + ridge_shift)
    lane = lax.broadcasted_iota(jnp.int32, (1, BLK), 1)
    dhead_ref[0, :, :] = jnp.where(lane == 0, d_bias, d_lam)

    taps = taps_ref.shape[2]
    live = live_ref[...]
    scale_k = sc.scale[1:2, :]
    rho_bar = jnp.concatenate([row[0, n : n + 1, :] for n in range(blocks)], axis=1)
    sc.wide[0] = jnp.broadcast_to(2.0 * rho_bar, (CHUNK, total))
    sc.wide[1] = jnp.broadcast_to(sc.scale[0:1, :], (CHUNK, total))
    sc.wide[2] = jnp.broadcast_to(live, (CHUNK, total))
    sc.wide[3] = jnp.broadcast_to(scale_k, (CHUNK, total))

    def query_grad(at, acc):
        q = sc.q[at, :]
        grad = rb_s[at, :] + pb_s[at, :] + sc.wide[0] * q
        pb_s[at, :] = grad
        return acc + q * grad

    def key_grad(at, acc):
        grad = dkt[at, :] * sc.wide[2]
        dkt[at, :] = grad
        return acc + (sc.xk[at, :] * sc.wide[3]) * grad

    zero = jnp.zeros((CHUNK, total), F32)
    mean_q = col_sum(by_chunks(width, query_grad, zero))
    mean_k = col_sum(by_chunks(width, key_grad, zero))
    sc.wide[0] = jnp.broadcast_to(mean_q, (CHUNK, total))
    sc.wide[4] = jnp.broadcast_to(mean_k, (CHUNK, total))

    def through(j, at, du):
        taps_now = taps_ref[j, at, :]
        rows = proj_ref[j, at, :]
        d_rows = du * taps_now[:, 0:1]
        sums = [jnp.sum(rows * du, axis=1, keepdims=True)]
        for i in range(1, taps):
            moved = pltpu.roll(du * sc.mask[i], total - i, 1)
            d_rows = d_rows + moved * taps_now[:, i : i + 1]
            sums.append(jnp.sum(rows * moved, axis=1, keepdims=True))
        dproj_ref[j, at, :] = d_rows.astype(BF)
        dtaps_ref[j, at, :] = jnp.concatenate(sums, axis=1)

    def query_rows(at, carry):
        grad = sc.wide[1] * (pb_s[at, :] - sc.q[at, :] * sc.wide[0])
        through(0, at, grad * sc.slope[0, at, :])
        return carry

    def key_rows(at, carry):
        scale = sc.wide[3]
        grad = scale * (dkt[at, :] - (sc.xk[at, :] * scale) * sc.wide[4])
        through(1, at, grad * sc.slope[1, at, :])
        return carry

    def value_rows(at, carry):
        through(2, at, (dvt[at, :] * sc.wide[2]) * sc.slope[2, at, :])
        return carry

    for fn in (query_rows, key_rows, value_rows):
        by_chunks(width, fn, 0)

    slots, rank = basis_ref.shape[0], basis_ref.shape[1]
    inner = jnp.concatenate(
        [high_low(halves(mm(high_low(basis_ref[j]), dproj_ref[j]))) for j in range(slots)], axis=0
    )
    both = mm(inner, packed_ref[...])
    deep = packed_ref.shape[1]
    for j in range(slots):
        at = slice(j * deep, (j + 1) * deep)
        sketch_ref[:, at] = left_ref[:, at] + halves(both[2 * rank * j : 2 * rank * (j + 1)])
    if left_ref.shape[1] > slots * deep:
        sketch_ref[:, slots * deep :] = left_ref[:, slots * deep :]


def scratch_of(width, total, backward):
    blocks = total // BLK
    flat = ((width, total), F32)
    flat_low = ((width, total), BF)
    square = ((blocks, BLK, BLK), F32)
    square_low = ((blocks, BLK, BLK), BF)
    own = dict(
        q=flat,
        mask=((4, CHUNK, total), F32),
        kt=flat_low,
        vt=flat_low,
        ks=((blocks, 2 * BLK, width), BF),
        g=square_low,
        dt=square,
        dec=((3, blocks, BLK), F32),
        scale=((8, total), F32),
        row=((5, blocks, BLK), F32),
        z=flat,
        p=flat,
        r=flat,
        w=flat,
        pl=flat_low,
        sl=square_low,
    )
    if backward:
        history = ((CG_STEPS, width, total), F32)
        own.update(
            xk=flat,
            xv=flat,
            slope=((3, width, total), F32),
            wide=((5, CHUNK, total), F32),
            vg=((blocks, 2 * BLK, width), BF),
            ph=history,
            wh=history,
            nh=history,
            lh=((blocks, width, 2 * CG_STEPS * BLK), BF),
            rh=((blocks, BLK, 2 * CG_STEPS * BLK), BF),
            fh=((blocks, width, CG_STEPS * BLK), BF),
            sh=((CG_STEPS, 4, blocks, BLK), F32),
            do=flat_low,
            sl2=square_low,
            dkt=flat,
            dvt=flat,
            zb=flat,
            rb=flat,
            pb=flat,
            dg0=square,
            ds0=square,
            xm=square,
            fm=((2, blocks, BLK), F32),
        )
    else:
        own.update(x=flat)
    return list(own), [pltpu.VMEM(shape, kind) for shape, kind in own.values()]


def mixer_call(kernel, backward, head, arrays, lens, bias, deps, cost):
    proj, pre_a, taps, live = arrays[:4]
    slots, columns, total = proj.shape
    heads = pre_a.shape[0]
    width = columns // heads
    names, scratch = scratch_of(width, total, backward)
    smem = pl.BlockSpec(memory_space=pltpu.SMEM)
    kinds, count = taps.shape[0], taps.shape[2]
    in_specs = [
        pl.BlockSpec((slots, width, total), lambda g: (0, head, 0)),
        pl.BlockSpec((1, 1, total), lambda g: (head, 0, 0)),
        pl.BlockSpec((kinds, width, count), lambda g: (0, head, 0)),
        pl.BlockSpec((1, total), lambda g: (0, 0)),
    ]
    if backward:
        basis, packed, left = arrays[5:]
        in_specs += [
            pl.BlockSpec((width, total), lambda g: (head, 0)),
            pl.BlockSpec((slots, basis.shape[1], width), lambda g: (0, 0, head)),
            pl.BlockSpec(packed.shape, lambda g: (0, 0)),
            pl.BlockSpec(left.shape, lambda g: (0, 0)),
        ]
        out_specs = (
            pl.BlockSpec((slots, width, total), lambda g: (0, 0, 0)),
            pl.BlockSpec((1, 1, total), lambda g: (0, 0, 0)),
            pl.BlockSpec((kinds, width, count), lambda g: (0, 0, 0)),
            pl.BlockSpec((1, 1, BLK), lambda g: (0, 0, 0)),
            pl.BlockSpec(left.shape, lambda g: (0, 0)),
        )
        out_shape = (
            jax.ShapeDtypeStruct((slots, width, total), BF),
            jax.ShapeDtypeStruct((1, 1, total), F32),
            jax.ShapeDtypeStruct((kinds, width, count), F32),
            jax.ShapeDtypeStruct((1, 1, BLK), F32),
            jax.ShapeDtypeStruct(left.shape, F32),
        )
    else:
        out_specs = pl.BlockSpec((width, total), lambda g: (0, 0))
        out_shape = jax.ShapeDtypeStruct((width, total), BF)
    in_specs += [smem, smem] + [pl.BlockSpec(memory_space=pl.ANY)] * len(deps)
    own = len(arrays) + 2

    def body(*refs):
        kernel(names, head, *refs[:own], *refs[own + len(deps) :])

    return pl.pallas_call(
        body,
        grid=(1,),
        in_specs=in_specs,
        out_specs=out_specs,
        out_shape=out_shape,
        scratch_shapes=scratch,
        compiler_params=pltpu.CompilerParams(vmem_limit_bytes=56 * 2**20),
        cost_estimate=pl.CostEstimate(flops=cost * 10**9, bytes_accessed=cost * 3 * 10**6, transcendentals=0),
        name="mixer_backward" if backward else "mixer_forward",
    )(*arrays, lens, bias, *deps)


def mixer_forward(head, proj, pre_a, taps, live, lens, bias, deps=()):
    return mixer_call(forward_kernel, False, head, (proj, pre_a, taps, live), lens, bias, deps, 11)


def mixer_backward(head, proj, pre_a, taps, live, d_gated, basis, packed, left, lens, bias, deps=()):
    arrays = (proj, pre_a, taps, live, d_gated, basis, packed, left)
    return mixer_call(backward_kernel, True, head, arrays, lens, bias, deps, 28)


def any_specs(deps):
    return [pl.BlockSpec(memory_space=pl.ANY)] * len(deps)


def row_of(pair, k):
    return pair, pl.BlockSpec((pl.squeezed,) + pair.shape[1:], lambda g: (k, 0, 0))


def call(body, name, inputs, outs, deps=(), cost=1):
    whole = pl.BlockSpec(memory_space=pltpu.VMEM)
    count = len(inputs)

    def kernel(*refs):
        body(*refs[:count], *refs[count + len(deps) :])

    kinds = [i[1] if isinstance(i, tuple) else whole for i in inputs]
    inputs = [i[0] if isinstance(i, tuple) else i for i in inputs]
    return pl.pallas_call(
        kernel,
        grid=(1,),
        in_specs=kinds + any_specs(deps),
        out_specs=[whole] * len(outs),
        out_shape=[jax.ShapeDtypeStruct(*o) for o in outs],
        compiler_params=pltpu.CompilerParams(vmem_limit_bytes=56 * 2**20),
        cost_estimate=pl.CostEstimate(flops=cost * 10**9, bytes_accessed=cost * 3 * 10**6, transcendentals=0),
        name=name,
    )(*inputs, *deps)


def pass_on(keep, received, deps=()):
    def body(keep_ref, got_ref, out_ref):
        out_ref[...] = (keep_ref[...].astype(F32) + got_ref[...].astype(F32)).astype(BF)

    return call(body, "pass_on", [row_of(keep, 1), row_of(received, 1)], [(keep.shape[1:], BF)], deps)[0]


def second_norm(tokens, keep, beside, across, gain, deps=()):
    def body(x_ref, keep_ref, beside_ref, across_ref, gain_ref, resid_ref, normed_ref):
        x = x_ref[...].astype(F32)
        x = x + (keep_ref[...].astype(F32) + beside_ref[...].astype(F32) + across_ref[...].astype(F32))
        resid_ref[...] = x
        scale = lax.rsqrt(jnp.mean(x * x, axis=1, keepdims=True) + tiny_eps)
        normed_ref[...] = (x * scale * gain_ref[...]).astype(BF)

    return call(
        body, "second_norm", [tokens, row_of(keep, 0), row_of(beside, 0), across, gain],
        [(tokens.shape, F32), (tokens.shape, BF)], deps,
    )


def pulled_back(x, keep, beside, across, gain):
    grad = keep.astype(F32) + beside.astype(F32) + across.astype(F32)
    x = x.astype(F32)
    scale = lax.rsqrt(jnp.mean(x * x, axis=1, keepdims=True) + tiny_eps)
    unit = x * scale
    scaled = grad * gain
    return scale * (scaled - unit * jnp.mean(unit * scaled, axis=1, keepdims=True)), grad, unit


def norm_back(base, x, keep, beside, across, gain, deps=()):
    def body(base_ref, x_ref, keep_ref, beside_ref, across_ref, gain_ref, out_ref, low_ref, gain_out_ref):
        back, grad, unit = pulled_back(x_ref[...], keep_ref[...], beside_ref[...], across_ref[...], gain_ref[...])
        out = base_ref[...] + back
        out_ref[...] = out
        low_ref[...] = out.astype(BF)
        gain_out_ref[...] = col_sum(grad * unit)

    return call(
        body, "norm_back", [base, x, row_of(keep, 0), row_of(beside, 0), across, gain],
        [(x.shape, F32), (x.shape, BF), (gain.shape, F32)], deps,
    )


def norm_back_into(target, m, count, base, x, keep, beside, across, gain):
    share, width = base.shape

    def body(base_ref, x_ref, keep_ref, beside_ref, across_ref, gain_ref, *refs):
        back, grad, unit = pulled_back(x_ref[...], keep_ref[...], beside_ref[...], across_ref[...], gain_ref[...])
        refs[-1][...] = base_ref[...] + back

    inputs = [base, row_of(x, m), row_of(keep, 0), row_of(beside, 0), across, gain]
    whole = pl.BlockSpec(memory_space=pltpu.VMEM)
    old = [] if target is None else [target]
    return pl.pallas_call(
        body,
        grid=(1,),
        in_specs=[i[1] if isinstance(i, tuple) else whole for i in inputs] + any_specs(old),
        out_specs=pl.BlockSpec((pl.squeezed, share, width), lambda g: (m, 0, 0)),
        out_shape=jax.ShapeDtypeStruct((count, share, width), F32),
        input_output_aliases={len(inputs): 0} if old else {},
        name="norm_back_into",
    )(*[i[0] if isinstance(i, tuple) else i for i in inputs], *old)


def add_rows(resid, parts, across, deps=()):
    count = len(resid)
    shape = (count,) + resid[0].shape

    def body(*refs):
        out_ref = refs[-1]
        for m in range(count):
            x, keep, beside, far = (r[...] for r in refs[4 * m : 4 * m + 4])
            out_ref[m] = (x + (keep.astype(F32) + beside.astype(F32) + far.astype(F32))).astype(BF)

    inputs = []
    for x, (keep, beside), far in zip(resid, parts, across):
        inputs += [x, row_of(keep, 0), row_of(beside, 0), far]
    return call(body, "add_rows", inputs, [(shape, BF)], deps)[0]


def ffn_pass(rows, grads, w_ff, basis_ff, basis_down, deps=()):
    share, width = rows[0].shape
    total = 4 * share
    hidden_width = w_ff.shape[2]
    rank = basis_ff.shape[1]
    tile = 2 * share

    def body(*refs):
        row_refs, grad_refs = refs[:4], refs[4:8]
        ff_ref, bff_ref, bdown_ref = refs[8:11]
        hidden_ref, dgu_ref, two_keep, two_send, ffn_keep, ffn_send, left_ff, left_down, x_s, dy_s = refs[11:]
        for k in range(4):
            x_s[k * share : (k + 1) * share, :] = row_refs[k][...]
            dy_s[k * share : (k + 1) * share, :] = grad_refs[k][...]
        left_ff[...] = jnp.zeros_like(left_ff)
        left_down[...] = jnp.zeros_like(left_down)

        def step(i):
            at = slice(i * tile, (i + 1) * tile)
            x, dy = x_s[at, :], dy_s[at, :]
            gate = mm(x, ff_ref[0])
            up = mm(x, ff_ref[1])
            sig = sigmoid(gate)
            act = gate * sig
            hidden = (act * up).astype(BF)
            d_hidden = mm(dy, ff_ref[2])
            d_gate = (d_hidden * up * sig * (1.0 + gate * (1.0 - sig))).astype(BF)
            d_up = (d_hidden * act).astype(BF)
            hidden_ref[at, :] = hidden
            dgu_ref[0, at, :] = d_gate
            dgu_ref[1, at, :] = d_up
            two = (nt(d_gate, ff_ref[0]) + nt(d_up, ff_ref[1])).astype(BF)
            two_keep[i] = two[:share]
            two_send[i] = two[share:]
            ffn = nt(hidden, ff_ref[2]).astype(BF)
            ffn_keep[i] = ffn[:share]
            ffn_send[i] = ffn[share:]
            for j, d in enumerate((d_gate, d_up)):
                inner = halves(nt(high_low(bff_ref[j]), d))
                left_ff[j] += halves(mm(high_low(inner), x))
            inner = halves(nt(high_low(bdown_ref[...]), dy))
            left_down[...] += halves(mm(high_low(inner), hidden))

        for i in range(2):
            step(i)

    pair = ((2, share, width), BF)
    return call(
        body, "ffn_pass", [*rows, *grads, w_ff, basis_ff, basis_down],
        [
            ((total, hidden_width), BF), ((2, total, hidden_width), BF), pair, pair, pair, pair,
            ((2, rank, width), F32), ((rank, hidden_width), F32), ((total, width), BF), ((total, width), BF),
        ],
        deps, cost=12,
    )


momentum_decay = 0.5
step_rate = 1.0
small_rate = 0.05


def add_steps(values, axis):
    flip, count = 1, lax.axis_size(axis)
    moved, deps = [jnp.zeros_like(v) for v in values], ()
    while flip < count:
        moved = [swap(v, axis, flip) for v in values]
        deps = yield values
        flip *= 2
        if flip < count:
            values = add_after(values, moved, deps)
    return values, moved, deps


def add_after(left, right, deps=()):
    count = len(left)

    def body(*refs):
        for k in range(count):
            refs[2 * count + k][...] = refs[k][...] + refs[count + k][...]

    return call(body, "add_after", [*left, *right], [(v.shape, v.dtype) for v in left], deps)


def finish_steps(steps, deps=None):
    try:
        if deps is None:
            next(steps)
        while True:
            steps.send(deps or ())
    except StopIteration as end:
        return end.value


def gate(value, deps):
    return pl.pallas_call(
        lambda *refs: None,
        in_specs=any_specs((value, *deps)),
        out_specs=pl.BlockSpec(memory_space=pl.ANY),
        out_shape=jax.ShapeDtypeStruct(value.shape, value.dtype),
        input_output_aliases={0: 0},
        name="gate",
    )(value, *deps)


def each_block(groups):
    out = []
    for k, (array, flipped) in enumerate(groups):
        count, m, n = array.shape
        m, n = (n, m) if flipped else (m, n)
        out += [(k, j, flipped, m, n) for j in range(count)]
    return out


def frames_and_basis(left, right, groups, count, deps=()):
    rank = left.shape[0]
    blocks = each_block(groups)

    def body(left_ref, right_ref, *refs):
        frame_ref, right_out = refs[len(groups) :]
        edge, edge_n = 0, 0
        for k, j, flipped, m, n in blocks:
            sketch = (left_ref[:, edge : edge + m] + right_ref[:, edge : edge + m]) * (1.0 / count)
            done = []
            for r in range(rank):
                column = sketch[0:1]
                column = column * lax.rsqrt(jnp.sum(column * column, axis=1, keepdims=True) + tiny_eps)
                done.append(column)
                if r + 1 < rank:
                    sketch = sketch[1:]
                    sketch = sketch - jnp.sum(column * sketch, axis=1, keepdims=True) * column
            frame = jnp.concatenate(done, axis=0)
            frame_ref[:, edge : edge + m] = frame
            right_out[:, edge_n : edge_n + n] = times_block(frame, refs[k][j], flipped)
            edge, edge_n = edge + m, edge_n + n

    return call(
        body, "frames_and_basis", [left, right] + [a for a, f in groups],
        [(left.shape, F32), ((rank, sum(b[4] for b in blocks)), F32)], deps,
    )


def times_block(few, block, transposed):
    both = high_low(few)
    high = block.astype(BF)
    low = (block - high.astype(F32)).astype(BF)
    by = nt if transposed else mm
    return halves(by(both, high)) + by(both, low)[: few.shape[0]]


def outer_terms(frame, basis, flipped):
    high_f, high_b = frame.astype(BF).astype(F32), basis.astype(BF).astype(F32)
    f = jnp.concatenate([high_f, frame - high_f, high_f, jnp.zeros_like(frame)], axis=0)
    b = jnp.concatenate([high_b, high_b, basis - high_b, jnp.zeros_like(basis)], axis=0)
    if flipped:
        f, b = b, f
    return f.T.astype(BF), b.astype(BF)


def basis_and_errors(frame, left, right, groups, count, update, deps=()):
    blocks = each_block(groups)
    total = len(groups)

    def body(frame_ref, left_ref, right_ref, part_ref, weight_ref, moment_ref, *refs):
        basis_ref, weight_out, moment_out = refs[total : total + 3]
        out_refs = refs[total + 3 :]
        edge, edge_n = 0, 0
        for k, j, flipped, m, n in blocks:
            basis = (left_ref[:, edge_n : edge_n + n] + right_ref[:, edge_n : edge_n + n]) * (1.0 / count)
            basis_ref[:, edge_n : edge_n + n] = basis
            f, b = outer_terms(frame_ref[:, edge : edge + m], basis, flipped)
            out_refs[k][j] = refs[k][j] - mm(f, b)
            if k == 0:
                f, b = outer_terms(part_ref[j], basis, flipped)
                moment = momentum_decay * moment_ref[j] + mm(f, b)
                moment_out[j] = moment
                weight_out[j] = weight_ref[j] - step_rate * moment
            edge, edge_n = edge + m, edge_n + n

    arrays = [a for a, f in groups]
    shapes = [(a.shape, F32) for a in (left, update[1], update[2], *arrays)]
    return call(body, "basis_and_errors", [frame, left, right, *update, *arrays], shapes, deps)


def sketches(groups, bases, deps=()):
    rank = bases[0].shape[1]
    blocks = each_block(groups)

    def body(*refs):
        edge = 0
        for k, j, flipped, m, n in blocks:
            refs[-1][:, edge : edge + m] = times_block(refs[len(groups) + k][j], refs[k][j], not flipped)
            edge += m

    return call(
        body, "sketches", [a for a, f in groups] + bases, [((rank, sum(b[3] for b in blocks)), F32)], deps
    )[0]


def swap(value, axis, flip):
    count = lax.axis_size(axis)
    return lax.ppermute(value, axis, [(i, i ^ flip) for i in range(count)])


def gather_rows(own):
    beside = swap(own, "tensor", 1)
    across = swap(own, "tensor", 2)
    return [own, beside, across, swap(across, "tensor", 1)]


def advance_weight(weight, moment, grad_now, rate):
    moment_new = momentum_decay * moment + grad_now
    return (weight - rate * moment_new, moment_new)


def dot32(spec, a, b):
    return jnp.einsum(spec, a, b, preferred_element_type=jnp.float32)


def on_device(
    tokens,
    cotangent,
    slot_order,
    lengths,
    live_mask,
    w_in,
    w_out,
    w_ff,
    w_down,
    norm_gains,
    conv_taps,
    decay_w,
    mesa_bias,
    mom_in,
    mom_out,
    mom_ff,
    mom_down,
    mom_gains,
    mom_conv,
    mom_decay,
    mom_bias,
    err_in,
    err_out,
    err_ff,
    err_down,
    basis_in,
    basis_out,
    basis_ff,
    basis_down,
):
    dp_count = lax.axis_size("dp")
    dp_index = lax.axis_index("dp")
    mine = lax.axis_index("tensor")
    shard_count = lax.axis_size("tensor")
    micro_count, share, width = tokens.shape
    total = share * shard_count
    decay_low = decay_w.astype(BF)
    first = jnp.concatenate([w_in.astype(BF), jnp.transpose(w_out.astype(BF))[None]], axis=0)
    second = jnp.concatenate([w_ff.astype(BF), jnp.transpose(w_down.astype(BF))[None]], axis=0)
    weights_first = lax.all_gather(first, "dp", axis=1, tiled=True)
    weights_in = weights_first[:4]
    weights_out = weights_first[4]
    weights_ff = lax.all_gather(second, "dp", axis=1, tiled=True)
    taps_cols = jnp.transpose(conv_taps, (0, 2, 1))
    gain_one, gain_two = norm_gains[0:1], norm_gains[1:2]
    bases = [jnp.swapaxes(b, 1, 2) for b in (basis_in, basis_out, basis_ff, basis_down)]
    micros = range(micro_count)
    heads = range(mesa_bias.shape[1])
    last = micro_count - 1
    pieces_one, group_one, pieces_dy, place, live, lens = [], [], [], [], [], []
    for m in micros:
        row = tokens[m].astype(F32)
        scale = lax.rsqrt(jnp.mean(row * row, axis=1, keepdims=True) + tiny_eps)
        pieces_one.append(gather_rows((row * scale * gain_one).astype(BF)))
        group_one.append(jnp.concatenate(pieces_one[m], axis=0))
        order_now = slot_order[m, 0]
        near = jnp.bitwise_xor(order_now // share, mine) * share + order_now % share
        slots = lax.broadcasted_iota(jnp.int32, (total, total), 1)
        place.append((near[:, None] == slots).astype(BF))
        live.append(live_mask[m].astype(F32))
        lens.append(lengths[m, 0])

    packed, proj, pre_decay, gated_u = [], [], [], []
    resid, group_two, passed_mix, send_two, keep_mix, beside_mix = [], [], [], [], [], []

    def project(m):
        proj.append(dot32("jdc,td->jct", weights_in, packed[m]))
        pre_decay.append(dot32("dh,td->ht", decay_low, packed[m])[:, None, :])

    def forward(m, h, deps):
        return mixer_forward(h, proj[m], pre_decay[m], taps_cols, live[m], lens[m], mesa_bias, deps)

    def mix_out(m, gated):
        gated_u.append(dot32("cj,ji->ci", jnp.concatenate(gated, axis=0), place[m]).astype(BF))
        terms = dot32("ci,dc->id", gated_u[m], weights_out).astype(BF).reshape(2, 2, share, width)
        keep_mix.append(terms[:, 0])
        send = terms[:, 1]
        beside_mix.append(swap(send, "tensor", 1))
        return send

    def pass_mix(m, deps):
        passed_mix.append(pass_on(keep_mix[m], beside_mix[m], deps))

    def norm_two(m, deps):
        across = swap(passed_mix[m], "tensor", 2)
        own, low = second_norm(tokens[m], keep_mix[m], beside_mix[m], across, gain_two, deps)
        resid.append(own)
        send_two.append(low)
        group_two.append(gather_rows(low))

    err_ff_t = jnp.swapaxes(err_ff[0], 1, 2)
    err_left = sketches([(err_ff_t, True), (err_down, False)], [bases[2], bases[3]])
    left_in = sketches([(err_in[0], False)], [bases[0]])
    for m in micros:
        packed.append(dot32("ji,id->jd", place[m], group_one[m]).astype(BF))
        pieces_dy.append(gather_rows(gate(cotangent[m].astype(BF), (pieces_one[last][2],))))
    project(0)
    gated = [forward(0, h, (err_left, left_in, packed[last])) for h in heads]
    sent = mix_out(0, gated)
    project(1)
    pass_mix(0, (proj[1],))
    gated = [forward(1, 0, (passed_mix[0],))]
    norm_two(0, (gated[0],))
    gated.append(forward(1, 1, (send_two[0],)))
    sent = mix_out(1, gated)

    hidden, d_gate_up, two_keep, two_beside, two_passed, ffn_parts, left_ff, left_down = [[] for i in range(8)]
    rows_of_two, rows_of_dy = [], []

    def feed_forward(m, deps):
        h, dgu, keep, send, ffn_keep, ffn_send, lf, ld, rows_two, rows_dy = ffn_pass(
            group_two[m], pieces_dy[m], weights_ff, bases[2], bases[3][0], deps
        )
        hidden.append(h)
        d_gate_up.append(dgu)
        two_keep.append(keep)
        two_beside.append(swap(send, "tensor", 1))
        ffn_parts.append((ffn_keep, swap(ffn_send, "tensor", 1)))
        left_ff.append(lf)
        left_down.append(ld)
        rows_of_two.append(rows_two)
        rows_of_dy.append(rows_dy)
        return send

    d_resid, send_back, gains_two, d_group = [], [], [], []

    def back_two(m, deps):
        across = swap(two_passed[m], "tensor", 2)
        out, low, gain = norm_back(
            cotangent[m], resid[m], two_keep[m], two_beside[m], across, gain_two, deps
        )
        d_resid.append(out)
        send_back.append(low)
        gains_two.append(gain)
        d_group.append(gather_rows(low))

    def pass_two(m, deps):
        two_passed.append(pass_on(two_keep[m], two_beside[m], deps))

    def weight_grads(m):
        return dot32("jth,td->jhd", d_gate_up[m], rows_of_two[m]), dot32("th,td->hd", hidden[m], rows_of_dy[m])

    sent = feed_forward(0, (sent,))
    pass_mix(1, (sent,))
    grads_first = weight_grads(0)
    norm_two(1, grads_first)
    pass_two(0, (group_two[1][2],))
    sent = feed_forward(1, (two_passed[0],))
    back_two(0, (sent,))
    pass_two(1, (send_back[0],))
    grads_last = weight_grads(1)
    merged_early = [
        (grads_first[0] + grads_last[0] + err_ff_t, True),
        ((grads_first[1] + grads_last[1])[None] + err_down, False),
    ]
    left_ff = sum(left_ff)
    early = jnp.concatenate([left_ff[0], left_ff[1], sum(left_down)], axis=1) + err_left

    def owned_frames(frame, blocks, rows, count):
        starts = [j * rows + dp_index * count for j in range(blocks)]
        return jnp.stack([lax.dynamic_slice_in_dim(frame, s, count, 1) for s in starts])

    def factor_steps():
        (left,), (right,), deps = yield from add_steps([early], "dp")
        frame, own = frames_and_basis(left, right, merged_early, dp_count, deps)
        (left,), (right,), deps = yield from add_steps([own], "dp")
        update = (
            owned_frames(frame, 2, width, w_ff.shape[1]), jnp.swapaxes(w_ff, 1, 2), jnp.swapaxes(mom_ff, 1, 2)
        )
        return (frame,) + tuple(basis_and_errors(frame, left, right, merged_early, dp_count, update, deps))

    steps = factor_steps()
    next(steps)
    (waiting,) = steps.send((merged_early[0][0], merged_early[1][0]))
    grad_out, grad_in, grad_decay, grad_taps, grad_head = 0.0, 0.0, 0.0, 0.0, 0.0
    back_parts, ffn_passed, before_last = [], [], []
    for m in micros:
        grad_out = grad_out + dot32("ci,id->cd", gated_u[m], jnp.concatenate(d_group[m], axis=0))
        d_mix = dot32("ji,id->jd", place[m], jnp.concatenate(d_group[m], axis=0)).astype(BF)
        d_gated = dot32("dc,td->ct", weights_out, d_mix)
        pieces = []
        if m == last:
            merged_out = grad_out[None] + err_out
            left_in = jnp.concatenate([left_in, sketches([(merged_out, False)], [bases[1]])], axis=1)
        for h in heads:
            deps = [waiting] + before_last * (m == last and h == heads[-1])
            if m == 0 and h == 0:
                deps.append(two_passed[1])
            if m == 0 and h == 1:
                back_two(1, (pieces[0][3],))
                deps.append(send_back[1])
            pieces.append(
                mixer_backward(
                    h, proj[m], pre_decay[m], taps_cols, live[m], d_gated, bases[0], packed[m], left_in,
                    lens[m], mesa_bias, deps,
                )
            )
            left_in = pieces[-1][4]
            done = (pieces[-1][3],)
            if m < last:
                keep, beside = ffn_parts[h]
                ffn_passed.append(pass_on(keep, beside, done))
            if (m, h) != (last, heads[-1]):
                (waiting,) = steps.send(done)
        d_heads = [p[0] for p in pieces]
        d_proj = jnp.concatenate(d_heads, axis=1)
        d_decay = jnp.concatenate([p[1][0] for p in pieces], axis=0).astype(BF)
        grad_taps = grad_taps + jnp.concatenate([p[2] for p in pieces], axis=1)
        grad_head = grad_head + jnp.concatenate([p[3] for p in pieces], axis=0)[:, 0]
        d_proj = dot32("kcj,ji->kci", d_proj, place[m]).astype(BF)
        if m == last:
            late = add_steps([left_in], "dp")
            next(late)
            (summed,) = late.send((d_proj,))
            d_proj = gate(d_proj, (summed,))
        grad_in = grad_in + dot32("id,kci->kdc", group_one[m], d_proj)
        if m == last:
            merged = [(grad_in + err_in[0], False), (merged_out, False)]
            (summed,) = late.send((merged[0][0],))
            d_proj = gate(d_proj, (summed,))
        d_decay = dot32("hj,ji->hi", d_decay, place[m]).astype(BF)
        d_one = dot32("kci,kdc->id", d_proj, weights_in) + dot32("hi,dh->id", d_decay, decay_low)
        d_one = d_one.astype(BF).reshape(2, 2, share, width)
        back_parts.append((d_one[:, 0], swap(d_one[:, 1], "tensor", 1)))
        grad_decay = grad_decay + dot32("hi,id->hd", d_decay, group_one[m])
        before_last = [grad_in, d_one]

    gain_grad = jnp.sum(weights_in.astype(F32) * grad_in, axis=(0, 2)) + jnp.sum(
        decay_low.astype(F32).T * grad_decay, axis=0
    )
    gains = jnp.concatenate([gain_grad[None] / gain_one, sum(gains_two)], axis=0)
    (left,), (right,), unused = finish_steps(add_steps([gains.reshape(-1, BLK)], "tensor"))
    gains = (left + right).reshape(gains.shape)
    small = [jnp.transpose(grad_taps, (0, 2, 1)), grad_decay, grad_head, gains]
    flat = jnp.concatenate([s.reshape(-1, BLK) for s in small], axis=0)

    (left,), (right,), unused = finish_steps(late, (d_one,))
    frame_late, own = frames_and_basis(left, right, merged, dp_count, (d_one,))
    try:
        while True:
            steps.send((own,))
    except StopIteration as end:
        frame_early, basis_early, w_ff_new, mom_ff_new, *errors_early = end.value
    back_passed = [pass_on(*back_parts[m], (own,) if m == last else ()) for m in micros]
    (left, flat), (right, flat_moved), unused = finish_steps(add_steps([own, flat], "dp"))
    flat = (flat + flat_moved) / dp_count

    across = [swap(v, "tensor", 2) for v in ffn_passed]
    out_tokens = add_rows(resid, ffn_parts, across, (own,))
    back_across = [swap(v, "tensor", 2) for v in back_passed]
    d_tokens = None
    for m in micros:
        if m == last:
            deps = (back_passed[last], d_tokens, out_tokens)
            update = (owned_frames(frame_late, 4, width, w_in.shape[1]), w_in, mom_in)
            basis_late, w_in_new, mom_in_new, *errors_late = basis_and_errors(
                frame_late, left, right, merged, dp_count, update, deps
            )
        keep, beside = back_parts[m]
        d_tokens = norm_back_into(
            d_tokens, m, micro_count, d_resid[m], tokens, keep, beside, back_across[m], gain_one
        )
    parts, edge = [], 0
    for s in small:
        parts.append(flat[edge : edge + s.size // BLK].reshape(s.shape))
        edge += s.size // BLK
    grad_conv, grad_decay, grad_bias, gain_total = parts
    grad_decay = jnp.transpose(grad_decay)
    grad_bias = jnp.transpose(grad_bias[:, :2])

    def part(rows_of, count, axis):
        return lax.dynamic_slice_in_dim(rows_of, dp_index * count, count, axis)

    def cut(rows_of, sizes):
        edge, out = 0, []
        for size in sizes:
            out.append(rows_of[:, edge : edge + size])
            edge += size
        return out

    def outer(frame, basis):
        return jnp.einsum("rm,rn->mn", frame, basis, precision=precise)

    hidden_width = w_ff.shape[2]
    columns = w_in.shape[2]
    frames = cut(frame_late, [width] * 4 + [columns]) + cut(frame_early, [width] * 2 + [hidden_width])
    rights = cut(basis_late, [columns] * 4 + [width]) + cut(basis_early, [hidden_width] * 2 + [width])
    basis_in_new = jnp.stack([b.T for b in rights[:4]])
    basis_out_new = rights[4].T[None]
    basis_ff_new = jnp.stack([b.T for b in rights[5:7]])
    basis_down_new = rights[7].T[None]
    err_in_new, err_out_new = errors_late[0][None], errors_late[1]
    err_ff_new, err_down_new = jnp.swapaxes(errors_early[0], 1, 2)[None], errors_early[1]
    w_ff_new, mom_ff_new = jnp.swapaxes(w_ff_new, 1, 2), jnp.swapaxes(mom_ff_new, 1, 2)
    owned_out = outer(frames[4], part(rights[4], w_out.shape[1], 1))
    owned_down = outer(frames[7], part(rights[7], w_down.shape[1], 1))
    w_out_new, mom_out_new = advance_weight(w_out, mom_out, owned_out, step_rate)
    w_down_new, mom_down_new = advance_weight(w_down, mom_down, owned_down, step_rate)
    gains_new, mom_gains_new = advance_weight(norm_gains, mom_gains, gain_total, small_rate)
    conv_new, mom_conv_new = advance_weight(conv_taps, mom_conv, grad_conv, small_rate)
    decay_new, mom_decay_new = advance_weight(decay_w, mom_decay, grad_decay, small_rate)
    bias_new, mom_bias_new = advance_weight(mesa_bias, mom_bias, grad_bias, small_rate)
    return (
        out_tokens,
        d_tokens,
        w_in_new,
        mom_in_new,
        err_in_new,
        basis_in_new,
        w_out_new,
        mom_out_new,
        err_out_new,
        basis_out_new,
        w_ff_new,
        mom_ff_new,
        err_ff_new,
        basis_ff_new,
        w_down_new,
        mom_down_new,
        err_down_new,
        basis_down_new,
        gains_new,
        mom_gains_new,
        conv_new,
        mom_conv_new,
        decay_new,
        mom_decay_new,
        bias_new,
        mom_bias_new,
    )


def solution(mesh):
    placed = (
        P(None, ("dp", "tensor"), None),
        P(None, ("dp", "tensor"), None),
        P(None, "dp", None),
        P(None, "dp", None),
        P(None, "dp", None),
        P(None, "dp", "tensor"),
        P("tensor", "dp"),
        P(None, "dp", "tensor"),
        P("tensor", "dp"),
        P(),
        P(None, None, "tensor"),
        P(None, "tensor"),
        P(None, "tensor"),
        P(None, "dp", "tensor"),
        P("tensor", "dp"),
        P(None, "dp", "tensor"),
        P("tensor", "dp"),
        P(),
        P(None, None, "tensor"),
        P(None, "tensor"),
        P(None, "tensor"),
        P("dp", None, None, "tensor"),
        P("dp", "tensor", None),
        P("dp", None, None, "tensor"),
        P("dp", "tensor", None),
        P(None, "tensor", None),
        P("tensor", None, None),
        P(None, "tensor", None),
        P("tensor", None, None),
    )
    return jax.shard_map(
        on_device,
        mesh=mesh,
        in_specs=placed,
        out_specs=(
            P(None, ("dp", "tensor"), None),
            P(None, ("dp", "tensor"), None),
            P(None, "dp", "tensor"),
            P(None, "dp", "tensor"),
            P("dp", None, None, "tensor"),
            P(None, "tensor", None),
            P("tensor", "dp"),
            P("tensor", "dp"),
            P("dp", "tensor", None),
            P("tensor", None, None),
            P(None, "dp", "tensor"),
            P(None, "dp", "tensor"),
            P("dp", None, None, "tensor"),
            P(None, "tensor", None),
            P("tensor", "dp"),
            P("tensor", "dp"),
            P("dp", "tensor", None),
            P("tensor", None, None),
            P(),
            P(),
            P(None, None, "tensor"),
            P(None, None, "tensor"),
            P(None, "tensor"),
            P(None, "tensor"),
            P(None, "tensor"),
            P(None, "tensor"),
        ),
        check_vma=False,
    )
```

```python
import functools
from types import SimpleNamespace

import jax
import jax.numpy as jnp
from jax import lax
from jax.experimental import pallas as pl
from jax.experimental.pallas import tpu as pltpu
from jax.sharding import PartitionSpec as P

CG_STEPS = 8
BLK = 128
tiny_eps = 1e-06
solve_floor = 0.01
ridge_shift = 9.0
precise = lax.Precision.HIGHEST
F32 = jnp.float32
BF = jnp.bfloat16


def softplus(x):
    return jnp.maximum(x, 0.0) + jnp.log1p(jnp.exp(-jnp.abs(x)))


def spot_of(i):
    return pl.ds(i * BLK, BLK)


def sigmoid(x):
    return 0.5 * jnp.tanh(0.5 * x) + 0.5


def mm(a, b):
    return jnp.dot(a, b, preferred_element_type=F32)


def nt(a, b):
    return lax.dot_general(a, b, (((1,), (1,)), ((), ())), preferred_element_type=F32)


def high_low(x, axis=0):
    high = x.astype(BF).astype(F32)
    return jnp.concatenate([high, x - high], axis=axis).astype(BF)


def halves(x):
    count = x.shape[0] // 2
    return x[:count] + x[count:]


def col_sum(x):
    return jnp.sum(x, axis=0, keepdims=True)


def start_of(lens_ref, places):
    begin = jnp.zeros_like(places)
    edge = jnp.int32(0)
    for item in range(lens_ref.shape[0] - 1):
        edge = edge + lens_ref[item]
        begin = jnp.where(places >= edge, edge, begin)
    return begin


def conv_masks(lens_ref, total, taps):
    places = lax.broadcasted_iota(jnp.int32, (1, total), 1)
    begin = start_of(lens_ref, places)
    return [(places - i >= begin).astype(F32) for i in range(taps)]


def conv_rows(rows, taps_now, sc):
    acc = rows * taps_now[:, 0:1]
    for i in range(1, taps_now.shape[1]):
        acc = acc + (pltpu.roll(rows, i, 1) * sc.mask[i]) * taps_now[:, i : i + 1]
    return acc


CHUNK = 16
TOGETHER = 8


def by_chunks(width, fn, init):
    def body(c, carry):
        for k in range(TOGETHER):
            carry = fn(pl.ds(pl.multiple_of((c * TOGETHER + k) * CHUNK, CHUNK), CHUNK), carry)
        return carry

    return lax.fori_loop(0, width // (CHUNK * TOGETHER), body, init)


def set_up(head, proj_ref, prea_ref, taps_ref, live_ref, lens_ref, bias_ref, sc, keep_all):
    width, total = proj_ref.shape[1], proj_ref.shape[2]
    blocks = total // BLK
    taps = taps_ref.shape[2]
    for i, mask in enumerate(conv_masks(lens_ref, total, taps)):
        sc.mask[i] = jnp.broadcast_to(mask, (CHUNK, total))
    live = live_ref[...]

    def squares(j, dst):
        def body(at, acc):
            u = conv_rows(proj_ref[j, at, :], taps_ref[j, at, :], sc)
            sig = sigmoid(u)
            x = u * sig
            dst[at, :] = x
            if keep_all:
                sc.slope[j, at, :] = sig + x * (1.0 - sig)
            return acc + x * x

        acc = by_chunks(width, body, jnp.zeros((CHUNK, total), F32))
        return lax.rsqrt(col_sum(acc) + tiny_eps)

    keys, values = (sc.xk, sc.xv) if keep_all else (sc.x, sc.x)

    scale_q = squares(0, sc.q)
    scale_k = squares(1, keys)
    sc.scale[0:1, :] = scale_q
    sc.scale[1:2, :] = scale_k
    scale_k = scale_k * live
    for n in range(blocks):
        at = pl.ds(n * BLK, BLK)
        sc.q[:, at] = sc.q[:, at] * scale_q[:, n * BLK : (n + 1) * BLK]
        kt = keys[:, at] * scale_k[:, n * BLK : (n + 1) * BLK]
        sc.kt[:, at] = kt.astype(BF)
        sc.ks[n, 0:BLK, :] = kt.T.astype(BF)
    squares(2, values)
    for n in range(blocks):
        at = pl.ds(n * BLK, BLK)
        vt = values[:, at] * live[:, n * BLK : (n + 1) * BLK]
        sc.vt[:, at] = vt.astype(BF)
        if keep_all:
            sc.vg[n, 0:BLK, :] = vt.T.astype(BF)
    base = prea_ref[0, :, :] + jnp.full((1, total), bias_ref[0, head], F32)
    base = jnp.concatenate([base[:, n * BLK : (n + 1) * BLK] for n in range(blocks)], axis=0)
    forget = -softplus(base)
    row_i = lax.broadcasted_iota(jnp.int32, (BLK, BLK), 0)
    col_i = lax.broadcasted_iota(jnp.int32, (BLK, BLK), 1)
    cum = jnp.dot(forget, (row_i <= col_i).astype(F32), precision=precise, preferred_element_type=F32)
    first = lax.broadcasted_iota(jnp.int32, (blocks, BLK), 0) * BLK
    places = first + lax.broadcasted_iota(jnp.int32, (blocks, BLK), 1)
    begin = start_of(lens_ref, places)
    begin_last = start_of(lens_ref, first + (BLK - 1))
    end = jnp.broadcast_to(cum[:, BLK - 1 : BLK], cum.shape)
    from_start = jnp.where(begin < first, jnp.exp(cum), 0.0)
    to_end = jnp.where(places >= begin_last, jnp.exp(end - cum), 0.0)
    keep = jnp.where(begin_last < first, jnp.exp(end), 0.0)
    sc.dec[0] = from_start
    sc.dec[1] = to_end
    sc.dec[2] = keep
    cum_col = jnp.transpose(cum)
    for n in range(blocks):
        spread = cum[n : n + 1, :] - cum_col[:, n : n + 1]
        allowed = (row_i <= col_i) & (row_i + n * BLK >= begin[n : n + 1, :])
        sc.dt[n] = jnp.where(allowed, jnp.exp(jnp.where(allowed, spread, 0.0)), 0.0)
    state = jnp.zeros((2 * width, width), F32)
    for n in range(blocks):
        sc.ks[n, BLK:, :] = state[:width].astype(BF)
        sc.g[n] = state[width:].astype(BF)
        if keep_all:
            sc.vg[n, BLK:, :] = state[width:].T.astype(BF)
        if n + 1 < blocks:
            at = pl.ds(n * BLK, BLK)
            to_row = to_end[n : n + 1, :]
            scaled = jnp.concatenate(
                [sc.kt[:, at].astype(F32) * to_row, sc.vt[:, at].astype(F32) * to_row], axis=0
            ).astype(BF)
            state = keep[n : n + 1, :] * state + mm(scaled, sc.ks[n, 0:BLK, :])
    return softplus(jnp.full((1, BLK), bias_ref[1, head], F32) + ridge_shift)


def solve(lam, sc, keep_all):
    blocks = sc.dt.shape[0]
    spans = [pl.ds(n * BLK, BLK) for n in range(blocks)]
    row = sc.row
    for n, at in enumerate(spans):
        q = sc.q[:, at]
        row[0, n : n + 1, :] = col_sum(q * q)
        sc.z[:, at] = jnp.zeros_like(q)
        sc.p[:, at] = q
        sc.r[:, at] = q
        sc.pl[:, at] = q.astype(BF)

    def step(i, last):
        spot = spot_of(i)
        for n, at in enumerate(spans):
            both = mm(sc.ks[n], sc.pl[:, at])
            scores = (sc.dt[n] * both[:BLK]).astype(BF)
            sc.sl[n] = scores
            sc.w[:, at] = sc.dec[0, n : n + 1, :] * both[BLK:]
            if keep_all:
                far = spot_of(CG_STEPS + i)
                sc.rh[n, :, spot] = scores
                sc.lh[n, :, far] = sc.pl[:, at]
        for n, at in enumerate(spans):
            p = sc.p[:, at]
            w = mm(sc.kt[:, at], sc.sl[n]) + sc.w[:, at] + lam * p
            rho = row[0, n : n + 1, :]
            inv_c = 1.0 / (col_sum(p * w) + solve_floor)
            s = rho * inv_c
            sc.z[:, at] = sc.z[:, at] + s * p
            if keep_all:
                sc.ph[i, :, at] = p
                sc.wh[i, :, at] = w
                sc.fh[n, :, spot] = (sc.dec[0, n : n + 1, :] * p).astype(BF)
                sc.sh[i, 0, n : n + 1, :] = s
                sc.sh[i, 1, n : n + 1, :] = inv_c
            if not last:
                r = sc.r[:, at] - s * w
                sc.r[:, at] = r
                rho_next = col_sum(r * r)
                inv_rho = 1.0 / (rho + solve_floor)
                beta = rho_next * inv_rho
                row[0, n : n + 1, :] = rho_next
                if keep_all:
                    sc.nh[i, :, at] = r
                    sc.sh[i, 2, n : n + 1, :] = inv_rho
                    sc.sh[i, 3, n : n + 1, :] = beta
                p = r + beta * p
                sc.p[:, at] = p
                sc.pl[:, at] = p.astype(BF)

    for i in range(CG_STEPS):
        step(i, i == CG_STEPS - 1)


def forward_kernel(names, head, proj_ref, prea_ref, taps_ref, live_ref, lens_ref, bias_ref, out_ref, *scratch):
    sc = SimpleNamespace(**dict(zip(names, scratch)))
    lam = set_up(head, proj_ref, prea_ref, taps_ref, live_ref, lens_ref, bias_ref, sc, False)
    solve(lam, sc, False)
    spans = [pl.ds(n * BLK, BLK) for n in range(sc.dt.shape[0])]
    for n, at in enumerate(spans):
        z = sc.z[:, at].astype(BF)
        sc.sl[n] = (sc.dt[n] * mm(sc.ks[n, 0:BLK, :], z)).astype(BF)
        sc.w[:, at] = sc.dec[0, n : n + 1, :] * mm(sc.g[n], z)
    for n, at in enumerate(spans):
        o = mm(sc.vt[:, at], sc.sl[n]) + sc.w[:, at]
        out_ref[:, at] = (o * sigmoid(proj_ref[3, :, at])).astype(BF)


def backward_kernel(
    names, head, proj_ref, prea_ref, taps_ref, live_ref, dg_ref, basis_ref, packed_ref, left_ref, lens_ref, bias_ref,
    dproj_ref, da_ref, dtaps_ref, dhead_ref, sketch_ref, *scratch
):
    sc = SimpleNamespace(**dict(zip(names, scratch)))
    width, total = proj_ref.shape[1], proj_ref.shape[2]
    blocks = total // BLK
    lam = set_up(head, proj_ref, prea_ref, taps_ref, live_ref, lens_ref, bias_ref, sc, True)
    solve(lam, sc, True)
    row_i = lax.broadcasted_iota(jnp.int32, (BLK, BLK), 0)
    col_i = lax.broadcasted_iota(jnp.int32, (BLK, BLK), 1)
    dkt, dvt, zb, rb_s, pb_s = sc.dkt, sc.dvt, sc.zb, sc.rb, sc.pb

    spans = [pl.ds(n * BLK, BLK) for n in range(blocks)]
    row = sc.row
    last = CG_STEPS - 1

    for n, at in enumerate(spans):
        z_low = sc.z[:, at].astype(BF)
        sc.pl[:, at] = z_low
        sc.sl[n] = (sc.dt[n] * mm(sc.ks[n, 0:BLK, :], z_low)).astype(BF)
        sc.w[:, at] = sc.dec[0, n : n + 1, :] * mm(sc.g[n], z_low)
    for n, at in enumerate(spans):
        o = mm(sc.vt[:, at], sc.sl[n]) + sc.w[:, at]
        sig = sigmoid(proj_ref[3, :, at])
        dg = dg_ref[:, at]
        dproj_ref[3, :, at] = (dg * o * sig * (1.0 - sig)).astype(BF)
        sc.do[:, at] = (dg * sig).astype(BF)
    for n, at in enumerate(spans):
        from_row = sc.dec[0, n : n + 1, :]
        z = sc.z[:, at]
        both = mm(sc.vg[n], sc.do[:, at])
        state_part = from_row * both[BLK:]
        zb[:, at] = state_part
        sc.sl2[n] = (sc.dt[n] * both[:BLK]).astype(BF)
        sc.xm[n] = sc.sl[n].astype(F32) * both[:BLK]
        sc.fm[0, n : n + 1, :] = col_sum(z * state_part)
        sc.p[:, at] = from_row * z
    for n, at in enumerate(spans):
        do = sc.do[:, at]
        zb[:, at] = zb[:, at] + mm(sc.kt[:, at], sc.sl2[n])
        dvt[:, at] = nt(do, sc.sl[n])
        sc.dg0[n] = nt(do, sc.p[:, at].astype(BF))
        dkt[:, at] = nt(sc.pl[:, at], sc.sl2[n])
    for at in spans:
        zero = jnp.zeros((width, BLK), F32)
        rb_s[:, at] = zero
        pb_s[:, at] = zero
        sc.nh[last, :, at] = zero
    sc.sh[last, 2] = jnp.zeros((blocks, BLK), F32)
    sc.sh[last, 3] = jnp.zeros((blocks, BLK), F32)
    row[0] = jnp.zeros((blocks, BLK), F32)
    sc.fm[1] = jnp.zeros((blocks, BLK), F32)

    def reverse_step(i):
        spot = spot_of(i)
        far = spot_of(CG_STEPS + i)
        s_all, inv_c, inv_rho, beta = sc.sh[i, 0], sc.sh[i, 1], sc.sh[i, 2], sc.sh[i, 3]
        for n, at in enumerate(spans):
            row[1, n : n + 1, :] = col_sum(pb_s[:, at] * sc.ph[i, :, at])
        beta_bar = row[1]
        row[2] = 2.0 * (row[0] + beta_bar * inv_rho)
        for n, at in enumerate(spans):
            rb = rb_s[:, at] + pb_s[:, at] + row[2, n : n + 1, :] * sc.nh[i, :, at]
            rb_s[:, at] = rb
            row[3, n : n + 1, :] = col_sum(zb[:, at] * sc.ph[i, :, at] - rb * sc.wh[i, :, at])
        sbar = row[3]
        row[4] = -sbar * s_all * inv_c
        row[0] = sbar * inv_c - beta_bar * beta * inv_rho
        for n, at in enumerate(spans):
            p = sc.ph[i, :, at]
            cbar = row[4, n : n + 1, :]
            s = sc.sh[i, 0, n : n + 1, :]
            wb = cbar * p - s * rb_s[:, at]
            low = wb.astype(BF)
            sc.pl[:, at] = low
            sc.lh[n, :, spot] = low
            sc.fm[1, n : n + 1, :] += col_sum(wb * p)
            pb_s[:, at] = (
                sc.sh[i, 3, n : n + 1, :] * pb_s[:, at]
                + s * zb[:, at]
                + cbar * sc.wh[i, :, at]
                + lam * wb
            )
        for n, at in enumerate(spans):
            both = mm(sc.ks[n], sc.pl[:, at])
            scores = (sc.dt[n] * both[:BLK]).astype(BF)
            sc.sl[n] = scores
            sc.rh[n, :, far] = scores
            sc.xm[n] += sc.rh[n, :, spot].astype(F32) * both[:BLK]
            state_part = sc.dec[0, n : n + 1, :] * both[BLK:]
            pb_s[:, at] = pb_s[:, at] + state_part
            sc.fm[0, n : n + 1, :] += col_sum(sc.ph[i, :, at] * state_part)
        for n, at in enumerate(spans):
            pb_s[:, at] = pb_s[:, at] + mm(sc.kt[:, at], sc.sl[n])

    for i in reversed(range(CG_STEPS)):
        reverse_step(i)
    half = CG_STEPS * BLK
    for n, at in enumerate(spans):
        dkt[:, at] += nt(sc.lh[n], sc.rh[n])
        sc.ds0[n] = nt(sc.lh[n, :, 0:half], sc.fh[n])

    d_sym = jnp.zeros((width, width), F32)
    d_g = jnp.zeros((width, width), F32)
    g_rows = [None] * blocks
    f_rows = [None] * blocks
    x_rows = [None] * blocks
    keep_rows = [None] * blocks
    lower = (row_i >= col_i).astype(BF)
    before = row_i < col_i
    for n in reversed(range(blocks)):
        at = pl.ds(n * BLK, BLK)
        kt = sc.kt[:, at]
        to_row = sc.dec[1, n : n + 1, :]
        keep = sc.dec[2, n : n + 1, :]
        if n + 1 < blocks:
            vt = sc.vt[:, at]
            g_low = d_g.astype(BF)
            part_s = to_row * mm(d_sym.astype(BF), kt)
            part_v = to_row * mm(g_low, kt)
            part_k = to_row * mm(d_g.T.astype(BF), vt)
            dkt[:, at] += part_s + part_k
            dvt[:, at] += part_v
            g_rows[n] = col_sum(0.5 * kt.astype(F32) * part_s + vt.astype(F32) * part_v)
            inner = 0.5 * d_sym * sc.ks[n, BLK:, :].astype(F32) + d_g * sc.g[n].astype(F32)
            keep_rows[n] = keep * jnp.sum(col_sum(inner), axis=1, keepdims=True)
        else:
            g_rows[n] = jnp.zeros((1, BLK), F32)
            keep_rows[n] = jnp.zeros((1, BLK), F32)
        ds0 = sc.ds0[n]
        d_sym = keep * d_sym + ds0 + ds0.T
        d_g = keep * d_g + sc.dg0[n]
        x = sc.xm[n]
        high = x.astype(BF)
        low = (x - high.astype(F32)).astype(BF)
        summed = mm(high, lower) + mm(low, lower)
        x_rows[n] = col_sum(jnp.where(before, summed, 0.0))
        f_rows[n] = sc.fm[0, n : n + 1, :]
    f_all = jnp.concatenate(f_rows, axis=0)
    g_all = jnp.concatenate(g_rows, axis=0)
    da = (
        jnp.dot(f_all, (row_i >= col_i).astype(F32), precision=precise, preferred_element_type=F32)
        + jnp.dot(g_all, before.astype(F32), precision=precise, preferred_element_type=F32)
        + jnp.concatenate(x_rows, axis=0)
        + jnp.concatenate(keep_rows, axis=0)
    )
    da = jnp.concatenate([da[n : n + 1, :] for n in range(blocks)], axis=1)
    base = prea_ref[0, :, :] + jnp.full((1, total), bias_ref[0, head], F32)
    da = -sigmoid(base) * da
    da_ref[0, :, :] = da
    d_bias = jnp.sum(da, axis=1, keepdims=True)
    d_lam = jnp.sum(col_sum(sc.fm[1]), axis=1, keepdims=True)
    d_lam = d_lam * sigmoid(jnp.full((1, BLK), bias_ref[1, head], F32) + ridge_shift)
    lane = lax.broadcasted_iota(jnp.int32, (1, BLK), 1)
    dhead_ref[0, :, :] = jnp.where(lane == 0, d_bias, d_lam)

    taps = taps_ref.shape[2]
    live = live_ref[...]
    scale_k = sc.scale[1:2, :]
    rho_bar = jnp.concatenate([row[0, n : n + 1, :] for n in range(blocks)], axis=1)
    sc.wide[0] = jnp.broadcast_to(2.0 * rho_bar, (CHUNK, total))
    sc.wide[1] = jnp.broadcast_to(sc.scale[0:1, :], (CHUNK, total))
    sc.wide[2] = jnp.broadcast_to(live, (CHUNK, total))
    sc.wide[3] = jnp.broadcast_to(scale_k, (CHUNK, total))

    def query_grad(at, acc):
        q = sc.q[at, :]
        grad = rb_s[at, :] + pb_s[at, :] + sc.wide[0] * q
        pb_s[at, :] = grad
        return acc + q * grad

    def key_grad(at, acc):
        grad = dkt[at, :] * sc.wide[2]
        dkt[at, :] = grad
        return acc + (sc.xk[at, :] * sc.wide[3]) * grad

    zero = jnp.zeros((CHUNK, total), F32)
    mean_q = col_sum(by_chunks(width, query_grad, zero))
    mean_k = col_sum(by_chunks(width, key_grad, zero))
    sc.wide[0] = jnp.broadcast_to(mean_q, (CHUNK, total))
    sc.wide[4] = jnp.broadcast_to(mean_k, (CHUNK, total))

    def through(j, at, du):
        taps_now = taps_ref[j, at, :]
        rows = proj_ref[j, at, :]
        d_rows = du * taps_now[:, 0:1]
        sums = [jnp.sum(rows * du, axis=1, keepdims=True)]
        for i in range(1, taps):
            moved = pltpu.roll(du * sc.mask[i], total - i, 1)
            d_rows = d_rows + moved * taps_now[:, i : i + 1]
            sums.append(jnp.sum(rows * moved, axis=1, keepdims=True))
        dproj_ref[j, at, :] = d_rows.astype(BF)
        dtaps_ref[j, at, :] = jnp.concatenate(sums, axis=1)

    def query_rows(at, carry):
        grad = sc.wide[1] * (pb_s[at, :] - sc.q[at, :] * sc.wide[0])
        through(0, at, grad * sc.slope[0, at, :])
        return carry

    def key_rows(at, carry):
        scale = sc.wide[3]
        grad = scale * (dkt[at, :] - (sc.xk[at, :] * scale) * sc.wide[4])
        through(1, at, grad * sc.slope[1, at, :])
        return carry

    def value_rows(at, carry):
        through(2, at, (dvt[at, :] * sc.wide[2]) * sc.slope[2, at, :])
        return carry

    for fn in (query_rows, key_rows, value_rows):
        by_chunks(width, fn, 0)

    slots, rank = basis_ref.shape[0], basis_ref.shape[1]
    inner = jnp.concatenate(
        [high_low(halves(mm(high_low(basis_ref[j]), dproj_ref[j]))) for j in range(slots)], axis=0
    )
    both = mm(inner, packed_ref[...])
    deep = packed_ref.shape[1]
    for j in range(slots):
        at = slice(j * deep, (j + 1) * deep)
        sketch_ref[:, at] = left_ref[:, at] + halves(both[2 * rank * j : 2 * rank * (j + 1)])
    if left_ref.shape[1] > slots * deep:
        sketch_ref[:, slots * deep :] = left_ref[:, slots * deep :]


def scratch_of(width, total, backward):
    blocks = total // BLK
    flat = ((width, total), F32)
    flat_low = ((width, total), BF)
    square = ((blocks, BLK, BLK), F32)
    square_low = ((blocks, BLK, BLK), BF)
    own = dict(
        q=flat,
        mask=((4, CHUNK, total), F32),
        kt=flat_low,
        vt=flat_low,
        ks=((blocks, 2 * BLK, width), BF),
        g=square_low,
        dt=square,
        dec=((3, blocks, BLK), F32),
        scale=((8, total), F32),
        row=((5, blocks, BLK), F32),
        z=flat,
        p=flat,
        r=flat,
        w=flat,
        pl=flat_low,
        sl=square_low,
    )
    if backward:
        history = ((CG_STEPS, width, total), F32)
        own.update(
            xk=flat,
            xv=flat,
            slope=((3, width, total), F32),
            wide=((5, CHUNK, total), F32),
            vg=((blocks, 2 * BLK, width), BF),
            ph=history,
            wh=history,
            nh=history,
            lh=((blocks, width, 2 * CG_STEPS * BLK), BF),
            rh=((blocks, BLK, 2 * CG_STEPS * BLK), BF),
            fh=((blocks, width, CG_STEPS * BLK), BF),
            sh=((CG_STEPS, 4, blocks, BLK), F32),
            do=flat_low,
            sl2=square_low,
            dkt=flat,
            dvt=flat,
            zb=flat,
            rb=flat,
            pb=flat,
            dg0=square,
            ds0=square,
            xm=square,
            fm=((2, blocks, BLK), F32),
        )
    else:
        own.update(x=flat)
    return list(own), [pltpu.VMEM(shape, kind) for shape, kind in own.values()]


def mixer_call(kernel, backward, head, arrays, lens, bias, deps, cost):
    proj, pre_a, taps, live = arrays[:4]
    slots, columns, total = proj.shape
    heads = pre_a.shape[0]
    width = columns // heads
    names, scratch = scratch_of(width, total, backward)
    smem = pl.BlockSpec(memory_space=pltpu.SMEM)
    kinds, count = taps.shape[0], taps.shape[2]
    in_specs = [
        pl.BlockSpec((slots, width, total), lambda g: (0, head, 0)),
        pl.BlockSpec((1, 1, total), lambda g: (head, 0, 0)),
        pl.BlockSpec((kinds, width, count), lambda g: (0, head, 0)),
        pl.BlockSpec((1, total), lambda g: (0, 0)),
    ]
    if backward:
        basis, packed, left = arrays[5:]
        in_specs += [
            pl.BlockSpec((width, total), lambda g: (head, 0)),
            pl.BlockSpec((slots, basis.shape[1], width), lambda g: (0, 0, head)),
            pl.BlockSpec(packed.shape, lambda g: (0, 0)),
            pl.BlockSpec(left.shape, lambda g: (0, 0)),
        ]
        out_specs = (
            pl.BlockSpec((slots, width, total), lambda g: (0, 0, 0)),
            pl.BlockSpec((1, 1, total), lambda g: (0, 0, 0)),
            pl.BlockSpec((kinds, width, count), lambda g: (0, 0, 0)),
            pl.BlockSpec((1, 1, BLK), lambda g: (0, 0, 0)),
            pl.BlockSpec(left.shape, lambda g: (0, 0)),
        )
        out_shape = (
            jax.ShapeDtypeStruct((slots, width, total), BF),
            jax.ShapeDtypeStruct((1, 1, total), F32),
            jax.ShapeDtypeStruct((kinds, width, count), F32),
            jax.ShapeDtypeStruct((1, 1, BLK), F32),
            jax.ShapeDtypeStruct(left.shape, F32),
        )
    else:
        out_specs = pl.BlockSpec((width, total), lambda g: (0, 0))
        out_shape = jax.ShapeDtypeStruct((width, total), BF)
    in_specs += [smem, smem] + [pl.BlockSpec(memory_space=pl.ANY)] * len(deps)
    own = len(arrays) + 2

    def body(*refs):
        kernel(names, head, *refs[:own], *refs[own + len(deps) :])

    return pl.pallas_call(
        body,
        grid=(1,),
        in_specs=in_specs,
        out_specs=out_specs,
        out_shape=out_shape,
        scratch_shapes=scratch,
        compiler_params=pltpu.CompilerParams(vmem_limit_bytes=56 * 2**20),
        cost_estimate=pl.CostEstimate(flops=cost * 10**9, bytes_accessed=cost * 3 * 10**6, transcendentals=0),
        name="mixer_backward" if backward else "mixer_forward",
    )(*arrays, lens, bias, *deps)


def mixer_forward(head, proj, pre_a, taps, live, lens, bias, deps=()):
    return mixer_call(forward_kernel, False, head, (proj, pre_a, taps, live), lens, bias, deps, 11)


def mixer_backward(head, proj, pre_a, taps, live, d_gated, basis, packed, left, lens, bias, deps=()):
    arrays = (proj, pre_a, taps, live, d_gated, basis, packed, left)
    return mixer_call(backward_kernel, True, head, arrays, lens, bias, deps, 28)


def any_specs(deps):
    return [pl.BlockSpec(memory_space=pl.ANY)] * len(deps)


def row_of(pair, k):
    return pair, pl.BlockSpec((pl.squeezed,) + pair.shape[1:], lambda g: (k, 0, 0))


def call(body, name, inputs, outs, deps=(), cost=1):
    whole = pl.BlockSpec(memory_space=pltpu.VMEM)
    count = len(inputs)

    def kernel(*refs):
        body(*refs[:count], *refs[count + len(deps) :])

    kinds = [i[1] if isinstance(i, tuple) else whole for i in inputs]
    inputs = [i[0] if isinstance(i, tuple) else i for i in inputs]
    return pl.pallas_call(
        kernel,
        grid=(1,),
        in_specs=kinds + any_specs(deps),
        out_specs=[whole] * len(outs),
        out_shape=[jax.ShapeDtypeStruct(*o) for o in outs],
        compiler_params=pltpu.CompilerParams(vmem_limit_bytes=56 * 2**20),
        cost_estimate=pl.CostEstimate(flops=cost * 10**9, bytes_accessed=cost * 3 * 10**6, transcendentals=0),
        name=name,
    )(*inputs, *deps)


def pass_on(keep, received, deps=()):
    def body(keep_ref, got_ref, out_ref):
        out_ref[...] = (keep_ref[...].astype(F32) + got_ref[...].astype(F32)).astype(BF)

    return call(body, "pass_on", [row_of(keep, 1), row_of(received, 1)], [(keep.shape[1:], BF)], deps)[0]


def second_norm(tokens, keep, beside, across, gain, deps=()):
    def body(x_ref, keep_ref, beside_ref, across_ref, gain_ref, resid_ref, normed_ref):
        x = x_ref[...].astype(F32)
        x = x + (keep_ref[...].astype(F32) + beside_ref[...].astype(F32) + across_ref[...].astype(F32))
        resid_ref[...] = x
        scale = lax.rsqrt(jnp.mean(x * x, axis=1, keepdims=True) + tiny_eps)
        normed_ref[...] = (x * scale * gain_ref[...]).astype(BF)

    return call(
        body, "second_norm", [tokens, row_of(keep, 0), row_of(beside, 0), across, gain],
        [(tokens.shape, F32), (tokens.shape, BF)], deps,
    )


def pulled_back(x, keep, beside, across, gain):
    grad = keep.astype(F32) + beside.astype(F32) + across.astype(F32)
    x = x.astype(F32)
    scale = lax.rsqrt(jnp.mean(x * x, axis=1, keepdims=True) + tiny_eps)
    unit = x * scale
    scaled = grad * gain
    return scale * (scaled - unit * jnp.mean(unit * scaled, axis=1, keepdims=True)), grad, unit


def norm_back(base, x, keep, beside, across, gain, deps=()):
    def body(base_ref, x_ref, keep_ref, beside_ref, across_ref, gain_ref, out_ref, low_ref, gain_out_ref):
        back, grad, unit = pulled_back(x_ref[...], keep_ref[...], beside_ref[...], across_ref[...], gain_ref[...])
        out = base_ref[...] + back
        out_ref[...] = out
        low_ref[...] = out.astype(BF)
        gain_out_ref[...] = col_sum(grad * unit)

    return call(
        body, "norm_back", [base, x, row_of(keep, 0), row_of(beside, 0), across, gain],
        [(x.shape, F32), (x.shape, BF), (gain.shape, F32)], deps,
    )


def norm_back_into(target, m, count, base, x, keep, beside, across, gain):
    share, width = base.shape

    def body(base_ref, x_ref, keep_ref, beside_ref, across_ref, gain_ref, *refs):
        back, grad, unit = pulled_back(x_ref[...], keep_ref[...], beside_ref[...], across_ref[...], gain_ref[...])
        refs[-1][...] = base_ref[...] + back

    inputs = [base, row_of(x, m), row_of(keep, 0), row_of(beside, 0), across, gain]
    whole = pl.BlockSpec(memory_space=pltpu.VMEM)
    old = [] if target is None else [target]
    return pl.pallas_call(
        body,
        grid=(1,),
        in_specs=[i[1] if isinstance(i, tuple) else whole for i in inputs] + any_specs(old),
        out_specs=pl.BlockSpec((pl.squeezed, share, width), lambda g: (m, 0, 0)),
        out_shape=jax.ShapeDtypeStruct((count, share, width), F32),
        input_output_aliases={len(inputs): 0} if old else {},
        name="norm_back_into",
    )(*[i[0] if isinstance(i, tuple) else i for i in inputs], *old)


def add_rows(resid, parts, across, deps=()):
    count = len(resid)
    shape = (count,) + resid[0].shape

    def body(*refs):
        out_ref = refs[-1]
        for m in range(count):
            x, keep, beside, far = (r[...] for r in refs[4 * m : 4 * m + 4])
            out_ref[m] = (x + (keep.astype(F32) + beside.astype(F32) + far.astype(F32))).astype(BF)

    inputs = []
    for x, (keep, beside), far in zip(resid, parts, across):
        inputs += [x, row_of(keep, 0), row_of(beside, 0), far]
    return call(body, "add_rows", inputs, [(shape, BF)], deps)[0]


def ffn_pass(rows, grads, w_ff, basis_ff, basis_down, old=None, deps=()):
    share, width = rows[0].shape
    total = 4 * share
    hidden_width = w_ff.shape[2]
    rank = basis_ff.shape[1]
    tile = 2 * share
    pieces = len(rows)
    steps = pieces // 2
    first = 0 if old is None else 1

    def body(*refs):
        row_refs, grad_refs = refs[:pieces], refs[pieces : 2 * pieces]
        ff_ref, bff_ref, bdown_ref = refs[2 * pieces : 2 * pieces + 3]
        left_ff, left_down, hidden_ref, dgu_ref, two_keep, two_send, ffn_keep, ffn_send, x_s, dy_s = refs[-10:]
        for k in range(pieces):
            x_s[k * share : (k + 1) * share, :] = row_refs[k][...]
            dy_s[k * share : (k + 1) * share, :] = grad_refs[k][...]
        if old is None:
            left_ff[...] = jnp.zeros_like(left_ff)
            left_down[...] = jnp.zeros_like(left_down)
        else:
            left_ff[...] = refs[2 * pieces + 3][...]
            left_down[...] = refs[2 * pieces + 4][...]

        def step(i):
            at = slice(i * tile, (i + 1) * tile)
            x, dy = x_s[at, :], dy_s[at, :]
            gate = mm(x, ff_ref[0])
            up = mm(x, ff_ref[1])
            sig = sigmoid(gate)
            act = gate * sig
            hidden = (act * up).astype(BF)
            d_hidden = mm(dy, ff_ref[2])
            d_gate = (d_hidden * up * sig * (1.0 + gate * (1.0 - sig))).astype(BF)
            d_up = (d_hidden * act).astype(BF)
            hidden_ref[at, :] = hidden
            dgu_ref[0, at, :] = d_gate
            dgu_ref[1, at, :] = d_up
            two = (nt(d_gate, ff_ref[0]) + nt(d_up, ff_ref[1])).astype(BF)
            two_keep[i] = two[:share]
            two_send[i] = two[share:]
            ffn = nt(hidden, ff_ref[2]).astype(BF)
            ffn_keep[i] = ffn[:share]
            ffn_send[i] = ffn[share:]
            for j, d in enumerate((d_gate, d_up)):
                inner = halves(nt(high_low(bff_ref[j]), d))
                left_ff[j] += halves(mm(high_low(inner), x))
            inner = halves(nt(high_low(bdown_ref[...]), dy))
            left_down[...] += halves(mm(high_low(inner), hidden))

        for i in range(steps):
            step(i)

    whole = pl.BlockSpec(memory_space=pltpu.VMEM)
    pair = ((2, share, width), BF)
    outs = [
        ((2, rank, width), F32), ((rank, hidden_width), F32),
        ((total, hidden_width), BF), ((2, total, hidden_width), BF), pair, pair, pair, pair,
        ((total, width), BF), ((total, width), BF),
    ]
    tall = pl.BlockSpec((steps * tile, width), lambda g: (first, 0))
    part = pl.BlockSpec((steps, share, width), lambda g: (first, 0, 0))
    out_specs = [
        whole, whole,
        pl.BlockSpec((steps * tile, hidden_width), lambda g: (first, 0)),
        pl.BlockSpec((2, steps * tile, hidden_width), lambda g: (0, first, 0)),
        part, part, part, part, tall, tall,
    ]
    inputs = [*rows, *grads, w_ff, basis_ff, basis_down]
    kept, aliases = [], {}
    if old is not None:
        inputs += old[:2]
        kept = list(old[2:])
        aliases = {len(inputs) + k: 2 + k for k in range(len(kept))}
    return pl.pallas_call(
        body,
        grid=(1,),
        in_specs=[whole] * len(inputs) + any_specs(kept) + any_specs(deps),
        out_specs=out_specs,
        out_shape=[jax.ShapeDtypeStruct(*o) for o in outs],
        input_output_aliases=aliases,
        compiler_params=pltpu.CompilerParams(vmem_limit_bytes=56 * 2**20),
        cost_estimate=pl.CostEstimate(flops=6 * steps * 10**9, bytes_accessed=18 * steps * 10**6, transcendentals=0),
        name="ffn_pass",
    )(*inputs, *kept, *deps)


momentum_decay = 0.5
step_rate = 1.0
small_rate = 0.05


def add_steps(values, axis):
    flip, count = 1, lax.axis_size(axis)
    moved, deps = [jnp.zeros_like(v) for v in values], ()
    while flip < count:
        moved = [swap(v, axis, flip) for v in values]
        deps = yield values
        flip *= 2
        if flip < count:
            values = add_after(values, moved, deps)
    return values, moved, deps


def add_after(left, right, deps=()):
    count = len(left)

    def body(*refs):
        for k in range(count):
            refs[2 * count + k][...] = refs[k][...] + refs[count + k][...]

    return call(body, "add_after", [*left, *right], [(v.shape, v.dtype) for v in left], deps)


def finish_steps(steps, deps=None):
    try:
        if deps is None:
            next(steps)
        while True:
            steps.send(deps or ())
    except StopIteration as end:
        return end.value


def gate(value, deps):
    return pl.pallas_call(
        lambda *refs: None,
        in_specs=any_specs((value, *deps)),
        out_specs=pl.BlockSpec(memory_space=pl.ANY),
        out_shape=jax.ShapeDtypeStruct(value.shape, value.dtype),
        input_output_aliases={0: 0},
        name="gate",
    )(value, *deps)


def each_block(groups):
    out = []
    for k, (array, flipped) in enumerate(groups):
        count, m, n = array.shape
        m, n = (n, m) if flipped else (m, n)
        out += [(k, j, flipped, m, n) for j in range(count)]
    return out


def frames_and_basis(left, right, groups, count, deps=()):
    rank = left.shape[0]
    blocks = each_block(groups)

    def body(left_ref, right_ref, *refs):
        frame_ref, right_out = refs[len(groups) :]
        edge, edge_n = 0, 0
        for k, j, flipped, m, n in blocks:
            sketch = (left_ref[:, edge : edge + m] + right_ref[:, edge : edge + m]) * (1.0 / count)
            done = []
            for r in range(rank):
                column = sketch[0:1]
                column = column * lax.rsqrt(jnp.sum(column * column, axis=1, keepdims=True) + tiny_eps)
                done.append(column)
                if r + 1 < rank:
                    sketch = sketch[1:]
                    sketch = sketch - jnp.sum(column * sketch, axis=1, keepdims=True) * column
            frame = jnp.concatenate(done, axis=0)
            frame_ref[:, edge : edge + m] = frame
            right_out[:, edge_n : edge_n + n] = times_block(frame, refs[k][j], flipped)
            edge, edge_n = edge + m, edge_n + n

    return call(
        body, "frames_and_basis", [left, right] + [a for a, f in groups],
        [(left.shape, F32), ((rank, sum(b[4] for b in blocks)), F32)], deps,
    )


def times_block(few, block, transposed):
    both = high_low(few)
    high = block.astype(BF)
    low = (block - high.astype(F32)).astype(BF)
    by = nt if transposed else mm
    return halves(by(both, high)) + by(both, low)[: few.shape[0]]


def outer_terms(frame, basis, flipped):
    high_f, high_b = frame.astype(BF).astype(F32), basis.astype(BF).astype(F32)
    f = jnp.concatenate([high_f, frame - high_f, high_f, jnp.zeros_like(frame)], axis=0)
    b = jnp.concatenate([high_b, high_b, basis - high_b, jnp.zeros_like(basis)], axis=0)
    if flipped:
        f, b = b, f
    return f.T.astype(BF), b.astype(BF)


def basis_and_errors(frame, left, right, groups, count, update, deps=()):
    blocks = each_block(groups)
    total = len(groups)

    def body(frame_ref, left_ref, right_ref, part_ref, weight_ref, moment_ref, *refs):
        basis_ref, weight_out, moment_out = refs[total : total + 3]
        out_refs = refs[total + 3 :]
        edge, edge_n = 0, 0
        for k, j, flipped, m, n in blocks:
            basis = (left_ref[:, edge_n : edge_n + n] + right_ref[:, edge_n : edge_n + n]) * (1.0 / count)
            basis_ref[:, edge_n : edge_n + n] = basis
            f, b = outer_terms(frame_ref[:, edge : edge + m], basis, flipped)
            out_refs[k][j] = refs[k][j] - mm(f, b)
            if k == 0:
                f, b = outer_terms(part_ref[j], basis, flipped)
                moment = momentum_decay * moment_ref[j] + mm(f, b)
                moment_out[j] = moment
                weight_out[j] = weight_ref[j] - step_rate * moment
            edge, edge_n = edge + m, edge_n + n

    arrays = [a for a, f in groups]
    shapes = [(a.shape, F32) for a in (left, update[1], update[2], *arrays)]
    return call(body, "basis_and_errors", [frame, left, right, *update, *arrays], shapes, deps)


def sketches(groups, bases, deps=()):
    rank = bases[0].shape[1]
    blocks = each_block(groups)

    def body(*refs):
        edge = 0
        for k, j, flipped, m, n in blocks:
            refs[-1][:, edge : edge + m] = times_block(refs[len(groups) + k][j], refs[k][j], not flipped)
            edge += m

    return call(
        body, "sketches", [a for a, f in groups] + bases, [((rank, sum(b[3] for b in blocks)), F32)], deps
    )[0]


def swap(value, axis, flip):
    count = lax.axis_size(axis)
    return lax.ppermute(value, axis, [(i, i ^ flip) for i in range(count)])


def gather_rows(own):
    beside = swap(own, "tensor", 1)
    across = swap(own, "tensor", 2)
    return [own, beside, across, swap(across, "tensor", 1)]


def advance_weight(weight, moment, grad_now, rate):
    moment_new = momentum_decay * moment + grad_now
    return (weight - rate * moment_new, moment_new)


def dot32(spec, a, b):
    return jnp.einsum(spec, a, b, preferred_element_type=jnp.float32)


def on_device(
    tokens,
    cotangent,
    slot_order,
    lengths,
    live_mask,
    w_in,
    w_out,
    w_ff,
    w_down,
    norm_gains,
    conv_taps,
    decay_w,
    mesa_bias,
    mom_in,
    mom_out,
    mom_ff,
    mom_down,
    mom_gains,
    mom_conv,
    mom_decay,
    mom_bias,
    err_in,
    err_out,
    err_ff,
    err_down,
    basis_in,
    basis_out,
    basis_ff,
    basis_down,
):
    dp_count = lax.axis_size("dp")
    dp_index = lax.axis_index("dp")
    mine = lax.axis_index("tensor")
    shard_count = lax.axis_size("tensor")
    micro_count, share, width = tokens.shape
    total = share * shard_count
    decay_low = decay_w.astype(BF)
    first = jnp.concatenate([w_in.astype(BF), jnp.transpose(w_out.astype(BF))[None]], axis=0)
    second = jnp.concatenate([w_ff.astype(BF), jnp.transpose(w_down.astype(BF))[None]], axis=0)
    weights_first = lax.all_gather(first, "dp", axis=1, tiled=True)
    weights_in = weights_first[:4]
    weights_out = weights_first[4]
    weights_ff = lax.all_gather(second, "dp", axis=1, tiled=True)
    taps_cols = jnp.transpose(conv_taps, (0, 2, 1))
    gain_one, gain_two = norm_gains[0:1], norm_gains[1:2]
    bases = [jnp.swapaxes(b, 1, 2) for b in (basis_in, basis_out, basis_ff, basis_down)]
    micros = range(micro_count)
    heads = range(mesa_bias.shape[1])
    last = micro_count - 1
    pieces_one, group_one, pieces_dy, place, live, lens = [], [], [], [], [], []
    for m in micros:
        row = tokens[m].astype(F32)
        scale = lax.rsqrt(jnp.mean(row * row, axis=1, keepdims=True) + tiny_eps)
        pieces_one.append(gather_rows((row * scale * gain_one).astype(BF)))
        group_one.append(jnp.concatenate(pieces_one[m], axis=0))
        order_now = slot_order[m, 0]
        near = jnp.bitwise_xor(order_now // share, mine) * share + order_now % share
        slots = lax.broadcasted_iota(jnp.int32, (total, total), 1)
        place.append((near[:, None] == slots).astype(BF))
        live.append(live_mask[m].astype(F32))
        lens.append(lengths[m, 0])

    packed, proj, pre_decay, gated_u = [], [], [], []
    resid, group_two, passed_mix, send_two, keep_mix, beside_mix = [], [], [], [], [], []

    def project(m):
        proj.append(dot32("jdc,td->jct", weights_in, packed[m]))
        pre_decay.append(dot32("dh,td->ht", decay_low, packed[m])[:, None, :])

    def forward(m, h, deps):
        return mixer_forward(h, proj[m], pre_decay[m], taps_cols, live[m], lens[m], mesa_bias, deps)

    def mix_out(m, gated):
        gated_u.append(dot32("cj,ji->ci", jnp.concatenate(gated, axis=0), place[m]).astype(BF))
        terms = dot32("ci,dc->id", gated_u[m], weights_out).astype(BF).reshape(2, 2, share, width)
        keep_mix.append(terms[:, 0])
        send = terms[:, 1]
        beside_mix.append(swap(send, "tensor", 1))
        return send

    def pass_mix(m, deps):
        passed_mix.append(pass_on(keep_mix[m], beside_mix[m], deps))

    def norm_two(m, deps):
        across = swap(passed_mix[m], "tensor", 2)
        own, low = second_norm(tokens[m], keep_mix[m], beside_mix[m], across, gain_two, deps)
        resid.append(own)
        send_two.append(low)
        group_two.append(gather_rows(low))

    err_ff_t = jnp.swapaxes(err_ff[0], 1, 2)
    err_left = sketches([(err_ff_t, True), (err_down, False)], [bases[2], bases[3]])
    left_in = sketches([(err_in[0], False)], [bases[0]])
    for m in micros:
        packed.append(dot32("ji,id->jd", place[m], group_one[m]).astype(BF))
        pieces_dy.append(gather_rows(gate(cotangent[m].astype(BF), (pieces_one[last][2],))))
    project(0)
    gated = [forward(0, h, (err_left, left_in, packed[last])) for h in heads]
    sent = mix_out(0, gated)
    project(1)
    pass_mix(0, (proj[1],))
    gated = [forward(1, 0, (passed_mix[0],))]
    norm_two(0, (gated[0],))
    gated.append(forward(1, 1, (send_two[0],)))
    sent = mix_out(1, gated)

    hidden, d_gate_up, two_keep, two_beside, two_passed, ffn_parts, left_ff, left_down = [[] for i in range(8)]
    rows_of_two, rows_of_dy = [], []

    def feed_forward(m, deps, early=None):
        if early is None:
            parts = ffn_pass(group_two[m], pieces_dy[m], weights_ff, bases[2], bases[3][0], None, deps)
        else:
            parts = ffn_pass(group_two[m][:2], pieces_dy[m][:2], weights_ff, bases[2], bases[3][0], None, early)
            parts = ffn_pass(group_two[m][2:], pieces_dy[m][2:], weights_ff, bases[2], bases[3][0], parts, deps)
        lf, ld, h, dgu, keep, send, ffn_keep, ffn_send, rows_two, rows_dy = parts
        hidden.append(h)
        d_gate_up.append(dgu)
        two_keep.append(keep)
        two_beside.append(swap(send, "tensor", 1))
        ffn_parts.append((ffn_keep, swap(ffn_send, "tensor", 1)))
        left_ff.append(lf)
        left_down.append(ld)
        rows_of_two.append(rows_two)
        rows_of_dy.append(rows_dy)
        return send

    d_resid, send_back, gains_two, d_group = [], [], [], []

    def back_two(m, deps):
        across = swap(two_passed[m], "tensor", 2)
        out, low, gain = norm_back(
            cotangent[m], resid[m], two_keep[m], two_beside[m], across, gain_two, deps
        )
        d_resid.append(out)
        send_back.append(low)
        gains_two.append(gain)
        d_group.append(gather_rows(low))

    def pass_two(m, deps):
        two_passed.append(pass_on(two_keep[m], two_beside[m], deps))

    def weight_grads(m):
        return dot32("jth,td->jhd", d_gate_up[m], rows_of_two[m]), dot32("th,td->hd", hidden[m], rows_of_dy[m])

    sent = feed_forward(0, (sent,))
    pass_mix(1, (sent,))
    grads_first = weight_grads(0)
    norm_two(1, grads_first)
    pass_two(0, (group_two[1][2],))
    sent = feed_forward(1, (two_passed[0],), (send_two[1],))
    back_two(0, (sent,))
    pass_two(1, (send_back[0],))
    grads_last = weight_grads(1)
    merged_early = [
        (grads_first[0] + grads_last[0] + err_ff_t, True),
        ((grads_first[1] + grads_last[1])[None] + err_down, False),
    ]
    left_ff = sum(left_ff)
    early = jnp.concatenate([left_ff[0], left_ff[1], sum(left_down)], axis=1) + err_left

    def owned_frames(frame, blocks, rows, count):
        starts = [j * rows + dp_index * count for j in range(blocks)]
        return jnp.stack([lax.dynamic_slice_in_dim(frame, s, count, 1) for s in starts])

    def factor_steps():
        (left,), (right,), deps = yield from add_steps([early], "dp")
        frame, own = frames_and_basis(left, right, merged_early, dp_count, deps)
        (left,), (right,), deps = yield from add_steps([own], "dp")
        update = (
            owned_frames(frame, 2, width, w_ff.shape[1]), jnp.swapaxes(w_ff, 1, 2), jnp.swapaxes(mom_ff, 1, 2)
        )
        return (frame,) + tuple(basis_and_errors(frame, left, right, merged_early, dp_count, update, deps))

    steps = factor_steps()
    next(steps)
    (waiting,) = steps.send((merged_early[0][0], merged_early[1][0]))
    grad_out, grad_in, grad_decay, grad_taps, grad_head = 0.0, 0.0, 0.0, 0.0, 0.0
    back_parts, ffn_passed, before_last = [], [], []
    for m in micros:
        grad_out = grad_out + dot32("ci,id->cd", gated_u[m], jnp.concatenate(d_group[m], axis=0))
        d_mix = dot32("ji,id->jd", place[m], jnp.concatenate(d_group[m], axis=0)).astype(BF)
        d_gated = dot32("dc,td->ct", weights_out, d_mix)
        pieces = []
        if m == last:
            merged_out = grad_out[None] + err_out
            left_in = jnp.concatenate([left_in, sketches([(merged_out, False)], [bases[1]])], axis=1)
        for h in heads:
            deps = [waiting] + before_last * (m == last and h == heads[-1])
            if m == 0 and h == 0:
                deps.append(two_passed[1])
            if m == 0 and h == 1:
                back_two(1, (pieces[0][3],))
                deps.append(send_back[1])
            pieces.append(
                mixer_backward(
                    h, proj[m], pre_decay[m], taps_cols, live[m], d_gated, bases[0], packed[m], left_in,
                    lens[m], mesa_bias, deps,
                )
            )
            left_in = pieces[-1][4]
            done = (pieces[-1][3],)
            if m < last:
                keep, beside = ffn_parts[h]
                ffn_passed.append(pass_on(keep, beside, done))
            if (m, h) != (last, heads[-1]):
                (waiting,) = steps.send(done)
        d_heads = [p[0] for p in pieces]
        d_proj = jnp.concatenate(d_heads, axis=1)
        d_decay = jnp.concatenate([p[1][0] for p in pieces], axis=0).astype(BF)
        grad_taps = grad_taps + jnp.concatenate([p[2] for p in pieces], axis=1)
        grad_head = grad_head + jnp.concatenate([p[3] for p in pieces], axis=0)[:, 0]
        d_proj = dot32("kcj,ji->kci", d_proj, place[m]).astype(BF)
        if m == last:
            late = add_steps([left_in], "dp")
            next(late)
            (summed,) = late.send((d_proj,))
            d_proj = gate(d_proj, (summed,))
        grad_in = grad_in + dot32("id,kci->kdc", group_one[m], d_proj)
        if m == last:
            merged = [(grad_in + err_in[0], False), (merged_out, False)]
            (summed,) = late.send((merged[0][0],))
            d_proj = gate(d_proj, (summed,))
        d_decay = dot32("hj,ji->hi", d_decay, place[m]).astype(BF)
        d_one = dot32("kci,kdc->id", d_proj, weights_in) + dot32("hi,dh->id", d_decay, decay_low)
        d_one = d_one.astype(BF).reshape(2, 2, share, width)
        back_parts.append((d_one[:, 0], swap(d_one[:, 1], "tensor", 1)))
        grad_decay = grad_decay + dot32("hi,id->hd", d_decay, group_one[m])
        before_last = [grad_in, d_one]

    gain_grad = jnp.sum(weights_in.astype(F32) * grad_in, axis=(0, 2)) + jnp.sum(
        decay_low.astype(F32).T * grad_decay, axis=0
    )
    gains = jnp.concatenate([gain_grad[None] / gain_one, sum(gains_two)], axis=0)
    (left,), (right,), unused = finish_steps(add_steps([gains.reshape(-1, BLK)], "tensor"))
    gains = (left + right).reshape(gains.shape)
    small = [jnp.transpose(grad_taps, (0, 2, 1)), grad_decay, grad_head, gains]
    flat = jnp.concatenate([s.reshape(-1, BLK) for s in small], axis=0)

    (left,), (right,), unused = finish_steps(late, (d_one,))
    frame_late, own = frames_and_basis(left, right, merged, dp_count, (d_one,))
    try:
        while True:
            steps.send((own,))
    except StopIteration as end:
        frame_early, basis_early, w_ff_new, mom_ff_new, *errors_early = end.value
    back_passed = [pass_on(*back_parts[m], (own,) if m == last else ()) for m in micros]
    (left, flat), (right, flat_moved), unused = finish_steps(add_steps([own, flat], "dp"))
    flat = (flat + flat_moved) / dp_count

    across = [swap(v, "tensor", 2) for v in ffn_passed]
    out_tokens = add_rows(resid, ffn_parts, across, (own,))
    back_across = [swap(v, "tensor", 2) for v in back_passed]
    d_tokens = None
    for m in micros:
        if m == last:
            deps = (back_passed[last], d_tokens, out_tokens)
            update = (owned_frames(frame_late, 4, width, w_in.shape[1]), w_in, mom_in)
            basis_late, w_in_new, mom_in_new, *errors_late = basis_and_errors(
                frame_late, left, right, merged, dp_count, update, deps
            )
        keep, beside = back_parts[m]
        d_tokens = norm_back_into(
            d_tokens, m, micro_count, d_resid[m], tokens, keep, beside, back_across[m], gain_one
        )
    parts, edge = [], 0
    for s in small:
        parts.append(flat[edge : edge + s.size // BLK].reshape(s.shape))
        edge += s.size // BLK
    grad_conv, grad_decay, grad_bias, gain_total = parts
    grad_decay = jnp.transpose(grad_decay)
    grad_bias = jnp.transpose(grad_bias[:, :2])

    def part(rows_of, count, axis):
        return lax.dynamic_slice_in_dim(rows_of, dp_index * count, count, axis)

    def cut(rows_of, sizes):
        edge, out = 0, []
        for size in sizes:
            out.append(rows_of[:, edge : edge + size])
            edge += size
        return out

    def outer(frame, basis):
        return jnp.einsum("rm,rn->mn", frame, basis, precision=precise)

    hidden_width = w_ff.shape[2]
    columns = w_in.shape[2]
    frames = cut(frame_late, [width] * 4 + [columns]) + cut(frame_early, [width] * 2 + [hidden_width])
    rights = cut(basis_late, [columns] * 4 + [width]) + cut(basis_early, [hidden_width] * 2 + [width])
    basis_in_new = jnp.stack([b.T for b in rights[:4]])
    basis_out_new = rights[4].T[None]
    basis_ff_new = jnp.stack([b.T for b in rights[5:7]])
    basis_down_new = rights[7].T[None]
    err_in_new, err_out_new = errors_late[0][None], errors_late[1]
    err_ff_new, err_down_new = jnp.swapaxes(errors_early[0], 1, 2)[None], errors_early[1]
    w_ff_new, mom_ff_new = jnp.swapaxes(w_ff_new, 1, 2), jnp.swapaxes(mom_ff_new, 1, 2)
    owned_out = outer(frames[4], part(rights[4], w_out.shape[1], 1))
    owned_down = outer(frames[7], part(rights[7], w_down.shape[1], 1))
    w_out_new, mom_out_new = advance_weight(w_out, mom_out, owned_out, step_rate)
    w_down_new, mom_down_new = advance_weight(w_down, mom_down, owned_down, step_rate)
    gains_new, mom_gains_new = advance_weight(norm_gains, mom_gains, gain_total, small_rate)
    conv_new, mom_conv_new = advance_weight(conv_taps, mom_conv, grad_conv, small_rate)
    decay_new, mom_decay_new = advance_weight(decay_w, mom_decay, grad_decay, small_rate)
    bias_new, mom_bias_new = advance_weight(mesa_bias, mom_bias, grad_bias, small_rate)
    return (
        out_tokens,
        d_tokens,
        w_in_new,
        mom_in_new,
        err_in_new,
        basis_in_new,
        w_out_new,
        mom_out_new,
        err_out_new,
        basis_out_new,
        w_ff_new,
        mom_ff_new,
        err_ff_new,
        basis_ff_new,
        w_down_new,
        mom_down_new,
        err_down_new,
        basis_down_new,
        gains_new,
        mom_gains_new,
        conv_new,
        mom_conv_new,
        decay_new,
        mom_decay_new,
        bias_new,
        mom_bias_new,
    )


def solution(mesh):
    placed = (
        P(None, ("dp", "tensor"), None),
        P(None, ("dp", "tensor"), None),
        P(None, "dp", None),
        P(None, "dp", None),
        P(None, "dp", None),
        P(None, "dp", "tensor"),
        P("tensor", "dp"),
        P(None, "dp", "tensor"),
        P("tensor", "dp"),
        P(),
        P(None, None, "tensor"),
        P(None, "tensor"),
        P(None, "tensor"),
        P(None, "dp", "tensor"),
        P("tensor", "dp"),
        P(None, "dp", "tensor"),
        P("tensor", "dp"),
        P(),
        P(None, None, "tensor"),
        P(None, "tensor"),
        P(None, "tensor"),
        P("dp", None, None, "tensor"),
        P("dp", "tensor", None),
        P("dp", None, None, "tensor"),
        P("dp", "tensor", None),
        P(None, "tensor", None),
        P("tensor", None, None),
        P(None, "tensor", None),
        P("tensor", None, None),
    )
    return jax.shard_map(
        on_device,
        mesh=mesh,
        in_specs=placed,
        out_specs=(
            P(None, ("dp", "tensor"), None),
            P(None, ("dp", "tensor"), None),
            P(None, "dp", "tensor"),
            P(None, "dp", "tensor"),
            P("dp", None, None, "tensor"),
            P(None, "tensor", None),
            P("tensor", "dp"),
            P("tensor", "dp"),
            P("dp", "tensor", None),
            P("tensor", None, None),
            P(None, "dp", "tensor"),
            P(None, "dp", "tensor"),
            P("dp", None, None, "tensor"),
            P(None, "tensor", None),
            P("tensor", "dp"),
            P("tensor", "dp"),
            P("dp", "tensor", None),
            P("tensor", None, None),
            P(),
            P(),
            P(None, None, "tensor"),
            P(None, None, "tensor"),
            P(None, "tensor"),
            P(None, "tensor"),
            P(None, "tensor"),
            P(None, "tensor"),
        ),
        check_vma=False,
    )
```
